32 devices in a mesh: rep: 8 (over z, y), ep: 4 (over x, core).
Axes of the slice: x: 2, y: 2, z: 4, core: 2. Of those that a mesh axis runs over, the one named last changes fastest.
Arguments:
- tokens: bfloat16 [32768, 1024], P(('rep', 'ep')), may hold values from -6 to 6
- cotangent: bfloat16 [32768, 1024], P(('rep', 'ep')), may hold values from -6 to 6
- gain_attn: float32 [1024], replicated, may hold values from 0.5 to 1.5
- w_qkv: bfloat16 [1024, 3072], replicated, may hold values from -0.1875 to 0.1875
- w_out: bfloat16 [1024, 1024], replicated, may hold values from -0.75 to 0.75
- rel_table: float32 [32, 16], replicated, may hold values from -3 to 3
- gain_moe: float32 [1024], replicated, may hold values from 0.5 to 1.5
- w_router: bfloat16 [1024, 4], replicated, may hold values from -0.125 to 0.125
- w_gate: bfloat16 [4, 1024, 2816], P('ep'), may hold values from -0.1875 to 0.1875
- w_up: bfloat16 [4, 1024, 2816], P('ep'), may hold values from -0.1875 to 0.1875
- w_down: bfloat16 [4, 2816, 1024], P('ep'), may hold values from -0.109375 to 0.109375
- expert_ids: int32 [32768, 2], P(('rep', 'ep')), may hold values from 0 to 3, all different within a row
- priority: int32 [32, 2048], P(('rep', 'ep')), may hold values from 0 to 2047, each once within a row
- span_starts: int32 [32, 2], P(('rep', 'ep')), may hold values from 0 to 768, as said below
Outputs:
- block_out: bfloat16 [32768, 1024], P(('rep', 'ep'))
- grad_tokens: float32 [32768, 1024], P(('rep', 'ep'))
- grad_gain_attn: float32 [1024], replicated
- grad_w_qkv: float32 [1024, 3072], replicated
- grad_w_out: float32 [1024, 1024], replicated
- grad_rel_table: float32 [32, 16], replicated
- grad_gain_moe: float32 [1024], replicated
- grad_w_router: float32 [1024, 4], replicated
- grad_w_gate: float32 [4, 1024, 2816], P('ep', 'rep')
- grad_w_up: float32 [4, 1024, 2816], P('ep', 'rep')
- grad_w_down: float32 [4, 2816, 1024], P('ep', 'rep')
The draws below stay inside these ranges and needn't reach their ends.
Inputs may be any that keep to these rules, and one draw needn't show every extreme that they name: `expert_ids`: each token names two different experts. `priority`: each row is a permutation of the 2048 pairs of one device. `span_starts`: the spans of a sequence rise, are disjoint and lie inside the sequence.
All inputs are finite; a program needn't handle non-finite values.
Results may differ from the reference program's by a relative error of at most 0.015.
Values may be sent and summed in bfloat16 or wider, within the bound.
A program may use at most 640 MiB of HBM per device.

```python
from functools import partial
import jax
import jax.numpy as jnp
import numpy as np
from jax import lax

D = 1024
H = 16
HD = 64
FF = 2816
BUCKETS = 32
MAXDIST = 128
SEQ = 1024
PIC = 256
SPANS = 2
TOK_DEV = 1024
EXPERTS = 4
CAP = 640
SEQS = 32
TOKENS = 32768
N_REP = 8
N_EP = 4
DEVICES = 32


def draw_span_starts(key, part):
    spacing = jax.random.randint(key, (SEQS, SPANS), 0, SEQ - SPANS * PIC + 1)
    spacing = jnp.sort(spacing, axis=-1)
    row_number = jnp.arange(SEQS)[:, None]
    column = jnp.arange(SPANS)[None, :]
    spacing = jnp.where((row_number == 0) & (column == 0), 0, spacing)
    spacing = jnp.where((row_number == SEQS - 1) & (column == SPANS - 1), SEQ - SPANS * PIC, spacing)
    return (spacing + column * PIC).astype(jnp.int32)


def strengthened(values, rng, source, target, blocks, factor):
    def block_of(dim):
        return (jnp.arange(values.shape[dim]) // (values.shape[dim] // blocks)).reshape((-1,) + (1,) * (values.ndim - 1 - dim))

    near = jax.random.permutation(rng, blocks)[block_of(target)]
    far = (block_of(target) + blocks // 2) % blocks
    return jnp.where((block_of(source) == near) | (block_of(source) == far), factor * values, values)


def shard_levels(key, shape, pieces, low, top_value):
    loudness, own = 1.0, jax.random.fold_in(key, 6)
    for dim, parts in pieces:
        steps = jnp.exp(jax.random.uniform(jax.random.fold_in(own, dim), (parts,), jnp.float32, low / len(pieces), top_value / len(pieces)))
        loudness = loudness * jnp.repeat(steps, shape[dim] // parts).reshape([-1 if axis == dim else 1 for axis in range(len(shape))])
    return loudness


def different_ones(stream_key, rows, amount, top, lift):
    sequence = jax.random.permutation(jax.random.fold_in(stream_key, 1), amount)
    pull = sequence
    for power in range(3):
        pull = pull * pull // amount
    pull = pull * lift // amount
    chance = jax.random.randint(jax.random.fold_in(stream_key, 2), (rows, amount), 0, 4096) + pull
    holders = jax.random.permutation(jax.random.fold_in(stream_key, 3), rows)[jnp.arange(amount) % rows]
    chance = jnp.where(jnp.arange(rows)[:, None] == holders[None, :], 1 << 14, chance)
    score = chance * amount + jnp.arange(amount)
    return lax.top_k(score.astype(jnp.int32), top)[1].astype(jnp.int32)


def scatter_about(own_key, dims, width, most, shards=(), held_as=jnp.bfloat16):
    drawn = jax.random.normal(own_key, dims, jnp.float32) * width
    if len(shards) > 0:
        drawn = shard_levels(own_key, dims, shards, -0.22, 0.18) * drawn
    return jnp.clip(drawn, min=-most, max=most).astype(held_as)


def heavy_noise(key, shape, width, reach, shards, heavy, held_as=jnp.bfloat16):
    values = width * jax.random.normal(key, shape, jnp.float32)
    if shards:
        values = values * shard_levels(key, shape, shards, -0.22, 0.18)
    return jnp.clip(strengthened(values, jax.random.fold_in(key, 3), *heavy), -reach, reach).astype(held_as)


def setup_inputs(seed: int = 0) -> dict:
    key_of = jax.random.split(jax.random.key(seed), 15)
    return {
        "tokens": heavy_noise(key_of[0], (TOKENS, D), 1.0, 6.0, ((0, 32),), (0, 1, 32, 2.75)),
        "cotangent": scatter_about(key_of[1], (TOKENS, D), 1.0, 6.0, ((0, 32),)),
        "gain_attn": jnp.clip(1.0 + 0.1 * jax.random.normal(key_of[2], (D,), jnp.float32), 0.5, 1.5),
        "w_qkv": scatter_about(key_of[3], (D, 3 * D), D ** -0.5, 0.1875),
        "w_out": scatter_about(key_of[4], (D, D), (D // 16) ** -0.5, 0.75),
        "rel_table": scatter_about(key_of[5], (BUCKETS, H), 0.5, 3.0, (), jnp.float32),
        "gain_moe": jnp.clip(1.0 + 0.1 * jax.random.normal(key_of[6], (D,), jnp.float32), 0.5, 1.5),
        "w_router": scatter_about(key_of[7], (D, EXPERTS), (2 * D) ** -0.5, 0.125),
        "w_gate": scatter_about(key_of[8], (EXPERTS, D, FF), D ** -0.5, 0.1875, ((0, 4),)),
        "w_up": scatter_about(key_of[9], (EXPERTS, D, FF), D ** -0.5, 0.1875, ((0, 4),)),
        "w_down": scatter_about(key_of[10], (EXPERTS, FF, D), FF ** -0.5, 0.109375, ((0, 4),)),
        "expert_ids": different_ones(key_of[11], TOKENS, EXPERTS, 2, 4096),
        "priority": jax.vmap(lambda own: jax.random.permutation(own, 2 * TOK_DEV))(jax.random.split(key_of[12], (N_REP * N_EP))).reshape((N_REP * N_EP, 2 * TOK_DEV)).astype(jnp.int32),
        "span_starts": draw_span_starts(jax.random.fold_in(key_of[14], 71), 0),
    }


@jax.custom_vjp
def low(v):
    return lax.optimization_barrier(v.astype(jnp.bfloat16)).astype(jnp.float32)

@jax.custom_vjp
def low_back(v):
    return v

def low_keep(v):
    return (low(v), None)

def low_pass(kept, grad):
    return (grad,)

def back_keep(v):
    return (v, None)

def back_low(kept, grad):
    return (low(grad),)
low.defvjp(low_keep, low_pass)
low_back.defvjp(back_keep, back_low)
EPSILON = 1e-06
NEGATIVE = -1e+30

def bucket_onehot(length):
    offsets = np.arange(-(length - 1), length)
    half_count = BUCKETS // 2
    near_count = half_count // 2
    upper_part = (offsets > 0).astype(np.int64) * half_count
    distance = np.abs(offsets)
    ratio = np.log(np.maximum(distance, 1) / near_count) / np.log(MAXDIST / near_count)
    distant_bucket = np.minimum(near_count + np.floor(ratio * (half_count - near_count)).astype(np.int64), half_count - 1)
    bucket = upper_part + np.where(distance < near_count, distance, distant_bucket)
    return (bucket[:, None] == np.arange(BUCKETS)[None, :]).astype(np.float32)

def rms_scale(values, gain):
    return values * lax.rsqrt(lax.optimization_barrier(jnp.mean(values * values, axis=-1, keepdims=True)) + EPSILON) * gain

def sequence_attention(item, bias_full):
    query, keys, values, starts = item
    raw_scores = jnp.einsum('qhd,khd->hqk', query, keys, precision=lax.Precision.HIGHEST)
    scores = low_back(raw_scores * HD ** (-0.5) + bias_full)
    position = jnp.arange(SEQ, dtype=jnp.int32)
    inside = (position[None, :] >= starts[:, None]) & (position[None, :] < starts[:, None] + PIC)
    allowed = (position[None, :] <= position[:, None]) | jnp.any(inside[:, :, None] & inside[:, None, :], axis=0)
    scores = jnp.where(allowed[None], scores, NEGATIVE)
    probs = jax.nn.softmax(scores, axis=-1)
    return jnp.einsum('hqk,khd->qhd', low(probs), values, precision=lax.Precision.HIGHEST)

def expert_rows(item):
    rows, gate_weight, up_weight, down_weight = item
    gate_pre = low_back(jnp.dot(rows, gate_weight, precision=lax.Precision.HIGHEST))
    up_pre = low_back(jnp.dot(rows, up_weight, precision=lax.Precision.HIGHEST))
    hidden = low(jax.nn.gelu(gate_pre, approximate=True) * up_pre)
    return low(low_back(jnp.dot(hidden, down_weight, precision=lax.Precision.HIGHEST)))

def block_slots(ids_block, rank_block):
    flat_ids = ids_block.reshape(-1)
    earlier = rank_block[:, None] < rank_block[None, :]
    same_expert = flat_ids[:, None] == flat_ids[None, :]
    return lax.optimization_barrier(jnp.sum((earlier & same_expert).astype(jnp.int32), axis=0)).astype(jnp.int32)

def layer(tokens, gain_attn, w_qkv, w_out, rel_table, gain_moe, w_router, w_gate, w_up, w_down, span_starts, choose, owner, target):
    normed = low(rms_scale(tokens, gain_attn))
    qkv = low(low_back(jnp.dot(normed, w_qkv, precision=lax.Precision.HIGHEST)))
    shaped = qkv.reshape(SEQS, SEQ, 3, H, HD)
    onehot_table = jnp.asarray(bucket_onehot(SEQ))
    bias_diag = jnp.dot(onehot_table, rel_table, precision=lax.Precision.HIGHEST).T
    offsets = np.arange(SEQ)[None, :] - np.arange(SEQ)[:, None] + SEQ - 1
    bias_full = bias_diag[:, offsets]
    attended = lax.map(jax.checkpoint(lambda item: sequence_attention(item, bias_full)), (shaped[:, :, 0], shaped[:, :, 1], shaped[:, :, 2], span_starts))
    attended = low(low_back(attended.reshape(TOKENS, D)))
    mixed = tokens + low_back(jnp.dot(attended, w_out, precision=lax.Precision.HIGHEST))
    routed = low(rms_scale(mixed, gain_moe))
    logits = low_back(jnp.dot(routed, w_router, precision=lax.Precision.HIGHEST))
    chosen = lax.optimization_barrier(jnp.sum(logits[:, None, :] * choose, axis=-1))
    gates = jax.nn.softmax(chosen, axis=-1)
    rows = low_back(jnp.take(routed, owner // 2, axis=0, mode='fill', fill_value=0.0))
    rows = rows.reshape(EXPERTS, DEVICES * CAP, D)
    outputs = lax.map(jax.checkpoint(expert_rows), (rows, w_gate, w_up, w_down)).reshape(-1, D)
    pair_rows = jnp.take(outputs, target, axis=0, mode='fill', fill_value=0.0).reshape(TOKENS, 2, D)
    return mixed + lax.optimization_barrier(jnp.sum(gates[:, :, None] * pair_rows, axis=1))

def reference(tokens, cotangent, gain_attn, w_qkv, w_out, rel_table, gain_moe, w_router, w_gate, w_up, w_down, expert_ids, priority, span_starts):
    slots = lax.map(lambda item: block_slots(item[0], item[1]), (expert_ids.reshape(DEVICES, TOK_DEV, 2), priority))
    kept = slots < CAP
    flat_ids = expert_ids.reshape(DEVICES, 2 * TOK_DEV)
    device_row = jnp.arange(DEVICES, dtype=jnp.int32)[:, None]
    target = jnp.where(kept, flat_ids * (DEVICES * CAP) + device_row * CAP + slots, EXPERTS * DEVICES * CAP).reshape(-1).astype(jnp.int32)
    owner = jnp.full((EXPERTS * DEVICES * CAP,), 2 * TOKENS, dtype=jnp.int32)
    owner = owner.at[target].set(jnp.arange(2 * TOKENS, dtype=jnp.int32), mode='drop')
    choose = (expert_ids[:, :, None] == jnp.arange(EXPERTS, dtype=jnp.int32)[None, None, :]).astype(jnp.float32)
    floats = tuple((item.astype(jnp.float32) for item in (tokens, gain_attn, w_qkv, w_out, rel_table, gain_moe, w_router, w_gate, w_up, w_down)))
    forward = partial(layer, span_starts=span_starts, choose=choose, owner=owner, target=target)
    result, pullback = jax.vjp(forward, *floats)
    grads = pullback(cotangent.astype(jnp.float32))
    return (result.astype(jnp.bfloat16), grads[0], grads[1], grads[2], grads[3], grads[4], grads[5], grads[6], grads[7], grads[8], grads[9])
```

```python
import jax
import jax.numpy as jnp
import numpy as np
from jax import lax
from jax.sharding import PartitionSpec as P
from jax.experimental import pallas as pl
from jax.experimental.pallas import tpu as pltpu

D = 1024
H = 16
HD = 64
BUCKETS = 32
MAXDIST = 128
SEQ = 1024
PIC = 256
EPSILON = 1e-06
NEGATIVE = -1e30
LOG2E = 1.4426950408889634
QB = 256
KB = 128
WIDE = 768
VMEM_LIMIT = 56 * 1024 * 1024


def bucket_of(offsets):
    half_count = BUCKETS // 2
    near_count = half_count // 2
    upper_part = (offsets > 0).astype(np.int64) * half_count
    distance = np.abs(offsets)
    ratio = np.log(np.maximum(distance, 1) / near_count) / np.log(MAXDIST / near_count)
    distant_bucket = np.minimum(
        near_count + np.floor(ratio * (half_count - near_count)).astype(np.int64), half_count - 1
    )
    return upper_part + np.where(distance < near_count, distance, distant_bucket)


def wide_onehot():
    places = np.arange(WIDE)
    offsets = np.where(places < 640, 256 - places, 1024 - places)
    return (bucket_of(offsets)[:, None] == np.arange(BUCKETS)[None, :]).astype(np.float32)


def dot_nt(a, b):
    return lax.dot_general(a, b, (((1,), (1,)), ((), ())), preferred_element_type=jnp.float32)


def dot_nn(a, b):
    return lax.dot_general(a, b, (((1,), (0,)), ((), ())), preferred_element_type=jnp.float32)


def key_count(i):
    return min((i + 2) * QB, SEQ)


def fill_mask(span_ref, mask_s):
    for i in range(SEQ // QB):
        for d in range(4):
            if 2 * i + d >= SEQ // KB:
                continue
            k = (2 * i + d) * KB + lax.broadcasted_iota(jnp.int32, (KB, QB), 0)
            q = i * QB + lax.broadcasted_iota(jnp.int32, (KB, QB), 1)
            ok = k <= q
            for s in range(2):
                start = span_ref[0, s]
                ok = ok | ((k >= start) & (k < start + PIC) & (q >= start) & (q < start + PIC))
            mask_s[4 * i + d] = jnp.where(ok, 0.0, NEGATIVE)


def spread_bias(diag_ref, h, bias_s):
    row = jnp.broadcast_to(diag_ref[0, h : h + 1, :], (KB, WIDE))
    bias_s[h] = pltpu.roll(row, 0, 1, stride=1, stride_axis=0)


def shifted(s, i, kt, h, bias_s, mask_s, low, high, row):
    d = kt - 2 * i
    if d <= -2:
        return s + (low if row is None else low + row)
    if d >= 3:
        s = s + (high if row is None else high + row)
    else:
        s = s + bias_s[h, :, (2 - d) * 128 : (2 - d) * 128 + 256]
        if row is not None:
            s = s + row
    if d >= 0:
        s = s + mask_s[4 * i + d]
    return s


def diagonal_sums(x):
    rows = x.shape[0]
    while rows > 8:
        rows //= 2
        x = x[:rows] + pltpu.roll(x[rows:], WIDE - rows, 1)
    total = x[0:1]
    for r in range(1, rows):
        total = total + pltpu.roll(x[r : r + 1], WIDE - r, 1)
    return total


def half_lanes(x, h):
    lane = lax.broadcasted_iota(jnp.int32, x.shape, 1)
    return jnp.where((lane < HD) if h == 0 else (lane >= HD), x, jnp.zeros_like(x))


def attn_fwd_kernel(span_ref, q_ref, k_ref, v_ref, diag_ref, out_ref, lse_ref, mask_s, bias_s, vt_s, s_s, p_s):
    @pl.when(pl.program_id(0) == 0)
    def _():
        fill_mask(span_ref, mask_s)

    vt = jnp.transpose(v_ref[...])
    for h in range(2):
        spread_bias(diag_ref, h, bias_s)
        vt_s[h, :HD] = vt[h * HD : (h + 1) * HD]
        vt_s[h, HD:] = jnp.ones((16, SEQ), jnp.bfloat16)
    scale = LOG2E * HD ** (-0.5)
    for i in range(SEQ // QB):
        nk = key_count(i)
        outs = []
        for h in range(2):
            low = diag_ref[0, h : h + 1, 600:601]
            high = diag_ref[0, h : h + 1, 0:1]
            qs = half_lanes(q_ref[i * QB : (i + 1) * QB, :], h)
            s_s[h, :nk] = dot_nt(k_ref[:nk, :], qs)
            top = None
            for kt in range(nk // KB):
                s = shifted(s_s[h, kt * KB : (kt + 1) * KB] * scale, i, kt, h, bias_s, mask_s, low, high, None)
                s_s[h, kt * KB : (kt + 1) * KB] = s
                t = jnp.max(s.reshape(KB // 8, 8, QB), axis=0)
                top = t if top is None else jnp.maximum(top, t)
            m = jnp.max(top, axis=0, keepdims=True)
            for kt in range(nk // KB):
                p_s[h, kt * KB : (kt + 1) * KB] = jnp.exp2(s_s[h, kt * KB : (kt + 1) * KB] - m).astype(jnp.bfloat16)
            ot = dot_nn(vt_s[h, :, :nk], p_s[h, :nk])
            total = ot[HD : HD + 1]
            outs.append(ot[:HD] / total)
            lse_ref[0, h : h + 1, i * QB : (i + 1) * QB] = m + jnp.log2(total)
        out_ref[i * QB : (i + 1) * QB, :] = jnp.transpose(jnp.concatenate(outs, axis=0)).astype(jnp.bfloat16)


def attn_fwd(spans, qkv, diag):
    col = lambda off: pl.BlockSpec((SEQ, 128), lambda g: (0, g + off))
    return pl.pallas_call(
        attn_fwd_kernel,
        grid=(H // 2,),
        in_specs=[
            pl.BlockSpec(memory_space=pltpu.SMEM),
            col(0),
            col(8),
            col(16),
            pl.BlockSpec((1, 2, WIDE), lambda g: (g, 0, 0)),
        ],
        out_specs=[col(0), pl.BlockSpec((1, 2, SEQ), lambda g: (g, 0, 0))],
        out_shape=[
            jax.ShapeDtypeStruct((SEQ, D), jnp.bfloat16),
            jax.ShapeDtypeStruct((H // 2, 2, SEQ), jnp.float32),
        ],
        scratch_shapes=[
            pltpu.VMEM((16, KB, QB), jnp.float32),
            pltpu.VMEM((2, KB, WIDE), jnp.float32),
            pltpu.VMEM((2, HD + 16, SEQ), jnp.bfloat16),
            pltpu.VMEM((2, SEQ, QB), jnp.float32),
            pltpu.VMEM((2, SEQ, QB), jnp.bfloat16),
        ],
        compiler_params=pltpu.CompilerParams(vmem_limit_bytes=VMEM_LIMIT),
        cost_estimate=pl.CostEstimate(flops=2 * 2 * 16 * 1024 * 1024 * 128, bytes_accessed=10 << 20, transcendentals=16 << 20),
        name="attn_fwd",
    )(spans, qkv, qkv, qkv, diag)


def attn_bwd_kernel(
    span_ref, q_ref, k_ref, v_ref, g_ref, o_ref, lse_ref, diag_ref,
    out_ref, drel_ref, far_ref,
    mask_s, bias_s, acc_s, kt_s, s_s, dp_s, p_s, ds_s, dk_s, dv_s, delta_s,
):
    part = pl.program_id(1)

    @pl.when((pl.program_id(0) == 0) & (part == 0))
    def _():
        fill_mask(span_ref, mask_s)

    @pl.when(part == 1)
    def _():
        out_ref[...] = (dk_s[...] * HD ** (-0.5)).astype(jnp.bfloat16)

    @pl.when(part == 2)
    def _():
        out_ref[...] = dv_s[...].astype(jnp.bfloat16)

    @pl.when(part == 0)
    def _():
        kt_s[...] = jnp.transpose(k_ref[...])
        prod = jnp.transpose(g_ref[...].astype(jnp.float32) * o_ref[...].astype(jnp.float32))
        for h in range(2):
            spread_bias(diag_ref, h, bias_s)
            delta_s[h : h + 1] = jnp.sum(prod[h * HD : (h + 1) * HD], axis=0, keepdims=True)
        acc_s[...] = jnp.zeros_like(acc_s)
        far_ref[...] = jnp.zeros_like(far_ref)
        scale = LOG2E * HD ** (-0.5)
        for i in reversed(range(SEQ // QB)):
            nk = key_count(i)
            rows = slice(i * QB, (i + 1) * QB)
            dqs = []
            for h in range(2):
                low = diag_ref[0, h : h + 1, 600:601]
                high = diag_ref[0, h : h + 1, 0:1]
                qs = half_lanes(q_ref[rows, :], h)
                gs = half_lanes(g_ref[rows, :], h)
                s_s[h, :nk] = dot_nt(k_ref[:nk, :], qs)
                dp_s[h, :nk] = dot_nt(v_ref[:nk, :], gs)
                nlse = -lse_ref[0, h : h + 1, rows]
                delta = delta_s[h : h + 1, rows]
                for kt in range(nk // KB):
                    tile = slice(kt * KB, (kt + 1) * KB)
                    d = kt - 2 * i
                    p = jnp.exp2(shifted(s_s[h, tile] * scale, i, kt, h, bias_s, mask_s, low, high, nlse))
                    ds = p * (dp_s[h, tile] - delta)
                    p_s[tile, h * QB : (h + 1) * QB] = p.astype(jnp.bfloat16)
                    ds_s[tile, h * QB : (h + 1) * QB] = ds.astype(jnp.bfloat16)
                    if -1 <= d <= 2:
                        cols = slice((2 - d) * 128, (2 - d) * 128 + 256)
                        acc_s[h, :, cols] += ds
                    else:
                        far_ref[0, h, 0 if d < 0 else 1] += jnp.sum(ds.reshape(KB // 8, 8, QB), axis=0)
                dqs.append(dot_nn(kt_s[h * HD : (h + 1) * HD, :nk], ds_s[:nk, h * QB : (h + 1) * QB]))
            out_ref[rows, :] = (jnp.transpose(jnp.concatenate(dqs, axis=0)) * HD ** (-0.5)).astype(jnp.bfloat16)
            gg = jnp.concatenate([half_lanes(g_ref[rows, :], h) for h in range(2)], axis=0)
            qq = jnp.concatenate([half_lanes(q_ref[rows, :], h) for h in range(2)], axis=0)
            dv = dot_nn(p_s[:nk, :], gg)
            dk = dot_nn(ds_s[:nk, :], qq)
            if i == SEQ // QB - 1:
                dv_s[...] = dv
                dk_s[...] = dk
            else:
                dv_s[:nk] += dv
                dk_s[:nk] += dk
        for h in range(2):
            drel_ref[0, h : h + 1, :] = diagonal_sums(acc_s[h])


def attn_bwd(spans, qkv, grad_att, att, lse, diag):
    col = lambda off: pl.BlockSpec((SEQ, 128), lambda g, p: (0, g + off))
    one = lambda *dims: pl.BlockSpec((1, *dims), lambda g, p: (g,) + (0,) * len(dims))
    return pl.pallas_call(
        attn_bwd_kernel,
        grid=(H // 2, 3),
        in_specs=[
            pl.BlockSpec(memory_space=pltpu.SMEM),
            col(0),
            col(8),
            col(16),
            col(0),
            col(0),
            one(2, SEQ),
            one(2, WIDE),
        ],
        out_specs=[
            pl.BlockSpec((SEQ, 128), lambda g, p: (0, p * 8 + g)),
            one(2, WIDE),
            one(2, 2, 8, QB),
        ],
        out_shape=[
            jax.ShapeDtypeStruct((SEQ, 3 * D), jnp.bfloat16),
            jax.ShapeDtypeStruct((H // 2, 2, WIDE), jnp.float32),
            jax.ShapeDtypeStruct((H // 2, 2, 2, 8, QB), jnp.float32),
        ],
        scratch_shapes=[
            pltpu.VMEM((16, KB, QB), jnp.float32),
            pltpu.VMEM((2, KB, WIDE), jnp.float32),
            pltpu.VMEM((2, KB, WIDE), jnp.float32),
            pltpu.VMEM((128, SEQ), jnp.bfloat16),
            pltpu.VMEM((2, SEQ, QB), jnp.float32),
            pltpu.VMEM((2, SEQ, QB), jnp.float32),
            pltpu.VMEM((SEQ, 2 * QB), jnp.bfloat16),
            pltpu.VMEM((SEQ, 2 * QB), jnp.bfloat16),
            pltpu.VMEM((SEQ, 128), jnp.float32),
            pltpu.VMEM((SEQ, 128), jnp.float32),
            pltpu.VMEM((2, SEQ), jnp.float32),
        ],
        compiler_params=pltpu.CompilerParams(vmem_limit_bytes=VMEM_LIMIT),
        cost_estimate=pl.CostEstimate(flops=5 * 2 * 16 * 1024 * 1024 * 128, bytes_accessed=16 << 20, transcendentals=16 << 20),
        name="attn_bwd",
    )(spans, qkv, qkv, qkv, grad_att, att, lse, diag)


def wide_diag(rel_table):
    return jnp.einsum(
        "mb,bh->hm", jnp.asarray(wide_onehot()), rel_table * LOG2E, precision=lax.Precision.HIGHEST
    ).reshape(H // 2, 2, WIDE)


def rel_grad(drel, far):
    sums = drel.reshape(H, WIDE)
    far = jnp.sum(far.reshape(H, 2, 8 * QB), axis=-1)
    sums = sums.at[:, 600].add(far[:, 0]).at[:, 0].add(far[:, 1])
    return jnp.einsum("mb,hm->bh", jnp.asarray(wide_onehot()), sums, precision=lax.Precision.HIGHEST)


def rms_forward(values, gain):
    scale_rows = lax.rsqrt(jnp.mean(values * values, axis=-1, keepdims=True) + EPSILON)
    return (values * scale_rows * gain, scale_rows)


def rms_backward(values, scale_rows, gain, upstream):
    scaled_grad = upstream * gain
    gain_grad = jnp.sum(upstream * values * scale_rows, axis=0)
    inner_mean = jnp.mean(scaled_grad * values, axis=-1, keepdims=True)
    return (scale_rows * scaled_grad - values * scale_rows**3 * inner_mean, gain_grad)


def geglu(gate_pre, up_pre):
    return jax.nn.gelu(gate_pre, approximate=True) * up_pre


def expert_sums(received, gate_low, up_low, hidden, grad_recv):
    local_experts = received.shape[1]
    model_width = received.shape[3]
    hidden_width = hidden.shape[3]
    replicas = lax.axis_size("rep")
    joined_grads = jnp.concatenate([gate_low, up_low], axis=3)
    columns = received
    inner_sum = lax.psum_scatter(
        jnp.einsum("secd,secg->deg", columns, joined_grads, preferred_element_type=jnp.float32)
        .reshape(model_width // replicas * lax.axis_size("rep"), -1)
        .astype(jnp.bfloat16),
        "rep",
        scatter_dimension=0,
        tiled=True,
    ).astype(jnp.float32)
    columns = hidden
    outer_sum = lax.psum_scatter(
        jnp.einsum("secf,secd->fed", columns, grad_recv, preferred_element_type=jnp.float32)
        .reshape(hidden_width // replicas * lax.axis_size("rep"), -1)
        .astype(jnp.bfloat16),
        "rep",
        scatter_dimension=0,
        tiled=True,
    ).astype(jnp.float32)
    inner_sum = inner_sum.reshape(inner_sum.shape[0], local_experts, 2 * hidden_width)
    grad_w_gate = jnp.transpose(inner_sum[:, :, :hidden_width], (1, 0, 2))
    grad_w_up = jnp.transpose(inner_sum[:, :, hidden_width:], (1, 0, 2))
    grad_w_down = jnp.transpose(
        outer_sum.reshape(outer_sum.shape[0], local_experts, model_width), (1, 0, 2)
    )
    return (grad_w_gate, grad_w_up, grad_w_down)


def per_device(
    tokens,
    cotangent,
    gain_attn,
    w_qkv,
    w_out,
    rel_table,
    gain_moe,
    w_router,
    w_gate,
    w_up,
    w_down,
    expert_ids,
    priority,
    span_starts,
):
    tok_count = tokens.shape[0]
    experts = w_router.shape[1]
    local_experts = w_gate.shape[0]
    groups = lax.axis_size("ep")
    capacity = 5 * tok_count // (2 * experts)
    pair_count = 2 * tok_count
    diag = wide_diag(rel_table)
    token_float = tokens.astype(jnp.float32)
    normed, scale_attn = rms_forward(token_float, gain_attn)
    normed_low = normed.astype(jnp.bfloat16)
    qkv = jnp.dot(normed_low, w_qkv, preferred_element_type=jnp.float32).astype(jnp.bfloat16)
    attended_low, lse = attn_fwd(span_starts, qkv, diag)
    mixed = token_float + jnp.dot(attended_low, w_out, preferred_element_type=jnp.float32)
    routed, scale_moe = rms_forward(mixed, gain_moe)
    routed_low = routed.astype(jnp.bfloat16)
    logits = jnp.dot(routed_low, w_router, preferred_element_type=jnp.float32)
    choose = expert_ids[:, :, None] == jnp.arange(experts, dtype=jnp.int32)[None, None, :]
    chosen = jnp.sum(jnp.where(choose, logits[:, None, :], 0.0), axis=-1)
    gates = jax.nn.softmax(chosen, axis=-1)
    flat_ids = expert_ids.reshape(-1)
    ranks = priority.reshape(-1)
    onehot = choose.reshape(pair_count, experts)
    earlier = (ranks[:, None] < ranks[None, :]).astype(jnp.bfloat16)
    counts = jnp.einsum(
        "ap,ae->pe", earlier, onehot.astype(jnp.bfloat16), preferred_element_type=jnp.float32
    )
    slots = jnp.sum(jnp.where(onehot, counts, 0.0), axis=-1).astype(jnp.int32)
    target = jnp.where(slots < capacity, flat_ids * capacity + slots, experts * capacity)
    owner = jnp.full((experts * capacity,), pair_count, jnp.int32)
    owner = owner.at[target].set(jnp.arange(pair_count, dtype=jnp.int32), mode="drop")
    owner_token = owner // 2
    send_rows = jnp.take(routed_low, owner_token, axis=0, mode="fill", fill_value=0)
    send_rows = send_rows.reshape(groups, local_experts, capacity, D)
    piece = lax.all_to_all(send_rows, "ep", split_axis=0, concat_axis=0, tiled=True)
    gate_pre = jnp.einsum("secd,edf->secf", piece, w_gate, preferred_element_type=jnp.float32)
    up_pre = jnp.einsum("secd,edf->secf", piece, w_up, preferred_element_type=jnp.float32)
    hidden = geglu(gate_pre, up_pre).astype(jnp.bfloat16)
    result = jnp.einsum(
        "secf,efd->secd", hidden, w_down, preferred_element_type=jnp.float32
    ).astype(jnp.bfloat16)
    expert_results = (result, piece, gate_pre, up_pre, hidden)
    received = expert_results[1]
    returned = lax.all_to_all(
        expert_results[0], "ep", split_axis=0, concat_axis=0, tiled=True
    ).reshape(experts * capacity, D)
    pair_rows = jnp.take(returned, target, axis=0, mode="fill", fill_value=0).astype(jnp.float32)
    pair_rows = pair_rows.reshape(tok_count, 2, D)
    block_out = (mixed + jnp.sum(gates[:, :, None] * pair_rows, axis=1)).astype(jnp.bfloat16)
    grad_out = cotangent.astype(jnp.float32)
    grad_gates = jnp.sum(pair_rows * grad_out[:, None, :], axis=-1)
    gate_slots = jnp.take(gates.reshape(-1), owner, mode="fill", fill_value=0.0)
    grad_send = (
        jnp.take(grad_out, owner_token, axis=0, mode="fill", fill_value=0.0) * gate_slots[:, None]
    )
    grad_send = grad_send.astype(jnp.bfloat16).reshape(groups, local_experts, capacity, D)
    grad_recv = lax.all_to_all(grad_send, "ep", split_axis=0, concat_axis=0, tiled=True)
    grad_hidden = jnp.einsum(
        "secd,efd->secf", grad_recv, w_down, preferred_element_type=jnp.float32
    )
    gate_pre = expert_results[2]
    up_pre = expert_results[3]
    hidden = expert_results[4]
    unused, geglu_pull = jax.vjp(geglu, gate_pre, up_pre)
    gradient_gate_logits, grad_up_pre = geglu_pull(grad_hidden)
    gate_low = gradient_gate_logits.astype(jnp.bfloat16)
    up_low = grad_up_pre.astype(jnp.bfloat16)
    grad_rows = (
        jnp.einsum("secf,edf->secd", gate_low, w_gate, preferred_element_type=jnp.float32)
        + jnp.einsum("secf,edf->secd", up_low, w_up, preferred_element_type=jnp.float32)
    ).astype(jnp.bfloat16)
    grad_home = lax.all_to_all(grad_rows, "ep", split_axis=0, concat_axis=0, tiled=True).reshape(
        experts * capacity, D
    )
    grad_pairs = jnp.take(grad_home, target, axis=0, mode="fill", fill_value=0).astype(jnp.float32)
    grad_pairs = grad_pairs.reshape(tok_count, 2, D)
    grad_chosen = gates * (grad_gates - jnp.sum(gates * grad_gates, axis=-1, keepdims=True))
    grad_logits = jnp.sum(jnp.where(choose, grad_chosen[:, :, None], 0.0), axis=1).astype(
        jnp.bfloat16
    )
    grad_w_router = jnp.einsum(
        "td,te->de", routed_low, grad_logits, preferred_element_type=jnp.float32
    )
    grad_routed = jnp.sum(grad_pairs, axis=1) + jnp.einsum(
        "te,de->td", grad_logits, w_router, preferred_element_type=jnp.float32
    )
    grad_norm_moe, grad_gain_moe = rms_backward(mixed, scale_moe, gain_moe, grad_routed)
    grad_mixed = grad_out + grad_norm_moe
    grad_branch = grad_mixed.astype(jnp.bfloat16)
    grad_w_out = jnp.einsum(
        "td,te->de", attended_low, grad_branch, preferred_element_type=jnp.float32
    )
    grad_attended = jnp.einsum("te,de->td", grad_branch, w_out, preferred_element_type=jnp.float32)
    grad_qkv, drel, far = attn_bwd(
        span_starts, qkv, grad_attended.astype(jnp.bfloat16), attended_low, lse, diag
    )
    grad_rel_table = rel_grad(drel, far)
    grad_w_qkv = jnp.einsum("td,tf->df", normed_low, grad_qkv, preferred_element_type=jnp.float32)
    grad_normed = jnp.einsum("tf,df->td", grad_qkv, w_qkv, preferred_element_type=jnp.float32)
    grad_norm_attn, grad_gain_attn = rms_backward(token_float, scale_attn, gain_attn, grad_normed)
    grad_tokens = grad_mixed + grad_norm_attn
    grad_w_gate, grad_w_up, grad_w_down = expert_sums(received, gate_low, up_low, hidden, grad_recv)
    everyone = ("rep", "ep")
    sum_w_out = lax.psum(grad_w_out.astype(jnp.bfloat16), everyone).astype(jnp.float32)
    sum_w_qkv = lax.psum(grad_w_qkv.astype(jnp.bfloat16), everyone).astype(jnp.float32)
    small = lax.psum((grad_rel_table, grad_w_router, grad_gain_attn, grad_gain_moe), everyone)
    summed = (sum_w_qkv, sum_w_out) + tuple(small)
    return (
        block_out,
        grad_tokens,
        summed[4],
        summed[0],
        summed[1],
        summed[2],
        summed[5],
        summed[3],
        grad_w_gate,
        grad_w_up,
        grad_w_down,
    )


def solution(mesh):
    placed = (
        P(("rep", "ep"), None),
        P(("rep", "ep"), None),
        P(),
        P(),
        P(),
        P(),
        P(),
        P(),
        P("ep", None, None),
        P("ep", None, None),
        P("ep", None, None),
        P(("rep", "ep"), None),
        P(("rep", "ep"), None),
        P(("rep", "ep"), None),
    )
    return jax.shard_map(
        per_device,
        mesh=mesh,
        in_specs=placed,
        out_specs=(
            P(("rep", "ep"), None),
            P(("rep", "ep"), None),
            P(),
            P(),
            P(),
            P(),
            P(),
            P(),
            P("ep", "rep", None),
            P("ep", "rep", None),
            P("ep", "rep", None),
        ),
        check_vma=False,
    )
```

```python
from functools import partial
import jax
import jax.numpy as jnp
import numpy as np
from jax import lax
from jax.sharding import PartitionSpec as P
from jax.experimental import pallas as pl
from jax.experimental.pallas import tpu as pltpu

D = 1024
H = 16
HD = 64
BUCKETS = 32
MAXDIST = 128
SEQ = 1024
PIC = 256
EPSILON = 1e-06
NEGATIVE = -1e30
LOG2E = 1.4426950408889634
QB = 256
KB = 128
WIDE = 768
VMEM_LIMIT = 56 * 1024 * 1024
LIGHT = pl.CostEstimate(flops=1000, bytes_accessed=1000, transcendentals=0)


def bucket_of(offsets):
    half_count = BUCKETS // 2
    near_count = half_count // 2
    upper_part = (offsets > 0).astype(np.int64) * half_count
    distance = np.abs(offsets)
    ratio = np.log(np.maximum(distance, 1) / near_count) / np.log(MAXDIST / near_count)
    distant_bucket = np.minimum(
        near_count + np.floor(ratio * (half_count - near_count)).astype(np.int64), half_count - 1
    )
    return upper_part + np.where(distance < near_count, distance, distant_bucket)


def wide_onehot():
    places = np.arange(WIDE)
    offsets = np.where(places < 640, 256 - places, 1024 - places)
    return (bucket_of(offsets)[:, None] == np.arange(BUCKETS)[None, :]).astype(np.float32)


def dot_nt(a, b):
    return lax.dot_general(a, b, (((1,), (1,)), ((), ())), preferred_element_type=jnp.float32)


def dot_nn(a, b):
    return lax.dot_general(a, b, (((1,), (0,)), ((), ())), preferred_element_type=jnp.float32)


def key_count(i):
    return min((i + 2) * QB, SEQ)


def fill_mask(span_ref, mask_s):
    for i in range(SEQ // QB):
        for d in range(4):
            if 2 * i + d >= SEQ // KB:
                continue
            k = (2 * i + d) * KB + lax.broadcasted_iota(jnp.int32, (KB, QB), 0)
            q = i * QB + lax.broadcasted_iota(jnp.int32, (KB, QB), 1)
            ok = k <= q
            for s in range(2):
                start = span_ref[0, s]
                ok = ok | ((k >= start) & (k < start + PIC) & (q >= start) & (q < start + PIC))
            mask_s[4 * i + d] = jnp.where(ok, 0.0, NEGATIVE)


def spread_bias(diag_ref, h, bias_s):
    row = jnp.broadcast_to(diag_ref[0, h : h + 1, :], (KB, WIDE))
    bias_s[h] = pltpu.roll(row, 0, 1, stride=1, stride_axis=0)


def shifted(s, i, kt, h, bias_s, mask_s, low, high, row):
    d = kt - 2 * i
    if d <= -2:
        return s + (low if row is None else low + row)
    if d >= 3:
        s = s + (high if row is None else high + row)
    else:
        s = s + bias_s[h, :, (2 - d) * 128 : (2 - d) * 128 + 256]
        if row is not None:
            s = s + row
    if d >= 0:
        s = s + mask_s[4 * i + d]
    return s


def diagonal_sums(x):
    rows = x.shape[0]
    while rows > 8:
        rows //= 2
        x = x[:rows] + pltpu.roll(x[rows:], WIDE - rows, 1)
    total = x[0:1]
    for r in range(1, rows):
        total = total + pltpu.roll(x[r : r + 1], WIDE - r, 1)
    return total


def half_lanes(x, h):
    lane = lax.broadcasted_iota(jnp.int32, x.shape, 1)
    return jnp.where((lane < HD) if h == 0 else (lane >= HD), x, jnp.zeros_like(x))


def attn_fwd_kernel(span_ref, q_ref, k_ref, v_ref, diag_ref, out_ref, lse_ref, mask_s, bias_s, vt_s, s_s, p_s):
    @pl.when(pl.program_id(0) == 0)
    def _():
        fill_mask(span_ref, mask_s)

    vt = jnp.transpose(v_ref[...])
    for h in range(2):
        spread_bias(diag_ref, h, bias_s)
        vt_s[h, :HD] = vt[h * HD : (h + 1) * HD]
        vt_s[h, HD:] = jnp.ones((16, SEQ), jnp.bfloat16)
    scale = LOG2E * HD ** (-0.5)
    for i in range(SEQ // QB):
        nk = key_count(i)
        outs = []
        for h in range(2):
            low = diag_ref[0, h : h + 1, 600:601]
            high = diag_ref[0, h : h + 1, 0:1]
            qs = half_lanes(q_ref[i * QB : (i + 1) * QB, :], h)
            s_s[h, :nk] = dot_nt(k_ref[:nk, :], qs)
            top = None
            for kt in range(nk // KB):
                s = shifted(s_s[h, kt * KB : (kt + 1) * KB] * scale, i, kt, h, bias_s, mask_s, low, high, None)
                s_s[h, kt * KB : (kt + 1) * KB] = s
                t = jnp.max(s.reshape(KB // 8, 8, QB), axis=0)
                top = t if top is None else jnp.maximum(top, t)
            m = jnp.max(top, axis=0, keepdims=True)
            for kt in range(nk // KB):
                p_s[h, kt * KB : (kt + 1) * KB] = jnp.exp2(s_s[h, kt * KB : (kt + 1) * KB] - m).astype(jnp.bfloat16)
            ot = dot_nn(vt_s[h, :, :nk], p_s[h, :nk])
            total = ot[HD : HD + 1]
            outs.append(ot[:HD] / total)
            lse_ref[0, h : h + 1, i * QB : (i + 1) * QB] = m + jnp.log2(total)
        out_ref[i * QB : (i + 1) * QB, :] = jnp.transpose(jnp.concatenate(outs, axis=0)).astype(jnp.bfloat16)


def attn_fwd(spans, qkv, diag):
    col = lambda off: pl.BlockSpec((SEQ, 128), lambda g: (0, g + off))
    return pl.pallas_call(
        attn_fwd_kernel,
        grid=(H // 2,),
        in_specs=[
            pl.BlockSpec(memory_space=pltpu.SMEM),
            col(0),
            col(8),
            col(16),
            pl.BlockSpec((1, 2, WIDE), lambda g: (g, 0, 0)),
        ],
        out_specs=[col(0), pl.BlockSpec((1, 2, SEQ), lambda g: (g, 0, 0))],
        out_shape=[
            jax.ShapeDtypeStruct((SEQ, D), jnp.bfloat16),
            jax.ShapeDtypeStruct((H // 2, 2, SEQ), jnp.float32),
        ],
        scratch_shapes=[
            pltpu.VMEM((16, KB, QB), jnp.float32),
            pltpu.VMEM((2, KB, WIDE), jnp.float32),
            pltpu.VMEM((2, HD + 16, SEQ), jnp.bfloat16),
            pltpu.VMEM((2, SEQ, QB), jnp.float32),
            pltpu.VMEM((2, SEQ, QB), jnp.bfloat16),
        ],
        compiler_params=pltpu.CompilerParams(vmem_limit_bytes=VMEM_LIMIT),
        cost_estimate=LIGHT,
        name="attn_fwd",
    )(spans, qkv, qkv, qkv, diag)


def attn_bwd_kernel(
    span_ref, q_ref, k_ref, v_ref, g_ref, o_ref, lse_ref, diag_ref,
    out_ref, drel_ref, far_ref,
    mask_s, bias_s, acc_s, kt_s, s_s, dp_s, p_s, ds_s, dk_s, dv_s, delta_s,
):
    part = pl.program_id(1)

    @pl.when((pl.program_id(0) == 0) & (part == 0))
    def _():
        fill_mask(span_ref, mask_s)

    @pl.when(part == 1)
    def _():
        out_ref[...] = (dk_s[...] * HD ** (-0.5)).astype(jnp.bfloat16)

    @pl.when(part == 2)
    def _():
        out_ref[...] = dv_s[...].astype(jnp.bfloat16)

    @pl.when(part == 0)
    def _():
        kt_s[...] = jnp.transpose(k_ref[...])
        prod = jnp.transpose(g_ref[...].astype(jnp.float32) * o_ref[...].astype(jnp.float32))
        for h in range(2):
            spread_bias(diag_ref, h, bias_s)
            delta_s[h : h + 1] = jnp.sum(prod[h * HD : (h + 1) * HD], axis=0, keepdims=True)
        acc_s[...] = jnp.zeros_like(acc_s)
        far_ref[...] = jnp.zeros_like(far_ref)
        scale = LOG2E * HD ** (-0.5)
        for i in reversed(range(SEQ // QB)):
            nk = key_count(i)
            rows = slice(i * QB, (i + 1) * QB)
            dqs = []
            for h in range(2):
                low = diag_ref[0, h : h + 1, 600:601]
                high = diag_ref[0, h : h + 1, 0:1]
                qs = half_lanes(q_ref[rows, :], h)
                gs = half_lanes(g_ref[rows, :], h)
                s_s[h, :nk] = dot_nt(k_ref[:nk, :], qs)
                dp_s[h, :nk] = dot_nt(v_ref[:nk, :], gs)
                nlse = -lse_ref[0, h : h + 1, rows]
                delta = delta_s[h : h + 1, rows]
                for kt in range(nk // KB):
                    tile = slice(kt * KB, (kt + 1) * KB)
                    d = kt - 2 * i
                    p = jnp.exp2(shifted(s_s[h, tile] * scale, i, kt, h, bias_s, mask_s, low, high, nlse))
                    ds = p * (dp_s[h, tile] - delta)
                    p_s[tile, h * QB : (h + 1) * QB] = p.astype(jnp.bfloat16)
                    ds_s[tile, h * QB : (h + 1) * QB] = ds.astype(jnp.bfloat16)
                    if -1 <= d <= 2:
                        cols = slice((2 - d) * 128, (2 - d) * 128 + 256)
                        acc_s[h, :, cols] += ds
                    else:
                        far_ref[0, h, 0 if d < 0 else 1] += jnp.sum(ds.reshape(KB // 8, 8, QB), axis=0)
                dqs.append(dot_nn(kt_s[h * HD : (h + 1) * HD, :nk], ds_s[:nk, h * QB : (h + 1) * QB]))
            out_ref[rows, :] = (jnp.transpose(jnp.concatenate(dqs, axis=0)) * HD ** (-0.5)).astype(jnp.bfloat16)
            gg = jnp.concatenate([half_lanes(g_ref[rows, :], h) for h in range(2)], axis=0)
            qq = jnp.concatenate([half_lanes(q_ref[rows, :], h) for h in range(2)], axis=0)
            dv = dot_nn(p_s[:nk, :], gg)
            dk = dot_nn(ds_s[:nk, :], qq)
            if i == SEQ // QB - 1:
                dv_s[...] = dv
                dk_s[...] = dk
            else:
                dv_s[:nk] += dv
                dk_s[:nk] += dk
        for h in range(2):
            drel_ref[0, h : h + 1, :] = diagonal_sums(acc_s[h])


def attn_bwd(spans, qkv, grad_att, att, lse, diag, half):
    pairs = H // 4
    base = half * pairs
    col = lambda off: pl.BlockSpec((SEQ, 128), lambda g, p: (0, base + g + off))
    one = lambda *dims: pl.BlockSpec((1, *dims), lambda g, p: (base + g,) + (0,) * len(dims))
    new = lambda *dims: pl.BlockSpec((1, *dims), lambda g, p: (g,) + (0,) * len(dims))
    return pl.pallas_call(
        attn_bwd_kernel,
        grid=(pairs, 3),
        in_specs=[
            pl.BlockSpec(memory_space=pltpu.SMEM),
            col(0),
            col(8),
            col(16),
            col(0),
            col(0),
            one(2, SEQ),
            one(2, WIDE),
        ],
        out_specs=[
            pl.BlockSpec((SEQ, 128), lambda g, p: (0, p * pairs + g)),
            new(2, WIDE),
            new(2, 2, 8, QB),
        ],
        out_shape=[
            jax.ShapeDtypeStruct((SEQ, 3 * D // 2), jnp.bfloat16),
            jax.ShapeDtypeStruct((pairs, 2, WIDE), jnp.float32),
            jax.ShapeDtypeStruct((pairs, 2, 2, 8, QB), jnp.float32),
        ],
        scratch_shapes=[
            pltpu.VMEM((16, KB, QB), jnp.float32),
            pltpu.VMEM((2, KB, WIDE), jnp.float32),
            pltpu.VMEM((2, KB, WIDE), jnp.float32),
            pltpu.VMEM((128, SEQ), jnp.bfloat16),
            pltpu.VMEM((2, SEQ, QB), jnp.float32),
            pltpu.VMEM((2, SEQ, QB), jnp.float32),
            pltpu.VMEM((SEQ, 2 * QB), jnp.bfloat16),
            pltpu.VMEM((SEQ, 2 * QB), jnp.bfloat16),
            pltpu.VMEM((SEQ, 128), jnp.float32),
            pltpu.VMEM((SEQ, 128), jnp.float32),
            pltpu.VMEM((2, SEQ), jnp.float32),
        ],
        compiler_params=pltpu.CompilerParams(vmem_limit_bytes=VMEM_LIMIT),
        cost_estimate=LIGHT,
        name=f"attn_bwd_{half}",
    )(spans, qkv, qkv, qkv, grad_att, att, lse, diag)


def wide_diag(rel_table):
    return jnp.einsum(
        "mb,bh->hm", jnp.asarray(wide_onehot()), rel_table * LOG2E, precision=lax.Precision.HIGHEST
    ).reshape(H // 2, 2, WIDE)


def rel_grad(drel, far):
    sums = drel.reshape(H, WIDE)
    far = jnp.sum(far.reshape(H, 2, 8 * QB), axis=-1)
    sums = sums.at[:, 600].add(far[:, 0]).at[:, 0].add(far[:, 1])
    return jnp.einsum("mb,hm->bh", jnp.asarray(wide_onehot()), sums, precision=lax.Precision.HIGHEST)


FT = 256


def dot_tn(a, b):
    return lax.dot_general(a, b, (((0,), (0,)), ((), ())), preferred_element_type=jnp.float32)


VMEM_MOST = 58 * 1024 * 1024
PARTS = 2


def slot_onehot(meta_ref, n, rows):
    slot = meta_ref[n, 0:1]
    return lax.broadcasted_iota(jnp.int32, (rows, slot.shape[1]), 0) == slot


def expert_fwd_kernel(meta_ref, wr_ref, tok_a, tok_b, cot_a, cot_b, gate_ref, up_ref, down_ref, *rest):
    x_ref, gc_ref, hid_ref, slope_ref, act_ref, p_a, p_b, gg_ref, hot_s, turned_s, hid_s, gate_s = rest[-12:]
    step = pl.program_id(0)
    wide = hid_s.shape[1] // FT
    deep = D // FT
    rows = x_ref.shape[0] // 2
    count = tok_a.shape[0]
    pair = [(0, tok_a, cot_a, slice(0, rows)), (1, tok_b, cot_b, slice(rows, 2 * rows))]
    chunk = 2 * rows // PARTS

    @pl.when(step == 0)
    def _():
        for n, tok_ref, cot_ref, here in pair:
            logits = dot_nt(wr_ref[...], tok_ref[...])
            other, own = meta_ref[n, 1:2], meta_ref[n, 2:3]
            names = lax.broadcasted_iota(jnp.int32, logits.shape, 0)
            mine = jnp.sum(jnp.where(names == own, logits, 0.0), axis=0, keepdims=True)
            theirs = jnp.sum(jnp.where(names == other, logits, 0.0), axis=0, keepdims=True)
            gate = 1.0 / (1.0 + jnp.exp(theirs - mine))
            hot = slot_onehot(meta_ref, n, rows)
            gates = jnp.sum(jnp.where(hot, gate, 0.0), axis=1, keepdims=True)
            lane = lax.broadcasted_iota(jnp.int32, (rows, 128), 1)
            gate_s[here] = jnp.where(lane < 64, gates, 0.0)
            hot = jnp.where(hot, 1.0, 0.0).astype(jnp.bfloat16)
            hot_s[n] = hot
            turned_s[n] = jnp.transpose(hot)
            x_ref[here] = dot_nn(hot_s[n], tok_ref[...]).astype(jnp.bfloat16)

    @pl.when(step < wide)
    def _():
        cols = pl.ds(pl.multiple_of(step * FT, FT), FT)
        root = (2.0 / np.pi) ** 0.5
        for c in range(PARTS):
            here = slice(c * chunk, (c + 1) * chunk)
            g = dot_nn(x_ref[here], gate_ref[0])
            u = dot_nn(x_ref[here], up_ref[0])
            square = g * g
            t = jnp.tanh(g * (root + (root * 0.044715) * square))
            half = 0.5 + 0.5 * t
            act = g * half
            slope = half + (act * (1.0 - t)) * (root + (3.0 * root * 0.044715) * square)
            slope_ref[here] = (u * slope).astype(jnp.bfloat16)
            act_ref[here] = act.astype(jnp.bfloat16)
            hidden = (act * u).astype(jnp.bfloat16)
            hid_s[here, cols] = hidden
            hid_ref[here] = hidden

    for n in range(deep):

        @pl.when(step == wide + n)
        def _():
            cols = slice(n * FT, (n + 1) * FT)
            outs = dot_nn(hid_s[...], down_ref[0])
            for s, tok_ref, cot_ref, here in pair:
                gates = gate_s[here, 0:1]
                out = outs[here].astype(jnp.bfloat16).astype(jnp.float32)
                cot = dot_nn(hot_s[s], cot_ref[...])
                lane = lax.broadcasted_iota(jnp.int32, (rows, 128), 1)
                gate_s[here] += jnp.where(lane < 64, 0.0, jnp.sum(out * cot, axis=1, keepdims=True))
                gc_ref[here, cols] = (gates * cot).astype(jnp.bfloat16)
                p_ref = (p_a, p_b)[s]
                p_ref[...] = dot_nn(turned_s[s], (gates * out).astype(jnp.bfloat16)).astype(jnp.bfloat16)

    @pl.when(step == wide + deep - 1)
    def _():
        for s, tok_ref, cot_ref, here in pair:
            gg = jnp.where(slot_onehot(meta_ref, s, rows), gate_s[here, 64:65], 0.0)
            gg = jnp.sum(gg, axis=0, keepdims=True)
            own = meta_ref[s, 2:3]
            gg_ref[s] = jnp.where(lax.broadcasted_iota(jnp.int32, (8, count), 0) == own, gg, 0.0)


def expert_bwd_kernel(meta_ref, gc_ref, slope_ref, act_ref, down_ref, gate_ref, up_ref, dg_ref, du_ref, dp_a, dp_b, turned_s, dg_s, du_s):
    step = pl.program_id(0)
    wide = dg_s.shape[1] // FT
    rows = gc_ref.shape[0] // 2

    @pl.when(step == 0)
    def _():
        for n in range(2):
            hot = jnp.where(slot_onehot(meta_ref, n, rows), 1.0, 0.0).astype(jnp.bfloat16)
            turned_s[n] = jnp.transpose(hot)

    @pl.when(step < wide)
    def _():
        cols = pl.ds(pl.multiple_of(step * FT, FT), FT)
        dh = dot_nt(gc_ref[...], down_ref[0])
        dg = (dh * slope_ref[...].astype(jnp.float32)).astype(jnp.bfloat16)
        du = (dh * act_ref[...].astype(jnp.float32)).astype(jnp.bfloat16)
        dg_s[:, cols] = dg
        du_s[:, cols] = du
        dg_ref[...] = dg
        du_ref[...] = du

    @pl.when(step >= wide)
    def _():
        dx = (dot_nt(dg_s[...], gate_ref[0]) + dot_nt(du_s[...], up_ref[0])).astype(jnp.bfloat16)
        for s in range(2):
            dp_ref = (dp_a, dp_b)[s]
            dp_ref[...] = dot_nn(turned_s[s], dx[s * rows : (s + 1) * rows]).astype(jnp.bfloat16)


def low_shape(*shape):
    return jax.ShapeDtypeStruct(shape, jnp.bfloat16)


def expert_fwd(place, chips, rows, meta, router_rows, toks, cots, w_gate, w_up, w_down, buffers):
    count = toks[0].shape[0]
    width = w_gate.shape[2]
    wide = width // FT
    deep = D // FT
    once = pl.Buffered(1)
    whole = lambda *shape: pl.BlockSpec(shape, lambda j: (0,) * len(shape), pipeline_mode=once)
    mine = pl.BlockSpec((2 * rows, D), lambda j: (place, 0), pipeline_mode=once)
    one = lambda j: jnp.minimum(j, wide - 1)
    two = lambda j: jnp.maximum(j - wide, 0)
    strip = pl.BlockSpec((2 * rows, FT), lambda j: (place, one(j)))
    total = 2 * chips * rows
    buffers = () if buffers is None else tuple(buffers)
    return pl.pallas_call(
        expert_fwd_kernel,
        grid=(wide + deep,),
        in_specs=[whole(2, 8, count), whole(8, D)]
        + [whole(count, D)] * 2
        + [pl.BlockSpec((count, FT), lambda j: (0, two(j)))] * 2
        + [pl.BlockSpec((1, D, FT), lambda j: (0, 0, one(j)))] * 2
        + [pl.BlockSpec((1, width, FT), lambda j: (0, 0, two(j)))]
        + [pl.BlockSpec(memory_space=pl.ANY)] * len(buffers),
        out_specs=[
            mine,
            mine,
            strip,
            strip,
            strip,
            pl.BlockSpec((count, FT), lambda j: (0, two(j))),
            pl.BlockSpec((count, FT), lambda j: (0, two(j))),
            whole(2, 8, count),
        ],
        out_shape=[low_shape(total, D)] * 2
        + [low_shape(total, width)] * 3
        + [low_shape(count, D)] * 2
        + [jax.ShapeDtypeStruct((2, 8, count), jnp.float32)],
        scratch_shapes=[
            pltpu.VMEM((2, rows, count), jnp.bfloat16),
            pltpu.VMEM((2, count, rows), jnp.bfloat16),
            pltpu.VMEM((2 * rows, width), jnp.bfloat16),
            pltpu.VMEM((2 * rows, 128), jnp.float32),
        ],
        input_output_aliases={9 + n: n for n in range(len(buffers))},
        compiler_params=pltpu.CompilerParams(vmem_limit_bytes=VMEM_MOST),
        cost_estimate=LIGHT,
        name=f"expert_fwd_{place}",
    )(meta, router_rows, *toks, *cots, w_gate, w_up, w_down, *buffers)


def expert_bwd(place, rows, meta, gc, slope, act, w_gate, w_up, w_down):
    count = meta.shape[2]
    total, width = slope.shape
    wide = width // FT
    deep = D // FT
    once = pl.Buffered(1)
    one = lambda j: jnp.minimum(j, wide - 1)
    two = lambda j: jnp.maximum(j - wide, 0)
    strip = pl.BlockSpec((2 * rows, FT), lambda j: (place, one(j)))
    return pl.pallas_call(
        expert_bwd_kernel,
        grid=(wide + deep,),
        in_specs=[
            pl.BlockSpec((2, 8, count), lambda j: (0, 0, 0), pipeline_mode=once),
            pl.BlockSpec((2 * rows, D), lambda j: (place, 0), pipeline_mode=once),
            strip,
            strip,
            pl.BlockSpec((1, FT, D), lambda j: (0, one(j), 0)),
            pl.BlockSpec((1, FT, width), lambda j: (0, two(j), 0)),
            pl.BlockSpec((1, FT, width), lambda j: (0, two(j), 0)),
        ],
        out_specs=[strip] * 2 + [pl.BlockSpec((count, FT), lambda j: (0, two(j)))] * 2,
        out_shape=[low_shape(total, width)] * 2 + [low_shape(count, D)] * 2,
        scratch_shapes=[
            pltpu.VMEM((2, count, rows), jnp.bfloat16),
            pltpu.VMEM((2 * rows, width), jnp.bfloat16),
            pltpu.VMEM((2 * rows, width), jnp.bfloat16),
        ],
        input_output_aliases={2: 0, 3: 1},
        compiler_params=pltpu.CompilerParams(vmem_limit_bytes=VMEM_MOST),
        cost_estimate=LIGHT,
        name=f"expert_bwd_{place}",
    )(meta, gc, slope, act, w_down, w_gate, w_up)


def grad_down_kernel(left_ref, right_ref, out_ref, turned_s):
    @pl.when(pl.program_id(0) == 0)
    def _():
        turned_s[...] = jnp.transpose(left_ref[...])

    tile = dot_nn(turned_s[...], right_ref[...])
    out_ref[...] = jnp.transpose(tile).astype(jnp.bfloat16)


def grad_in_kernel(left_ref, gate_ref, up_ref, out_gate_ref, out_up_ref, turned_s):
    @pl.when(pl.program_id(0) == 0)
    def _():
        turned_s[...] = jnp.transpose(left_ref[...])

    out_gate_ref[...] = dot_nn(turned_s[...], gate_ref[...]).astype(jnp.bfloat16)
    out_up_ref[...] = dot_nn(turned_s[...], up_ref[...]).astype(jnp.bfloat16)


def grad_down(gc, hidden):
    total, width = hidden.shape
    return pl.pallas_call(
        grad_down_kernel,
        grid=(width // FT,),
        in_specs=[pl.BlockSpec((total, D), lambda j: (0, 0)), pl.BlockSpec((total, FT), lambda j: (0, j))],
        out_specs=pl.BlockSpec((FT, D), lambda j: (j, 0)),
        out_shape=jax.ShapeDtypeStruct((width, D), jnp.bfloat16),
        scratch_shapes=[pltpu.VMEM((D, total), jnp.bfloat16)],
        compiler_params=pltpu.CompilerParams(vmem_limit_bytes=VMEM_LIMIT),
        cost_estimate=LIGHT,
        name="grad_down",
    )(gc, hidden)


def grad_in(rows, dgate, dup):
    total, width = dgate.shape
    strip = pl.BlockSpec((total, FT), lambda j: (0, j))
    out = pl.BlockSpec((D, FT), lambda j: (0, j))
    return pl.pallas_call(
        grad_in_kernel,
        grid=(width // FT,),
        in_specs=[pl.BlockSpec((total, D), lambda j: (0, 0)), strip, strip],
        out_specs=[out, out],
        out_shape=[jax.ShapeDtypeStruct((D, width), jnp.bfloat16)] * 2,
        scratch_shapes=[pltpu.VMEM((D, total), jnp.bfloat16)],
        compiler_params=pltpu.CompilerParams(vmem_limit_bytes=VMEM_LIMIT),
        cost_estimate=LIGHT,
        name="grad_in",
    )(rows, dgate, dup)


def grad_half_kernel(left_ref, right_ref, out_ref, turned_s):
    @pl.when(pl.program_id(0) == 0)
    def _():
        turned_s[...] = jnp.transpose(left_ref[...])

    out_ref[...] = dot_nn(turned_s[...], right_ref[...]).astype(jnp.bfloat16)


def grad_rows(left, right, name):
    count, width = right.shape
    return pl.pallas_call(
        grad_half_kernel,
        grid=(width // 512,),
        in_specs=[pl.BlockSpec((count, D), lambda j: (0, 0)), pl.BlockSpec((count, 512), lambda j: (0, j))],
        out_specs=pl.BlockSpec((D, 512), lambda j: (0, j)),
        out_shape=jax.ShapeDtypeStruct((D, width), jnp.bfloat16),
        scratch_shapes=[pltpu.VMEM((D, count), jnp.bfloat16)],
        compiler_params=pltpu.CompilerParams(vmem_limit_bytes=VMEM_LIMIT),
        cost_estimate=LIGHT,
        name=name,
    )(left, right)


def grad_normed_kernel(first_ref, second_ref, w_ref, out_ref):
    step = pl.program_id(0)

    @pl.when(step == 0)
    def _():
        out_ref[...] = jnp.zeros_like(out_ref)

    @pl.when(step % 2 == 0)
    def _():
        out_ref[...] += dot_nt(first_ref[...], w_ref[...])

    @pl.when(step % 2 == 1)
    def _():
        out_ref[...] += dot_nt(second_ref[...], w_ref[...])


def grad_normed_of(first, second, w_qkv):
    count = first.shape[0]
    part = pl.BlockSpec((count, D // 2), lambda j: (0, j // 2))
    return pl.pallas_call(
        grad_normed_kernel,
        grid=(6,),
        in_specs=[part, part, pl.BlockSpec((D, D // 2), lambda j: (0, j))],
        out_specs=pl.BlockSpec((count, D), lambda j: (0, 0)),
        out_shape=jax.ShapeDtypeStruct((count, D), jnp.float32),
        compiler_params=pltpu.CompilerParams(vmem_limit_bytes=VMEM_LIMIT),
        cost_estimate=LIGHT,
        name="grad_normed",
    )(first, second, w_qkv)


OUTER = 4


def rms_forward(values, gain):
    scale_rows = lax.rsqrt(jnp.mean(values * values, axis=-1, keepdims=True) + EPSILON)
    return (values * scale_rows * gain, scale_rows)


def rms_backward(values, scale_rows, gain, upstream):
    scaled_grad = upstream * gain
    gain_grad = jnp.sum(upstream * values * scale_rows, axis=0)
    inner_mean = jnp.mean(scaled_grad * values, axis=-1, keepdims=True)
    return (scale_rows * scaled_grad - values * scale_rows**3 * inner_mean, gain_grad)


def tie(*arrays):
    return lax.optimization_barrier(arrays)


def to_sibling(x):
    groups = lax.axis_size("ep")
    return lax.ppermute(x, "ep", [(e, e ^ 1) for e in range(groups)])


def from_chip(x, away, cross=0):
    groups = lax.axis_size("ep")
    return lax.ppermute(x, "ep", [(e, ((e - 2 * away) % groups) ^ cross) for e in range(groups)])


def core_pairs(step):
    return [(e, e ^ 1) for e in range(lax.axis_size("ep"))]


def chip_pairs(step):
    groups = lax.axis_size("ep")
    return [(e, (e + 2 * step) % groups) for e in range(groups)]


def inner_pairs(step):
    replicas = lax.axis_size("rep")
    inner = replicas // OUTER
    return [(r, r - r % inner + (r + step) % inner) for r in range(replicas)]


def outer_pairs(step):
    replicas = lax.axis_size("rep")
    return [(r, (r + step * (replicas // OUTER)) % replicas) for r in range(replicas)]


def levels():
    ep, rep = lax.axis_index("ep"), lax.axis_index("rep")
    inner = lax.axis_size("rep") // OUTER
    return (
        ("ep", 2, ep % 2, core_pairs),
        ("ep", lax.axis_size("ep") // 2, ep // 2, chip_pairs),
        ("rep", inner, rep % inner, inner_pairs),
        ("rep", OUTER, rep // inner, outer_pairs),
    )


def swapped(x, level):
    axis, size, place, pairs = level
    out = [lax.dynamic_index_in_dim(x, place, 0, keepdims=False)]
    for step in range(1, size):
        sent = lax.dynamic_index_in_dim(x, (place + step) % size, 0, keepdims=False)
        out.append(lax.ppermute(sent, axis, pairs(step)))
    return out


def total(arrays):
    return sum([x.astype(jnp.float32) for x in arrays[1:]], arrays[0].astype(jnp.float32))


def low_total(arrays):
    return total(arrays).astype(arrays[0].dtype)


def collected(x, level):
    axis, size, place, pairs = level
    if size == 2:
        other = lax.ppermute(x, axis, pairs(1))
        return jnp.concatenate([jnp.where(place == 0, x, other), jnp.where(place == 0, other, x)])
    out = lax.dynamic_update_index_in_dim(jnp.zeros((size, *x.shape), x.dtype), x, place, 0)
    for step in range(1, size):
        other = lax.ppermute(x, axis, pairs(step))
        out = lax.dynamic_update_index_in_dim(out, other, (place - step) % size, 0)
    return out.reshape(-1, *x.shape[1:])


def rows_swapped(x, level):
    return swapped(x.reshape(level[1], -1, x.shape[1]), level)


def near_swapped(x):
    replicas = lax.axis_size("rep")
    blocks = x.reshape(OUTER, replicas // OUTER, x.shape[0] // replicas, x.shape[1])
    return swapped(jnp.swapaxes(blocks, 0, 1), levels()[2])


def slot_table(expert_ids, priority, experts, capacity):
    ranks = priority.reshape(-1, 2)
    names = jnp.arange(experts, dtype=jnp.int32)[:, None]
    first, second = expert_ids[:, 0][None, :] == names, expert_ids[:, 1][None, :] == names
    rank = jnp.where(first, ranks[:, 0][None, :], jnp.where(second, ranks[:, 1][None, :], 1 << 20))
    slot = jnp.sum((rank[:, :, None] < rank[:, None, :]).astype(jnp.int32), axis=1)
    return jnp.where((first | second) & (slot < capacity), slot, -1)


def per_device(
    tokens,
    cotangent,
    gain_attn,
    w_qkv,
    w_out,
    rel_table,
    gain_moe,
    w_router,
    w_gate,
    w_up,
    w_down,
    expert_ids,
    priority,
    span_starts,
):
    tok_count = tokens.shape[0]
    experts = w_router.shape[1]
    groups = lax.axis_size("ep")
    chips = groups // 2
    capacity = 5 * tok_count // (2 * experts)
    own = lax.axis_index("ep")

    slots = slot_table(expert_ids, priority, experts, capacity)
    ids = jnp.transpose(expert_ids)
    table = jnp.concatenate([slots, ids], axis=0)
    info = [(table, to_sibling(table))] + [(from_chip(table, n), from_chip(table, n, 1)) for n in range(1, chips)]
    cot_sib = to_sibling(cotangent)
    cot_far = [from_chip(cotangent, n) for n in range(1, chips)]
    metas = []
    for pair in info:
        rows = []
        for table in pair:
            slot = lax.dynamic_slice_in_dim(table, own, 1, axis=0)
            one, two = table[experts : experts + 1], table[experts + 1 :]
            other = jnp.where(one == own, two, one)
            rows.append(jnp.concatenate([slot, other, jnp.full((6, tok_count), 1, jnp.int32) * own], axis=0))
        metas.append(jnp.stack(rows))

    diag = wide_diag(rel_table)
    token_float = tokens.astype(jnp.float32)
    normed, scale_attn = rms_forward(token_float, gain_attn)
    normed_low = normed.astype(jnp.bfloat16)
    qkv = jnp.dot(normed_low, w_qkv, preferred_element_type=jnp.float32).astype(jnp.bfloat16)
    attended_low, lse = attn_fwd(span_starts, qkv, diag)
    attended_low, cot_sib, cot_far, metas = tie(attended_low, cot_sib, cot_far, metas)
    mixed = token_float + jnp.dot(attended_low, w_out, preferred_element_type=jnp.float32)
    routed, scale_moe = rms_forward(mixed, gain_moe)
    routed_low = routed.astype(jnp.bfloat16)
    logits = jnp.dot(routed_low, w_router, preferred_element_type=jnp.float32)
    choose = expert_ids[:, :, None] == jnp.arange(experts, dtype=jnp.int32)[None, None, :]
    chosen = jnp.sum(jnp.where(choose, logits[:, None, :], 0.0), axis=-1)
    gates = jax.nn.softmax(chosen, axis=-1)

    router_rows = jnp.zeros((8, D), jnp.bfloat16).at[:experts].set(jnp.transpose(w_router))
    weights = (w_gate, w_up, w_down)
    core, chip, inner, outer = levels()

    tok_far = [from_chip(routed_low, n) for n in range(1, chips)]
    cots = [(cotangent, cot_sib)] + [(far, to_sibling(far)) for far in cot_far]
    pair = (routed_low, to_sibling(routed_low))
    made = expert_fwd(0, chips, capacity, metas[0], router_rows, pair, cots[0], *weights, None)
    made, tok_far, cots = tie(made, tok_far, cots)
    toks = [(far, to_sibling(far)) for far in tok_far]
    outs, dots = [made[5:7]], [(made[7][0], made[7][1])]
    buffers = made[:5]
    for away in range(1, chips):
        made = expert_fwd(
            away, chips, capacity, metas[away], router_rows, toks[away - 1], cots[away], *weights, buffers
        )
        buffers = made[:5]
        outs.append(made[5:7])
        dots.append((made[7][0], made[7][1]))
    rows_in, rows_out, hidden, slope, act = buffers

    met = [[to_sibling(other) for mine, other in part] for part in (dots, outs)]
    down_low = grad_down(rows_out, hidden)
    down_low, slope, met, dots, outs = tie(down_low, slope, met, dots, outs)
    dots, outs = [
        [total([mine[n][0], got[n]]) for n in range(chips)] for mine, got in zip((dots, outs), met)
    ]
    outs_low = [x.astype(jnp.bfloat16) for x in outs[1:]]
    slope, outs_low, down_low = tie(slope, outs_low, down_low)
    far_outs = [from_chip(x, chips - 1 - n) for n, x in enumerate(outs_low)]
    far_dots = [from_chip(x, chips - 1 - n) for n, x in enumerate(dots[1:])]
    down_near = near_swapped(down_low)
    grads = [None] * chips
    for away in reversed(range(1, chips)):
        slope, act, *grads[away] = expert_bwd(away, capacity, metas[away], rows_out, slope, act, *weights)
    slope, far_outs, far_dots = tie(slope, far_outs, far_dots)
    far_grads = []
    for away in range(1, chips):
        far_grads += [from_chip(grads[away][0], chips - away), from_chip(grads[away][1], chips - away, 1)]
    slope, act, *here = expert_bwd(0, capacity, metas[0], rows_out, slope, act, *weights)
    slope, down_near = tie(slope, down_near)
    down_near = low_total(down_near)
    slope, down_near = tie(slope, down_near)
    near_grads = to_sibling(here[1])
    down_far = swapped(down_near, outer)
    gate_low, up_low = grad_in(rows_in, slope, act)
    gate_low, up_low, far_grads, near_grads = tie(gate_low, up_low, far_grads, near_grads)
    grad_pairs = total([here[0], near_grads] + far_grads)
    grad_gates_all = total([dots[0]] + far_dots)
    block_out = (mixed + total([outs[0]] + far_outs)).astype(jnp.bfloat16)
    gate_near = near_swapped(gate_low)

    grad_out = cotangent.astype(jnp.float32)
    by_token = jnp.transpose(grad_gates_all[:experts])
    grad_gates = jnp.sum(jnp.where(choose, by_token[:, None, :], 0.0), axis=-1)
    grad_chosen = gates * (grad_gates - jnp.sum(gates * grad_gates, axis=-1, keepdims=True))
    grad_logits = jnp.sum(jnp.where(choose, grad_chosen[:, :, None], 0.0), axis=1).astype(jnp.bfloat16)
    grad_w_router = jnp.einsum("td,te->de", routed_low, grad_logits, preferred_element_type=jnp.float32)
    grad_routed = grad_pairs + jnp.einsum(
        "te,de->td", grad_logits, w_router, preferred_element_type=jnp.float32
    )
    grad_norm_moe, grad_gain_moe = rms_backward(mixed, scale_moe, gain_moe, grad_routed)
    grad_mixed = grad_out + grad_norm_moe
    grad_branch = grad_mixed.astype(jnp.bfloat16)
    grad_attended = jnp.einsum(
        "te,de->td", grad_branch, w_out, preferred_element_type=jnp.float32
    ).astype(jnp.bfloat16)

    grad_attended, grad_branch, block_out = tie(grad_attended, grad_branch, block_out)
    first = attn_bwd(span_starts, qkv, grad_attended, attended_low, lse, diag, 0)
    half_first = grad_rows(normed_low, first[0], "grad_qkv_0")
    grad_w_out = grad_rows(attended_low, grad_branch, "grad_out")
    half_first, grad_w_out, grad_attended, gate_near, down_far = tie(
        half_first, grad_w_out, grad_attended, gate_near, down_far
    )
    gate_near = low_total(gate_near)
    sum_down = total(down_far)
    gate_near, grad_attended, sum_down = tie(gate_near, grad_attended, sum_down)
    gate_far = swapped(gate_near, outer)
    up_near = near_swapped(up_low)
    early = [rows_swapped(x, core) for x in (half_first, grad_w_out)]
    second = attn_bwd(span_starts, qkv, grad_attended, attended_low, lse, diag, 1)
    second, early = tie(second, early)
    early = tie(*[low_total(x) for x in early])
    early = [rows_swapped(x, chip) for x in early]
    half_second = grad_rows(normed_low, second[0], "grad_qkv_1")
    grad_normed = grad_normed_of(first[0], second[0], w_qkv)
    half_second, grad_normed, early, gate_far, up_near = tie(half_second, grad_normed, early, gate_far, up_near)
    up_near = low_total(up_near)
    early = [low_total(x) for x in early]
    grad_norm_attn, grad_gain_attn = rms_backward(token_float, scale_attn, gain_attn, grad_normed)
    grad_tokens = grad_mixed + grad_norm_attn
    grad_rel_table = rel_grad(jnp.concatenate([first[1], second[1]]), jnp.concatenate([first[2], second[2]]))
    small = jnp.concatenate(
        [
            jnp.transpose(grad_w_router),
            jnp.pad(grad_rel_table.reshape(1, -1), ((0, 0), (0, D - BUCKETS * H))),
            grad_gain_attn[None],
            grad_gain_moe[None],
        ]
    )
    small = jnp.pad(jnp.transpose(small), ((0, 0), (0, 128 - small.shape[0])))
    up_near, half_second, small, early, grad_tokens = tie(up_near, half_second, small, early, grad_tokens)
    up_far = swapped(up_near, outer)
    late = tie(*[rows_swapped(x, core) for x in (half_second, small)])
    late = [low_total(x) for x in late]
    late = tie(*[rows_swapped(x, inner) for x in late])
    late, early = tie([low_total(x) for x in late], early)
    late, early = tie([rows_swapped(x, chip) for x in late], [rows_swapped(x, inner) for x in early])
    both = tie(*[low_total(x) for x in (*early, *late)])
    both, up_far = tie([rows_swapped(x, outer) for x in both], up_far)
    both = tie(*[low_total(x) for x in both])
    both = tie(*[collected(x, outer) for x in both])
    both = tie(*[collected(x, level) for x, level in zip(both, (inner, inner, chip, chip))])
    both = tie(*[collected(x, level) for x, level in zip(both, (chip, chip, inner, inner))])
    both = tie(*[collected(x, core) for x in both])
    sum_first, sum_w_out, sum_second, small = [x.astype(jnp.float32) for x in both]
    sum_gate, sum_up = total(gate_far), total(up_far)
    sum_w_qkv = jnp.concatenate(
        [x[:, n * D // 2 : (n + 1) * D // 2] for n in range(3) for x in (sum_first, sum_second)], axis=1
    )
    small = jnp.transpose(small)
    small = (
        small[experts, : BUCKETS * H].reshape(BUCKETS, H),
        jnp.transpose(small[:experts]),
        small[experts + 1],
        small[experts + 2],
    )
    return (
        block_out,
        grad_tokens,
        small[2],
        sum_w_qkv,
        sum_w_out,
        small[0],
        small[3],
        small[1],
        sum_gate[None],
        sum_up[None],
        sum_down[None],
    )


def solution(mesh):
    placed = (
        P(("rep", "ep"), None),
        P(("rep", "ep"), None),
        P(),
        P(),
        P(),
        P(),
        P(),
        P(),
        P("ep", None, None),
        P("ep", None, None),
        P("ep", None, None),
        P(("rep", "ep"), None),
        P(("rep", "ep"), None),
        P(("rep", "ep"), None),
    )
    return jax.shard_map(
        per_device,
        mesh=mesh,
        in_specs=placed,
        out_specs=(
            P(("rep", "ep"), None),
            P(("rep", "ep"), None),
            P(),
            P(),
            P(),
            P(),
            P(),
            P(),
            P("ep", "rep", None),
            P("ep", "rep", None),
            P("ep", "rep", None),
        ),
        check_vma=False,
    )
```

```python
from functools import partial
import jax
import jax.numpy as jnp
import numpy as np
from jax import lax
from jax.sharding import PartitionSpec as P
from jax.experimental import pallas as pl
from jax.experimental.pallas import tpu as pltpu

D = 1024
H = 16
HD = 64
BUCKETS = 32
MAXDIST = 128
SEQ = 1024
PIC = 256
EPSILON = 1e-06
NEGATIVE = -1e30
LOG2E = 1.4426950408889634
QB = 256
KB = 128
WIDE = 768
VMEM_LIMIT = 56 * 1024 * 1024
LIGHT = pl.CostEstimate(flops=1000, bytes_accessed=1000, transcendentals=0)


def bucket_of(offsets):
    half_count = BUCKETS // 2
    near_count = half_count // 2
    upper_part = (offsets > 0).astype(np.int64) * half_count
    distance = np.abs(offsets)
    ratio = np.log(np.maximum(distance, 1) / near_count) / np.log(MAXDIST / near_count)
    distant_bucket = np.minimum(
        near_count + np.floor(ratio * (half_count - near_count)).astype(np.int64), half_count - 1
    )
    return upper_part + np.where(distance < near_count, distance, distant_bucket)


def wide_onehot():
    places = np.arange(WIDE)
    offsets = np.where(places < 640, 256 - places, 1024 - places)
    return (bucket_of(offsets)[:, None] == np.arange(BUCKETS)[None, :]).astype(np.float32)


def dot_nt(a, b):
    return lax.dot_general(a, b, (((1,), (1,)), ((), ())), preferred_element_type=jnp.float32)


def dot_nn(a, b):
    return lax.dot_general(a, b, (((1,), (0,)), ((), ())), preferred_element_type=jnp.float32)


def key_count(i):
    return min((i + 2) * QB, SEQ)


def fill_mask(span_ref, mask_s):
    for i in range(SEQ // QB):
        for d in range(4):
            if 2 * i + d >= SEQ // KB:
                continue
            k = (2 * i + d) * KB + lax.broadcasted_iota(jnp.int32, (KB, QB), 0)
            q = i * QB + lax.broadcasted_iota(jnp.int32, (KB, QB), 1)
            ok = k <= q
            for s in range(2):
                start = span_ref[0, s]
                ok = ok | ((k >= start) & (k < start + PIC) & (q >= start) & (q < start + PIC))
            mask_s[4 * i + d] = jnp.where(ok, 0.0, NEGATIVE)


def spread_bias(diag_ref, h, bias_s):
    row = jnp.broadcast_to(diag_ref[0, h : h + 1, :], (KB, WIDE))
    bias_s[h] = pltpu.roll(row, 0, 1, stride=1, stride_axis=0)


def shifted(s, i, kt, h, bias_s, mask_s, low, high, row):
    d = kt - 2 * i
    if d <= -2:
        return s + (low if row is None else low + row)
    if d >= 3:
        s = s + (high if row is None else high + row)
    else:
        s = s + bias_s[h, :, (2 - d) * 128 : (2 - d) * 128 + 256]
        if row is not None:
            s = s + row
    if d >= 0:
        s = s + mask_s[4 * i + d]
    return s


def diagonal_sums(x):
    rows = x.shape[0]
    while rows > 8:
        rows //= 2
        x = x[:rows] + pltpu.roll(x[rows:], WIDE - rows, 1)
    total = x[0:1]
    for r in range(1, rows):
        total = total + pltpu.roll(x[r : r + 1], WIDE - r, 1)
    return total


def half_lanes(x, h):
    lane = lax.broadcasted_iota(jnp.int32, x.shape, 1)
    return jnp.where((lane < HD) if h == 0 else (lane >= HD), x, jnp.zeros_like(x))


def attn_fwd_kernel(span_ref, q_ref, k_ref, v_ref, diag_ref, out_ref, lse_ref, mask_s, bias_s, vt_s, s_s, p_s):
    @pl.when(pl.program_id(0) == 0)
    def _():
        fill_mask(span_ref, mask_s)

    vt = jnp.transpose(v_ref[...])
    for h in range(2):
        spread_bias(diag_ref, h, bias_s)
        vt_s[h, :HD] = vt[h * HD : (h + 1) * HD]
        vt_s[h, HD:] = jnp.ones((16, SEQ), jnp.bfloat16)
    scale = LOG2E * HD ** (-0.5)
    for i in range(SEQ // QB):
        nk = key_count(i)
        outs = []
        for h in range(2):
            low = diag_ref[0, h : h + 1, 600:601]
            high = diag_ref[0, h : h + 1, 0:1]
            qs = half_lanes(q_ref[i * QB : (i + 1) * QB, :], h)
            s_s[h, :nk] = dot_nt(k_ref[:nk, :], qs)
            top = None
            for kt in range(nk // KB):
                s = shifted(s_s[h, kt * KB : (kt + 1) * KB] * scale, i, kt, h, bias_s, mask_s, low, high, None)
                s_s[h, kt * KB : (kt + 1) * KB] = s
                t = jnp.max(s.reshape(KB // 8, 8, QB), axis=0)
                top = t if top is None else jnp.maximum(top, t)
            m = jnp.max(top, axis=0, keepdims=True)
            for kt in range(nk // KB):
                p_s[h, kt * KB : (kt + 1) * KB] = jnp.exp2(s_s[h, kt * KB : (kt + 1) * KB] - m).astype(jnp.bfloat16)
            ot = dot_nn(vt_s[h, :, :nk], p_s[h, :nk])
            total = ot[HD : HD + 1]
            outs.append(ot[:HD] / total)
            lse_ref[0, h : h + 1, i * QB : (i + 1) * QB] = m + jnp.log2(total)
        out_ref[i * QB : (i + 1) * QB, :] = jnp.transpose(jnp.concatenate(outs, axis=0)).astype(jnp.bfloat16)


def attn_fwd(spans, qkv, diag):
    col = lambda off: pl.BlockSpec((SEQ, 128), lambda g: (0, g + off))
    return pl.pallas_call(
        attn_fwd_kernel,
        grid=(H // 2,),
        in_specs=[
            pl.BlockSpec(memory_space=pltpu.SMEM),
            col(0),
            col(8),
            col(16),
            pl.BlockSpec((1, 2, WIDE), lambda g: (g, 0, 0)),
        ],
        out_specs=[col(0), pl.BlockSpec((1, 2, SEQ), lambda g: (g, 0, 0))],
        out_shape=[
            jax.ShapeDtypeStruct((SEQ, D), jnp.bfloat16),
            jax.ShapeDtypeStruct((H // 2, 2, SEQ), jnp.float32),
        ],
        scratch_shapes=[
            pltpu.VMEM((16, KB, QB), jnp.float32),
            pltpu.VMEM((2, KB, WIDE), jnp.float32),
            pltpu.VMEM((2, HD + 16, SEQ), jnp.bfloat16),
            pltpu.VMEM((2, SEQ, QB), jnp.float32),
            pltpu.VMEM((2, SEQ, QB), jnp.bfloat16),
        ],
        compiler_params=pltpu.CompilerParams(vmem_limit_bytes=VMEM_LIMIT),
        cost_estimate=LIGHT,
        name="attn_fwd",
    )(spans, qkv, qkv, qkv, diag)


def attn_bwd_kernel(
    span_ref, q_ref, k_ref, v_ref, g_ref, o_ref, lse_ref, diag_ref,
    out_ref, drel_ref, far_ref,
    mask_s, bias_s, acc_s, kt_s, s_s, dp_s, p_s, ds_s, dk_s, dv_s, delta_s,
):
    part = pl.program_id(1)

    @pl.when((pl.program_id(0) == 0) & (part == 0))
    def _():
        fill_mask(span_ref, mask_s)

    @pl.when(part == 1)
    def _():
        out_ref[...] = (dk_s[...] * HD ** (-0.5)).astype(jnp.bfloat16)

    @pl.when(part == 2)
    def _():
        out_ref[...] = dv_s[...].astype(jnp.bfloat16)

    @pl.when(part == 0)
    def _():
        kt_s[...] = jnp.transpose(k_ref[...])
        prod = jnp.transpose(g_ref[...].astype(jnp.float32) * o_ref[...].astype(jnp.float32))
        for h in range(2):
            spread_bias(diag_ref, h, bias_s)
            delta_s[h : h + 1] = jnp.sum(prod[h * HD : (h + 1) * HD], axis=0, keepdims=True)
        acc_s[...] = jnp.zeros_like(acc_s)
        far_ref[...] = jnp.zeros_like(far_ref)
        scale = LOG2E * HD ** (-0.5)
        for i in reversed(range(SEQ // QB)):
            nk = key_count(i)
            rows = slice(i * QB, (i + 1) * QB)
            dqs = []
            for h in range(2):
                low = diag_ref[0, h : h + 1, 600:601]
                high = diag_ref[0, h : h + 1, 0:1]
                qs = half_lanes(q_ref[rows, :], h)
                gs = half_lanes(g_ref[rows, :], h)
                s_s[h, :nk] = dot_nt(k_ref[:nk, :], qs)
                dp_s[h, :nk] = dot_nt(v_ref[:nk, :], gs)
                nlse = -lse_ref[0, h : h + 1, rows]
                delta = delta_s[h : h + 1, rows]
                for kt in range(nk // KB):
                    tile = slice(kt * KB, (kt + 1) * KB)
                    d = kt - 2 * i
                    p = jnp.exp2(shifted(s_s[h, tile] * scale, i, kt, h, bias_s, mask_s, low, high, nlse))
                    ds = p * (dp_s[h, tile] - delta)
                    p_s[tile, h * QB : (h + 1) * QB] = p.astype(jnp.bfloat16)
                    ds_s[tile, h * QB : (h + 1) * QB] = ds.astype(jnp.bfloat16)
                    if -1 <= d <= 2:
                        cols = slice((2 - d) * 128, (2 - d) * 128 + 256)
                        acc_s[h, :, cols] += ds
                    else:
                        far_ref[0, h, 0 if d < 0 else 1] += jnp.sum(ds.reshape(KB // 8, 8, QB), axis=0)
                dqs.append(dot_nn(kt_s[h * HD : (h + 1) * HD, :nk], ds_s[:nk, h * QB : (h + 1) * QB]))
            out_ref[rows, :] = (jnp.transpose(jnp.concatenate(dqs, axis=0)) * HD ** (-0.5)).astype(jnp.bfloat16)
            gg = jnp.concatenate([half_lanes(g_ref[rows, :], h) for h in range(2)], axis=0)
            qq = jnp.concatenate([half_lanes(q_ref[rows, :], h) for h in range(2)], axis=0)
            dv = dot_nn(p_s[:nk, :], gg)
            dk = dot_nn(ds_s[:nk, :], qq)
            if i == SEQ // QB - 1:
                dv_s[...] = dv
                dk_s[...] = dk
            else:
                dv_s[:nk] += dv
                dk_s[:nk] += dk
        for h in range(2):
            drel_ref[0, h : h + 1, :] = diagonal_sums(acc_s[h])


def attn_bwd(spans, qkv, grad_att, att, lse, diag, half):
    pairs = H // 4
    base = half * pairs
    col = lambda off: pl.BlockSpec((SEQ, 128), lambda g, p: (0, base + g + off))
    one = lambda *dims: pl.BlockSpec((1, *dims), lambda g, p: (base + g,) + (0,) * len(dims))
    new = lambda *dims: pl.BlockSpec((1, *dims), lambda g, p: (g,) + (0,) * len(dims))
    return pl.pallas_call(
        attn_bwd_kernel,
        grid=(pairs, 3),
        in_specs=[
            pl.BlockSpec(memory_space=pltpu.SMEM),
            col(0),
            col(8),
            col(16),
            col(0),
            col(0),
            one(2, SEQ),
            one(2, WIDE),
        ],
        out_specs=[
            pl.BlockSpec((SEQ, 128), lambda g, p: (0, p * pairs + g)),
            new(2, WIDE),
            new(2, 2, 8, QB),
        ],
        out_shape=[
            jax.ShapeDtypeStruct((SEQ, 3 * D // 2), jnp.bfloat16),
            jax.ShapeDtypeStruct((pairs, 2, WIDE), jnp.float32),
            jax.ShapeDtypeStruct((pairs, 2, 2, 8, QB), jnp.float32),
        ],
        scratch_shapes=[
            pltpu.VMEM((16, KB, QB), jnp.float32),
            pltpu.VMEM((2, KB, WIDE), jnp.float32),
            pltpu.VMEM((2, KB, WIDE), jnp.float32),
            pltpu.VMEM((128, SEQ), jnp.bfloat16),
            pltpu.VMEM((2, SEQ, QB), jnp.float32),
            pltpu.VMEM((2, SEQ, QB), jnp.float32),
            pltpu.VMEM((SEQ, 2 * QB), jnp.bfloat16),
            pltpu.VMEM((SEQ, 2 * QB), jnp.bfloat16),
            pltpu.VMEM((SEQ, 128), jnp.float32),
            pltpu.VMEM((SEQ, 128), jnp.float32),
            pltpu.VMEM((2, SEQ), jnp.float32),
        ],
        compiler_params=pltpu.CompilerParams(vmem_limit_bytes=VMEM_LIMIT),
        cost_estimate=LIGHT,
        name=f"attn_bwd_{half}",
    )(spans, qkv, qkv, qkv, grad_att, att, lse, diag)


def wide_diag(rel_table):
    return jnp.einsum(
        "mb,bh->hm", jnp.asarray(wide_onehot()), rel_table * LOG2E, precision=lax.Precision.HIGHEST
    ).reshape(H // 2, 2, WIDE)


def rel_grad(drel, far):
    sums = drel.reshape(H, WIDE)
    far = jnp.sum(far.reshape(H, 2, 8 * QB), axis=-1)
    sums = sums.at[:, 600].add(far[:, 0]).at[:, 0].add(far[:, 1])
    return jnp.einsum("mb,hm->bh", jnp.asarray(wide_onehot()), sums, precision=lax.Precision.HIGHEST)


FT = 256


def dot_tn(a, b):
    return lax.dot_general(a, b, (((0,), (0,)), ((), ())), preferred_element_type=jnp.float32)


VMEM_MOST = 58 * 1024 * 1024
PARTS = 2


def slot_onehot(meta_ref, n, rows):
    slot = meta_ref[n, 0:1]
    return lax.broadcasted_iota(jnp.int32, (rows, slot.shape[1]), 0) == slot


def expert_fwd_kernel(meta_ref, wr_ref, tok_a, tok_b, cot_a, cot_b, gate_ref, up_ref, down_ref, *rest):
    x_ref, gc_ref, hid_ref, slope_ref, act_ref, p_a, p_b, gg_ref, hot_s, turned_s, hid_s, gate_s = rest[-12:]
    step = pl.program_id(0)
    wide = hid_s.shape[1] // FT
    deep = D // FT
    rows = x_ref.shape[0] // 2
    count = tok_a.shape[0]
    pair = [(0, tok_a, cot_a, slice(0, rows)), (1, tok_b, cot_b, slice(rows, 2 * rows))]
    chunk = 2 * rows // PARTS

    @pl.when(step == 0)
    def _():
        for n, tok_ref, cot_ref, here in pair:
            logits = dot_nt(wr_ref[...], tok_ref[...])
            other, own = meta_ref[n, 1:2], meta_ref[n, 2:3]
            names = lax.broadcasted_iota(jnp.int32, logits.shape, 0)
            mine = jnp.sum(jnp.where(names == own, logits, 0.0), axis=0, keepdims=True)
            theirs = jnp.sum(jnp.where(names == other, logits, 0.0), axis=0, keepdims=True)
            gate = 1.0 / (1.0 + jnp.exp(theirs - mine))
            hot = slot_onehot(meta_ref, n, rows)
            gates = jnp.sum(jnp.where(hot, gate, 0.0), axis=1, keepdims=True)
            lane = lax.broadcasted_iota(jnp.int32, (rows, 128), 1)
            gate_s[here] = jnp.where(lane < 64, gates, 0.0)
            hot = jnp.where(hot, 1.0, 0.0).astype(jnp.bfloat16)
            hot_s[n] = hot
            turned_s[n] = jnp.transpose(hot)
            x_ref[here] = dot_nn(hot_s[n], tok_ref[...]).astype(jnp.bfloat16)

    @pl.when(step < wide)
    def _():
        cols = pl.ds(pl.multiple_of(step * FT, FT), FT)
        root = (2.0 / np.pi) ** 0.5
        for c in range(PARTS):
            here = slice(c * chunk, (c + 1) * chunk)
            g = dot_nn(x_ref[here], gate_ref[0])
            u = dot_nn(x_ref[here], up_ref[0])
            square = g * g
            t = jnp.tanh(g * (root + (root * 0.044715) * square))
            half = 0.5 + 0.5 * t
            act = g * half
            slope = half + (act * (1.0 - t)) * (root + (3.0 * root * 0.044715) * square)
            slope_ref[here] = (u * slope).astype(jnp.bfloat16)
            act_ref[here] = act.astype(jnp.bfloat16)
            hidden = (act * u).astype(jnp.bfloat16)
            hid_s[here, cols] = hidden
            hid_ref[here] = hidden

    for n in range(deep):

        @pl.when(step == wide + n)
        def _():
            cols = slice(n * FT, (n + 1) * FT)
            outs = dot_nn(hid_s[...], down_ref[0])
            for s, tok_ref, cot_ref, here in pair:
                gates = gate_s[here, 0:1]
                out = outs[here].astype(jnp.bfloat16).astype(jnp.float32)
                cot = dot_nn(hot_s[s], cot_ref[...])
                lane = lax.broadcasted_iota(jnp.int32, (rows, 128), 1)
                gate_s[here] += jnp.where(lane < 64, 0.0, jnp.sum(out * cot, axis=1, keepdims=True))
                gc_ref[here, cols] = (gates * cot).astype(jnp.bfloat16)
                p_ref = (p_a, p_b)[s]
                p_ref[...] = dot_nn(turned_s[s], (gates * out).astype(jnp.bfloat16)).astype(jnp.bfloat16)

    @pl.when(step == wide + deep - 1)
    def _():
        for s, tok_ref, cot_ref, here in pair:
            gg = jnp.where(slot_onehot(meta_ref, s, rows), gate_s[here, 64:65], 0.0)
            gg = jnp.sum(gg, axis=0, keepdims=True)
            own = meta_ref[s, 2:3]
            gg_ref[s] = jnp.where(lax.broadcasted_iota(jnp.int32, (8, count), 0) == own, gg, 0.0)


def expert_bwd_kernel(meta_ref, gc_ref, slope_ref, act_ref, down_ref, gate_ref, up_ref, dg_ref, du_ref, dp_a, dp_b, turned_s, dg_s, du_s):
    step = pl.program_id(0)
    wide = dg_s.shape[1] // FT
    rows = gc_ref.shape[0] // 2

    @pl.when(step == 0)
    def _():
        for n in range(2):
            hot = jnp.where(slot_onehot(meta_ref, n, rows), 1.0, 0.0).astype(jnp.bfloat16)
            turned_s[n] = jnp.transpose(hot)

    @pl.when(step < wide)
    def _():
        cols = pl.ds(pl.multiple_of(step * FT, FT), FT)
        dh = dot_nt(gc_ref[...], down_ref[0])
        dg = (dh * slope_ref[...].astype(jnp.float32)).astype(jnp.bfloat16)
        du = (dh * act_ref[...].astype(jnp.float32)).astype(jnp.bfloat16)
        dg_s[:, cols] = dg
        du_s[:, cols] = du
        dg_ref[...] = dg
        du_ref[...] = du

    @pl.when(step >= wide)
    def _():
        dx = (dot_nt(dg_s[...], gate_ref[0]) + dot_nt(du_s[...], up_ref[0])).astype(jnp.bfloat16)
        for s in range(2):
            dp_ref = (dp_a, dp_b)[s]
            dp_ref[...] = dot_nn(turned_s[s], dx[s * rows : (s + 1) * rows]).astype(jnp.bfloat16)


def low_shape(*shape):
    return jax.ShapeDtypeStruct(shape, jnp.bfloat16)


def expert_fwd(place, rows, meta, router_rows, toks, cots, w_gate, w_up, w_down):
    count = toks[0].shape[0]
    width = w_gate.shape[2]
    wide = width // FT
    deep = D // FT
    once = pl.Buffered(1)
    whole = lambda *shape: pl.BlockSpec(shape, lambda j: (0,) * len(shape), pipeline_mode=once)
    mine = whole(2 * rows, D)
    one = lambda j: jnp.minimum(j, wide - 1)
    two = lambda j: jnp.maximum(j - wide, 0)
    strip = pl.BlockSpec((2 * rows, FT), lambda j: (0, one(j)))
    total = 2 * rows
    return pl.pallas_call(
        expert_fwd_kernel,
        grid=(wide + deep,),
        in_specs=[whole(2, 8, count), whole(8, D)]
        + [whole(count, D)] * 2
        + [pl.BlockSpec((count, FT), lambda j: (0, two(j)))] * 2
        + [pl.BlockSpec((1, D, FT), lambda j: (0, 0, one(j)))] * 2
        + [pl.BlockSpec((1, width, FT), lambda j: (0, 0, two(j)))],
        out_specs=[
            mine,
            mine,
            strip,
            strip,
            strip,
            pl.BlockSpec((count, FT), lambda j: (0, two(j))),
            pl.BlockSpec((count, FT), lambda j: (0, two(j))),
            whole(2, 8, count),
        ],
        out_shape=[low_shape(total, D)] * 2
        + [low_shape(total, width)] * 3
        + [low_shape(count, D)] * 2
        + [jax.ShapeDtypeStruct((2, 8, count), jnp.float32)],
        scratch_shapes=[
            pltpu.VMEM((2, rows, count), jnp.bfloat16),
            pltpu.VMEM((2, count, rows), jnp.bfloat16),
            pltpu.VMEM((2 * rows, width), jnp.bfloat16),
            pltpu.VMEM((2 * rows, 128), jnp.float32),
        ],
        compiler_params=pltpu.CompilerParams(vmem_limit_bytes=VMEM_MOST),
        cost_estimate=LIGHT,
        name=f"expert_fwd_{place}",
    )(meta, router_rows, *toks, *cots, w_gate, w_up, w_down)


def expert_bwd(place, rows, meta, gc, slope, act, w_gate, w_up, w_down):
    count = meta.shape[2]
    total, width = slope.shape
    wide = width // FT
    deep = D // FT
    once = pl.Buffered(1)
    one = lambda j: jnp.minimum(j, wide - 1)
    two = lambda j: jnp.maximum(j - wide, 0)
    strip = pl.BlockSpec((2 * rows, FT), lambda j: (0, one(j)))
    return pl.pallas_call(
        expert_bwd_kernel,
        grid=(wide + deep,),
        in_specs=[
            pl.BlockSpec((2, 8, count), lambda j: (0, 0, 0), pipeline_mode=once),
            pl.BlockSpec((2 * rows, D), lambda j: (0, 0), pipeline_mode=once),
            strip,
            strip,
            pl.BlockSpec((1, FT, D), lambda j: (0, one(j), 0)),
            pl.BlockSpec((1, FT, width), lambda j: (0, two(j), 0)),
            pl.BlockSpec((1, FT, width), lambda j: (0, two(j), 0)),
        ],
        out_specs=[strip] * 2 + [pl.BlockSpec((count, FT), lambda j: (0, two(j)))] * 2,
        out_shape=[low_shape(total, width)] * 2 + [low_shape(count, D)] * 2,
        scratch_shapes=[
            pltpu.VMEM((2, count, rows), jnp.bfloat16),
            pltpu.VMEM((2 * rows, width), jnp.bfloat16),
            pltpu.VMEM((2 * rows, width), jnp.bfloat16),
        ],
        compiler_params=pltpu.CompilerParams(vmem_limit_bytes=VMEM_MOST),
        cost_estimate=LIGHT,
        name=f"expert_bwd_{place}",
    )(meta, gc, slope, act, w_down, w_gate, w_up)


def turn_into(turned_s, refs):
    first = 0
    for ref in refs:
        turned_s[:, first : first + ref.shape[0]] = jnp.transpose(ref[...])
        first += ref.shape[0]


def row_sums(turned_s, refs):
    first, out = 0, None
    for ref in refs:
        part = dot_nn(turned_s[:, first : first + ref.shape[0]], ref[...])
        out = part if out is None else out + part
        first += ref.shape[0]
    return out


def grad_down_kernel(*refs):
    out_ref, turned_s = refs[-2:]
    many = (len(refs) - 2) // 2

    @pl.when(pl.program_id(0) == 0)
    def _():
        turn_into(turned_s, refs[:many])

    out_ref[...] = jnp.transpose(row_sums(turned_s, refs[many : 2 * many])).astype(jnp.bfloat16)


def grad_in_kernel(*refs):
    out_gate_ref, out_up_ref, turned_s = refs[-3:]
    many = (len(refs) - 3) // 3

    @pl.when(pl.program_id(0) == 0)
    def _():
        turn_into(turned_s, refs[:many])

    out_gate_ref[...] = row_sums(turned_s, refs[many : 2 * many]).astype(jnp.bfloat16)
    out_up_ref[...] = row_sums(turned_s, refs[2 * many : 3 * many]).astype(jnp.bfloat16)


def grad_down(gc, hidden):
    rows, width = hidden[0].shape
    once = pl.Buffered(1)
    return pl.pallas_call(
        grad_down_kernel,
        grid=(width // FT,),
        in_specs=[pl.BlockSpec((rows, D), lambda j: (0, 0), pipeline_mode=once)] * len(gc)
        + [pl.BlockSpec((rows, FT), lambda j: (0, j))] * len(gc),
        out_specs=pl.BlockSpec((FT, D), lambda j: (j, 0)),
        out_shape=low_shape(width, D),
        scratch_shapes=[pltpu.VMEM((D, rows * len(gc)), jnp.bfloat16)],
        compiler_params=pltpu.CompilerParams(vmem_limit_bytes=VMEM_LIMIT),
        cost_estimate=LIGHT,
        name="grad_down",
    )(*gc, *hidden)


def grad_in(xs, dgate, dup):
    rows, width = dgate[0].shape
    once = pl.Buffered(1)
    out = pl.BlockSpec((D, FT), lambda j: (0, j))
    return pl.pallas_call(
        grad_in_kernel,
        grid=(width // FT,),
        in_specs=[pl.BlockSpec((rows, D), lambda j: (0, 0), pipeline_mode=once)] * len(xs)
        + [pl.BlockSpec((rows, FT), lambda j: (0, j))] * (2 * len(xs)),
        out_specs=[out, out],
        out_shape=[low_shape(D, width)] * 2,
        scratch_shapes=[pltpu.VMEM((D, rows * len(xs)), jnp.bfloat16)],
        compiler_params=pltpu.CompilerParams(vmem_limit_bytes=VMEM_LIMIT),
        cost_estimate=LIGHT,
        name="grad_in",
    )(*xs, *dgate, *dup)


def grad_half_kernel(left_ref, right_ref, *rest):
    out_ref, turned_s = rest[-2:]

    @pl.when(pl.program_id(0) == 0)
    def _():
        turned_s[...] = jnp.transpose(left_ref[...])

    out_ref[...] = dot_nn(turned_s[...], right_ref[...]).astype(jnp.bfloat16)


def grad_rows(left, right, name, wide=None, first=0, buffer=None):
    count, width = right.shape
    buffers = () if buffer is None else (buffer,)
    return pl.pallas_call(
        grad_half_kernel,
        grid=(width // 512,),
        in_specs=[pl.BlockSpec((count, D), lambda j: (0, 0)), pl.BlockSpec((count, 512), lambda j: (0, j))]
        + [pl.BlockSpec(memory_space=pl.ANY)] * len(buffers),
        out_specs=pl.BlockSpec((D, 512), lambda j: (0, first // 512 + j)),
        out_shape=jax.ShapeDtypeStruct((D, wide or width), jnp.bfloat16),
        scratch_shapes=[pltpu.VMEM((D, count), jnp.bfloat16)],
        input_output_aliases={2: 0} if buffers else {},
        compiler_params=pltpu.CompilerParams(vmem_limit_bytes=VMEM_LIMIT),
        cost_estimate=LIGHT,
        name=name,
    )(left, right, *buffers)


def grad_normed_kernel(first_ref, second_ref, w_ref, out_ref):
    step = pl.program_id(0)

    @pl.when(step == 0)
    def _():
        out_ref[...] = jnp.zeros_like(out_ref)

    @pl.when(step % 2 == 0)
    def _():
        out_ref[...] += dot_nt(first_ref[...], w_ref[...])

    @pl.when(step % 2 == 1)
    def _():
        out_ref[...] += dot_nt(second_ref[...], w_ref[...])


def grad_normed_of(first, second, w_qkv):
    count = first.shape[0]
    part = pl.BlockSpec((count, D // 2), lambda j: (0, j // 2))
    return pl.pallas_call(
        grad_normed_kernel,
        grid=(6,),
        in_specs=[part, part, pl.BlockSpec((D, D // 2), lambda j: (0, j))],
        out_specs=pl.BlockSpec((count, D), lambda j: (0, 0)),
        out_shape=jax.ShapeDtypeStruct((count, D), jnp.float32),
        compiler_params=pltpu.CompilerParams(vmem_limit_bytes=VMEM_LIMIT),
        cost_estimate=LIGHT,
        name="grad_normed",
    )(first, second, w_qkv)


OUTER = 4


def rms_forward(values, gain):
    scale_rows = lax.rsqrt(jnp.mean(values * values, axis=-1, keepdims=True) + EPSILON)
    return (values * scale_rows * gain, scale_rows)


def rms_backward(values, scale_rows, gain, upstream):
    scaled_grad = upstream * gain
    gain_grad = jnp.sum(upstream * values * scale_rows, axis=0)
    inner_mean = jnp.mean(scaled_grad * values, axis=-1, keepdims=True)
    return (scale_rows * scaled_grad - values * scale_rows**3 * inner_mean, gain_grad)


def tie(*arrays):
    return lax.optimization_barrier(arrays)


def to_sibling(x):
    groups = lax.axis_size("ep")
    return lax.ppermute(x, "ep", [(e, e ^ 1) for e in range(groups)])


def from_chip(x, away, cross=0):
    groups = lax.axis_size("ep")
    return lax.ppermute(x, "ep", [(e, ((e - 2 * away) % groups) ^ cross) for e in range(groups)])


def core_pairs(step):
    return [(e, e ^ 1) for e in range(lax.axis_size("ep"))]


def chip_pairs(step):
    groups = lax.axis_size("ep")
    return [(e, (e + 2 * step) % groups) for e in range(groups)]


def inner_pairs(step):
    replicas = lax.axis_size("rep")
    inner = replicas // OUTER
    return [(r, r - r % inner + (r + step) % inner) for r in range(replicas)]


def outer_pairs(step):
    replicas = lax.axis_size("rep")
    return [(r, (r + step * (replicas // OUTER)) % replicas) for r in range(replicas)]


def levels():
    ep, rep = lax.axis_index("ep"), lax.axis_index("rep")
    inner = lax.axis_size("rep") // OUTER
    return (
        ("ep", 2, ep % 2, core_pairs),
        ("ep", lax.axis_size("ep") // 2, ep // 2, chip_pairs),
        ("rep", inner, rep % inner, inner_pairs),
        ("rep", OUTER, rep // inner, outer_pairs),
    )


def swapped(x, level, steps=None):
    axis, size, place, pairs = level
    out = [] if steps else [lax.dynamic_index_in_dim(x, place, 0, keepdims=False)]
    for step in steps or range(1, size):
        sent = lax.dynamic_index_in_dim(x, (place + step) % size, 0, keepdims=False)
        out.append(lax.ppermute(sent, axis, pairs(step)))
    return out


def whole_swapped(x, level):
    axis, size, place, pairs = level
    return [x] + [lax.ppermute(x, axis, pairs(step)) for step in range(1, size)]


def total(arrays):
    return sum([x.astype(jnp.float32) for x in arrays[1:]], arrays[0].astype(jnp.float32))


def low_total(arrays):
    return total(arrays).astype(arrays[0].dtype)


def collected(x, level):
    axis, size, place, pairs = level
    if size == 2:
        other = lax.ppermute(x, axis, pairs(1))
        return jnp.concatenate([jnp.where(place == 0, x, other), jnp.where(place == 0, other, x)])
    out = lax.dynamic_update_index_in_dim(jnp.zeros((size, *x.shape), x.dtype), x, place, 0)
    for step in range(1, size):
        other = lax.ppermute(x, axis, pairs(step))
        out = lax.dynamic_update_index_in_dim(out, other, (place - step) % size, 0)
    return out.reshape(-1, *x.shape[1:])


def rows_swapped(x, level):
    return swapped(x.reshape(level[1], -1, x.shape[1]), level)


def near_swapped(x):
    replicas = lax.axis_size("rep")
    blocks = x.reshape(OUTER, replicas // OUTER, x.shape[0] // replicas, x.shape[1])
    return swapped(jnp.swapaxes(blocks, 0, 1), levels()[2])


def slot_table(expert_ids, priority, experts, capacity):
    ranks = priority.reshape(-1, 2)
    names = jnp.arange(experts, dtype=jnp.int32)[:, None]
    first, second = expert_ids[:, 0][None, :] == names, expert_ids[:, 1][None, :] == names
    rank = jnp.where(first, ranks[:, 0][None, :], jnp.where(second, ranks[:, 1][None, :], 1 << 20))
    slot = jnp.sum((rank[:, :, None] < rank[:, None, :]).astype(jnp.int32), axis=1)
    return jnp.where((first | second) & (slot < capacity), slot, -1)


def per_device(
    tokens,
    cotangent,
    gain_attn,
    w_qkv,
    w_out,
    rel_table,
    gain_moe,
    w_router,
    w_gate,
    w_up,
    w_down,
    expert_ids,
    priority,
    span_starts,
):
    tok_count = tokens.shape[0]
    experts = w_router.shape[1]
    groups = lax.axis_size("ep")
    chips = groups // 2
    capacity = 5 * tok_count // (2 * experts)
    own = lax.axis_index("ep")

    slots = slot_table(expert_ids, priority, experts, capacity)
    ids = jnp.transpose(expert_ids)
    table = jnp.concatenate([slots, ids], axis=0)
    info = [(table, to_sibling(table))] + [(from_chip(table, n), from_chip(table, n, 1)) for n in range(1, chips)]
    cot_sib = to_sibling(cotangent)
    cot_far = [from_chip(cotangent, n) for n in range(1, chips)]
    metas = []
    for pair in info:
        rows = []
        for table in pair:
            slot = lax.dynamic_slice_in_dim(table, own, 1, axis=0)
            one, two = table[experts : experts + 1], table[experts + 1 :]
            other = jnp.where(one == own, two, one)
            rows.append(jnp.concatenate([slot, other, jnp.full((6, tok_count), 1, jnp.int32) * own], axis=0))
        metas.append(jnp.stack(rows))

    diag = wide_diag(rel_table)
    token_float = tokens.astype(jnp.float32)
    normed, scale_attn = rms_forward(token_float, gain_attn)
    normed_low = normed.astype(jnp.bfloat16)
    qkv = jnp.dot(normed_low, w_qkv, preferred_element_type=jnp.float32).astype(jnp.bfloat16)
    attended_low, lse = attn_fwd(span_starts, qkv, diag)
    attended_low, cot_sib, cot_far, metas = tie(attended_low, cot_sib, cot_far, metas)
    mixed = token_float + jnp.dot(attended_low, w_out, preferred_element_type=jnp.float32)
    routed, scale_moe = rms_forward(mixed, gain_moe)
    routed_low = routed.astype(jnp.bfloat16)
    logits = jnp.dot(routed_low, w_router, preferred_element_type=jnp.float32)
    choose = expert_ids[:, :, None] == jnp.arange(experts, dtype=jnp.int32)[None, None, :]
    chosen = jnp.sum(jnp.where(choose, logits[:, None, :], 0.0), axis=-1)
    gates = jax.nn.softmax(chosen, axis=-1)

    router_rows = jnp.zeros((8, D), jnp.bfloat16).at[:experts].set(jnp.transpose(w_router))
    weights = (w_gate, w_up, w_down)
    core, chip, inner, outer = levels()

    tok_far = [from_chip(routed_low, n) for n in range(1, chips)]
    cots = [(cotangent, cot_sib)] + [(far, to_sibling(far)) for far in cot_far]
    pair = (routed_low, to_sibling(routed_low))
    made = expert_fwd(0, capacity, metas[0], router_rows, pair, cots[0], *weights)
    made, tok_far, cots = tie(made, tok_far, cots)
    toks = [(far, to_sibling(far)) for far in tok_far]
    outs, dots = [made[5:7]], [(made[7][0], made[7][1])]
    kept = [made[:5]]
    for away in range(1, chips):
        made = expert_fwd(away, capacity, metas[away], router_rows, toks[away - 1], cots[away], *weights)
        kept.append(made[:5])
        outs.append(made[5:7])
        dots.append((made[7][0], made[7][1]))
    rows_in, rows_out, hidden, slope, act = [list(x) for x in zip(*kept)]

    met = [[to_sibling(other) for mine, other in part] for part in (dots, outs)]
    down_low = grad_down(rows_out, hidden)
    down_low, slope, met, dots, outs = tie(down_low, slope, met, dots, outs)
    dots, outs = [
        [total([mine[n][0], got[n]]) for n in range(chips)] for mine, got in zip((dots, outs), met)
    ]
    outs_low = [x.astype(jnp.bfloat16) for x in outs[1:]]
    slope, outs_low, down_low = tie(slope, outs_low, down_low)
    far_outs = [from_chip(x, chips - 1 - n) for n, x in enumerate(outs_low)]
    far_dots = [from_chip(x, chips - 1 - n) for n, x in enumerate(dots[1:])]
    down_near = near_swapped(down_low)
    grads = [None] * chips
    for away in reversed(range(1, chips)):
        slope[away], act[away], *grads[away] = expert_bwd(
            away, capacity, metas[away], rows_out[away], slope[away], act[away], *weights
        )
    slope, far_outs, far_dots = tie(slope, far_outs, far_dots)
    far_grads = []
    for away in range(1, chips):
        far_grads += [from_chip(grads[away][0], chips - away), from_chip(grads[away][1], chips - away, 1)]
    slope[0], act[0], *here = expert_bwd(0, capacity, metas[0], rows_out[0], slope[0], act[0], *weights)
    slope, down_near = tie(slope, down_near)
    down_near = low_total(down_near)
    slope, down_near = tie(slope, down_near)
    near_grads = to_sibling(here[1])
    down_far = swapped(down_near, outer)
    gate_low, up_low = grad_in(rows_in, slope, act)
    gate_low, up_low, far_grads, near_grads = tie(gate_low, up_low, far_grads, near_grads)
    grad_pairs = total([here[0], near_grads] + far_grads)
    grad_gates_all = total([dots[0]] + far_dots)
    block_out = (mixed + total([outs[0]] + far_outs)).astype(jnp.bfloat16)
    gate_near = near_swapped(gate_low)

    grad_out = cotangent.astype(jnp.float32)
    by_token = jnp.transpose(grad_gates_all[:experts])
    grad_gates = jnp.sum(jnp.where(choose, by_token[:, None, :], 0.0), axis=-1)
    grad_chosen = gates * (grad_gates - jnp.sum(gates * grad_gates, axis=-1, keepdims=True))
    grad_logits = jnp.sum(jnp.where(choose, grad_chosen[:, :, None], 0.0), axis=1).astype(jnp.bfloat16)
    grad_w_router = jnp.einsum("td,te->de", routed_low, grad_logits, preferred_element_type=jnp.float32)
    grad_routed = grad_pairs + jnp.einsum(
        "te,de->td", grad_logits, w_router, preferred_element_type=jnp.float32
    )
    grad_norm_moe, grad_gain_moe = rms_backward(mixed, scale_moe, gain_moe, grad_routed)
    grad_mixed = grad_out + grad_norm_moe
    grad_branch = grad_mixed.astype(jnp.bfloat16)
    grad_attended = jnp.einsum(
        "te,de->td", grad_branch, w_out, preferred_element_type=jnp.float32
    ).astype(jnp.bfloat16)

    grad_attended, grad_branch, block_out = tie(grad_attended, grad_branch, block_out)
    first = attn_bwd(span_starts, qkv, grad_attended, attended_low, lse, diag, 0)
    early = grad_rows(attended_low, grad_branch, "grad_out", 5 * D // 2, 3 * D // 2)
    early = grad_rows(normed_low, first[0], "grad_qkv_0", 5 * D // 2, 0, early)
    early, grad_attended, gate_near, down_far = tie(early, grad_attended, gate_near, down_far)
    gate_near = low_total(gate_near)
    sum_down = total(down_far)
    gate_near, grad_attended, sum_down, up_low = tie(gate_near, grad_attended, sum_down, up_low)
    gate_far = swapped(gate_near, outer)
    up_near = near_swapped(up_low)
    early = rows_swapped(early, core)
    second = attn_bwd(span_starts, qkv, grad_attended, attended_low, lse, diag, 1)
    second, early, gate_far, up_near = tie(second, early, gate_far, up_near)
    second = list(second)
    up_near, early = tie(low_total(up_near), low_total(early))
    early = rows_swapped(early, chip)
    own = lax.dynamic_index_in_dim(up_near, levels()[3][2], 0, keepdims=False)
    up_far = swapped(up_near, outer, (1, OUTER - 1))
    half_second = grad_rows(normed_low, second[0], "grad_qkv_1")
    late = rows_swapped(half_second, core)
    half_second, *second[:1] = tie(half_second, second[0])
    grad_normed = grad_normed_of(first[0], second[0], w_qkv)
    late, grad_normed, early, up_far = tie(late, grad_normed, early, up_far)
    early, late = tie(low_total(early), low_total(late))
    late = rows_swapped(late, inner)
    last = swapped(up_near, outer, tuple(range(2, OUTER - 1)))
    grad_norm_attn, grad_gain_attn = rms_backward(token_float, scale_attn, gain_attn, grad_normed)
    grad_tokens = grad_mixed + grad_norm_attn
    grad_rel_table = rel_grad(jnp.concatenate([first[1], second[1]]), jnp.concatenate([first[2], second[2]]))
    small = jnp.concatenate(
        [
            jnp.transpose(grad_w_router),
            jnp.pad(grad_rel_table.reshape(1, -1), ((0, 0), (0, D - BUCKETS * H))),
            grad_gain_attn[None],
            grad_gain_moe[None],
        ]
    )
    late, small, grad_tokens = tie(late, small, grad_tokens)
    late, early = tie(low_total(late), early)
    small = whole_swapped(small, core)
    late, early, last, small = tie(rows_swapped(late, chip), rows_swapped(early, inner), last, small)
    wide = early[0].shape[1]
    both, small = tie(jnp.concatenate([low_total(early), low_total(late)], axis=1), total(small))
    both, small = tie(rows_swapped(both, outer), whole_swapped(small, chip))
    both, small = tie(low_total(both), total(small))
    both, small = tie(collected(both, outer), whole_swapped(small, inner))
    early, late, small = tie(both[:, :wide], both[:, wide:], total(small))
    early, late, small = tie(collected(early, inner), collected(late, chip), whole_swapped(small, outer))
    small = total(small)
    early, late = tie(collected(early, chip), collected(late, inner))
    early, late = tie(collected(early, core), collected(late, core))
    sum_first, sum_second = early[:, : 3 * D // 2].astype(jnp.float32), late.astype(jnp.float32)
    sum_w_out = early[:, 3 * D // 2 :].astype(jnp.float32)
    up_far = [own] + up_far + last
    sum_gate, sum_up = total(gate_far), total(up_far)
    sum_w_qkv = jnp.concatenate(
        [x[:, n * D // 2 : (n + 1) * D // 2] for n in range(3) for x in (sum_first, sum_second)], axis=1
    )
    small = (
        small[experts, : BUCKETS * H].reshape(BUCKETS, H),
        jnp.transpose(small[:experts]),
        small[experts + 1],
        small[experts + 2],
    )
    return (
        block_out,
        grad_tokens,
        small[2],
        sum_w_qkv,
        sum_w_out,
        small[0],
        small[3],
        small[1],
        sum_gate[None],
        sum_up[None],
        sum_down[None],
    )


def solution(mesh):
    placed = (
        P(("rep", "ep"), None),
        P(("rep", "ep"), None),
        P(),
        P(),
        P(),
        P(),
        P(),
        P(),
        P("ep", None, None),
        P("ep", None, None),
        P("ep", None, None),
        P(("rep", "ep"), None),
        P(("rep", "ep"), None),
        P(("rep", "ep"), None),
    )
    return jax.shard_map(
        per_device,
        mesh=mesh,
        in_specs=placed,
        out_specs=(
            P(("rep", "ep"), None),
            P(("rep", "ep"), None),
            P(),
            P(),
            P(),
            P(),
            P(),
            P(),
            P("ep", "rep", None),
            P("ep", "rep", None),
            P("ep", "rep", None),
        ),
        check_vma=False,
    )
```

```python
from functools import partial
import jax
import jax.numpy as jnp
import numpy as np
from jax import lax
from jax.sharding import PartitionSpec as P
from jax.experimental import pallas as pl
from jax.experimental.pallas import tpu as pltpu

D = 1024
H = 16
HD = 64
BUCKETS = 32
MAXDIST = 128
SEQ = 1024
PIC = 256
EPSILON = 1e-06
NEGATIVE = -1e30
LOG2E = 1.4426950408889634
QB = 256
KB = 128
WIDE = 768
VMEM_LIMIT = 56 * 1024 * 1024
LIGHT = pl.CostEstimate(flops=1000, bytes_accessed=1000, transcendentals=0)


def bucket_of(offsets):
    half_count = BUCKETS // 2
    near_count = half_count // 2
    upper_part = (offsets > 0).astype(np.int64) * half_count
    distance = np.abs(offsets)
    ratio = np.log(np.maximum(distance, 1) / near_count) / np.log(MAXDIST / near_count)
    distant_bucket = np.minimum(
        near_count + np.floor(ratio * (half_count - near_count)).astype(np.int64), half_count - 1
    )
    return upper_part + np.where(distance < near_count, distance, distant_bucket)


def wide_onehot():
    places = np.arange(WIDE)
    offsets = np.where(places < 640, 256 - places, 1024 - places)
    return (bucket_of(offsets)[:, None] == np.arange(BUCKETS)[None, :]).astype(np.float32)


def dot_nt(a, b):
    return lax.dot_general(a, b, (((1,), (1,)), ((), ())), preferred_element_type=jnp.float32)


def dot_nn(a, b):
    return lax.dot_general(a, b, (((1,), (0,)), ((), ())), preferred_element_type=jnp.float32)


def key_count(i):
    return min((i + 2) * QB, SEQ)


def fill_mask(span_ref, mask_s):
    for i in range(SEQ // QB):
        for d in range(4):
            if 2 * i + d >= SEQ // KB:
                continue
            k = (2 * i + d) * KB + lax.broadcasted_iota(jnp.int32, (KB, QB), 0)
            q = i * QB + lax.broadcasted_iota(jnp.int32, (KB, QB), 1)
            ok = k <= q
            for s in range(2):
                start = span_ref[0, s]
                ok = ok | ((k >= start) & (k < start + PIC) & (q >= start) & (q < start + PIC))
            mask_s[4 * i + d] = jnp.where(ok, 0.0, NEGATIVE)


def spread_bias(diag_ref, h, bias_s):
    row = jnp.broadcast_to(diag_ref[0, h : h + 1, :], (KB, WIDE))
    bias_s[h] = pltpu.roll(row, 0, 1, stride=1, stride_axis=0)


def shifted(s, i, kt, h, bias_s, mask_s, low, high, row):
    d = kt - 2 * i
    if d <= -2:
        return s + (low if row is None else low + row)
    if d >= 3:
        s = s + (high if row is None else high + row)
    else:
        s = s + bias_s[h, :, (2 - d) * 128 : (2 - d) * 128 + 256]
        if row is not None:
            s = s + row
    if d >= 0:
        s = s + mask_s[4 * i + d]
    return s


def diagonal_sums(x):
    rows = x.shape[0]
    while rows > 8:
        rows //= 2
        x = x[:rows] + pltpu.roll(x[rows:], WIDE - rows, 1)
    total = x[0:1]
    for r in range(1, rows):
        total = total + pltpu.roll(x[r : r + 1], WIDE - r, 1)
    return total


def half_lanes(x, h):
    lane = lax.broadcasted_iota(jnp.int32, x.shape, 1)
    return jnp.where((lane < HD) if h == 0 else (lane >= HD), x, jnp.zeros_like(x))


def both_halves(ref, i):
    rows = ref[i * QB : (i + 1) * QB, :]
    return jnp.concatenate([half_lanes(rows, h) for h in range(2)], axis=0)


def attn_fwd_kernel(span_ref, q_ref, k_ref, v_ref, diag_ref, out_ref, lse_ref, mask_s, bias_s, vt_s, s_s, p_s):
    @pl.when(pl.program_id(0) == 0)
    def _():
        fill_mask(span_ref, mask_s)

    vt_s[:128] = jnp.transpose(v_ref[...])
    vt_s[128:] = jnp.ones((16, SEQ), jnp.bfloat16)
    for h in range(2):
        spread_bias(diag_ref, h, bias_s)
    scale = LOG2E * HD ** (-0.5)
    blocks = SEQ // QB

    def products(i):
        s_s[i % 2, : key_count(i)] = dot_nt(k_ref[: key_count(i), :], both_halves(q_ref, i))

    products(0)
    for i in range(blocks):
        nk = key_count(i)
        if i + 1 < blocks:
            products(i + 1)
        tops = []
        for h in range(2):
            low = diag_ref[0, h : h + 1, 600:601]
            high = diag_ref[0, h : h + 1, 0:1]
            cols = slice(h * QB, (h + 1) * QB)
            top = None
            for kt in range(nk // KB):
                tile = slice(kt * KB, (kt + 1) * KB)
                s = shifted(s_s[i % 2, tile, cols] * scale, i, kt, h, bias_s, mask_s, low, high, None)
                s_s[i % 2, tile, cols] = s
                t = jnp.max(s.reshape(KB // 8, 8, QB), axis=0)
                top = t if top is None else jnp.maximum(top, t)
            m = jnp.max(top, axis=0, keepdims=True)
            tops.append(m)
            for kt in range(nk // KB):
                tile = slice(kt * KB, (kt + 1) * KB)
                p_s[i % 2, tile, cols] = jnp.exp2(s_s[i % 2, tile, cols] - m).astype(jnp.bfloat16)
        ot = dot_nn(vt_s[:, :nk], p_s[i % 2, :nk])
        outs = []
        for h in range(2):
            cols = slice(h * QB, (h + 1) * QB)
            total = ot[128:129, cols]
            outs.append(ot[h * HD : (h + 1) * HD, cols] / total)
            lse_ref[0, h : h + 1, i * QB : (i + 1) * QB] = tops[h] + jnp.log2(total)
        out_ref[i * QB : (i + 1) * QB, :] = jnp.transpose(jnp.concatenate(outs, axis=0)).astype(jnp.bfloat16)


def attn_fwd(spans, qkv, diag):
    col = lambda off: pl.BlockSpec((SEQ, 128), lambda g: (0, g + off))
    return pl.pallas_call(
        attn_fwd_kernel,
        grid=(H // 2,),
        in_specs=[
            pl.BlockSpec(memory_space=pltpu.SMEM),
            col(0),
            col(8),
            col(16),
            pl.BlockSpec((1, 2, WIDE), lambda g: (g, 0, 0)),
        ],
        out_specs=[col(0), pl.BlockSpec((1, 2, SEQ), lambda g: (g, 0, 0))],
        out_shape=[
            jax.ShapeDtypeStruct((SEQ, D), jnp.bfloat16),
            jax.ShapeDtypeStruct((H // 2, 2, SEQ), jnp.float32),
        ],
        scratch_shapes=[
            pltpu.VMEM((16, KB, QB), jnp.float32),
            pltpu.VMEM((2, KB, WIDE), jnp.float32),
            pltpu.VMEM((128 + 16, SEQ), jnp.bfloat16),
            pltpu.VMEM((2, SEQ, 2 * QB), jnp.float32),
            pltpu.VMEM((2, SEQ, 2 * QB), jnp.bfloat16),
        ],
        compiler_params=pltpu.CompilerParams(vmem_limit_bytes=VMEM_LIMIT),
        cost_estimate=LIGHT,
        name="attn_fwd",
    )(spans, qkv, qkv, qkv, diag)


def attn_bwd_kernel(
    span_ref, q_ref, k_ref, v_ref, g_ref, o_ref, lse_ref, diag_ref, *rest
):
    (
        out_ref, drel_ref, far_ref,
        mask_s, bias_s, acc_s, kt_s, s_s, dp_s, p_s, ds_s, dk_s, dv_s, delta_s,
    ) = rest[-14:]
    part = pl.program_id(1)

    @pl.when((pl.program_id(0) == 0) & (part == 0))
    def _():
        fill_mask(span_ref, mask_s)

    @pl.when(part == 1)
    def _():
        out_ref[...] = (dk_s[...] * HD ** (-0.5)).astype(jnp.bfloat16)

    @pl.when(part == 2)
    def _():
        out_ref[...] = dv_s[...].astype(jnp.bfloat16)

    @pl.when(part == 0)
    def _():
        kt_s[...] = jnp.transpose(k_ref[...])
        prod = jnp.transpose(g_ref[...].astype(jnp.float32) * o_ref[...].astype(jnp.float32))
        for h in range(2):
            spread_bias(diag_ref, h, bias_s)
            delta_s[h : h + 1] = jnp.sum(prod[h * HD : (h + 1) * HD], axis=0, keepdims=True)
        acc_s[...] = jnp.zeros_like(acc_s)
        far_ref[...] = jnp.zeros_like(far_ref)
        scale = LOG2E * HD ** (-0.5)
        blocks = SEQ // QB

        def products(i):
            nk = key_count(i)
            s_s[i % 2, :nk] = dot_nt(k_ref[:nk, :], both_halves(q_ref, i))
            dp_s[i % 2, :nk] = dot_nt(v_ref[:nk, :], both_halves(g_ref, i))

        products(blocks - 1)
        for i in reversed(range(blocks)):
            nk = key_count(i)
            rows = slice(i * QB, (i + 1) * QB)
            if i > 0:
                products(i - 1)
            for h in range(2):
                low = diag_ref[0, h : h + 1, 600:601]
                high = diag_ref[0, h : h + 1, 0:1]
                nlse = -lse_ref[0, h : h + 1, rows]
                delta = delta_s[h : h + 1, rows]
                cols = slice(h * QB, (h + 1) * QB)
                for kt in range(nk // KB):
                    tile = slice(kt * KB, (kt + 1) * KB)
                    d = kt - 2 * i
                    s = s_s[i % 2, tile, cols] * scale
                    p = jnp.exp2(shifted(s, i, kt, h, bias_s, mask_s, low, high, nlse))
                    ds = p * (dp_s[i % 2, tile, cols] - delta)
                    p_s[i % 2, tile, cols] = p.astype(jnp.bfloat16)
                    ds_s[i % 2, tile, cols] = ds.astype(jnp.bfloat16)
                    if -1 <= d <= 2:
                        near = slice((2 - d) * 128, (2 - d) * 128 + 256)
                        acc_s[h, :, near] += ds
                    else:
                        far_ref[0, h, 0 if d < 0 else 1] += jnp.sum(ds.reshape(KB // 8, 8, QB), axis=0)
            dq = dot_nn(kt_s[:, :nk], ds_s[i % 2, :nk])
            dq = jnp.concatenate([dq[h * HD : (h + 1) * HD, h * QB : (h + 1) * QB] for h in range(2)], axis=0)
            out_ref[rows, :] = (jnp.transpose(dq) * HD ** (-0.5)).astype(jnp.bfloat16)
            dv = dot_nn(p_s[i % 2, :nk], both_halves(g_ref, i))
            dk = dot_nn(ds_s[i % 2, :nk], both_halves(q_ref, i))
            if i == blocks - 1:
                dv_s[...] = dv
                dk_s[...] = dk
            else:
                dv_s[:nk] += dv
                dk_s[:nk] += dk
        for h in range(2):
            drel_ref[0, h : h + 1, :] = diagonal_sums(acc_s[h])


def attn_bwd(spans, qkv, grad_att, att, lse, diag, part, buffer):
    buffers = () if buffer is None else (buffer,)
    pairs = H // 8
    base = part * pairs
    col = lambda off: pl.BlockSpec((SEQ, 128), lambda g, p: (0, base + g + off))
    one = lambda *dims: pl.BlockSpec((1, *dims), lambda g, p: (base + g,) + (0,) * len(dims))
    new = lambda *dims: pl.BlockSpec((1, *dims), lambda g, p: (g,) + (0,) * len(dims))
    return pl.pallas_call(
        attn_bwd_kernel,
        grid=(pairs, 3),
        in_specs=[
            pl.BlockSpec(memory_space=pltpu.SMEM),
            col(0),
            col(8),
            col(16),
            col(0),
            col(0),
            one(2, SEQ),
            one(2, WIDE),
        ]
        + [pl.BlockSpec(memory_space=pl.ANY)] * len(buffers),
        out_specs=[
            pl.BlockSpec((SEQ, 128), lambda g, p: (0, p * (H // 2) + base + g)),
            new(2, WIDE),
            new(2, 2, 8, QB),
        ],
        out_shape=[
            jax.ShapeDtypeStruct((SEQ, 3 * D), jnp.bfloat16),
            jax.ShapeDtypeStruct((pairs, 2, WIDE), jnp.float32),
            jax.ShapeDtypeStruct((pairs, 2, 2, 8, QB), jnp.float32),
        ],
        scratch_shapes=[
            pltpu.VMEM((16, KB, QB), jnp.float32),
            pltpu.VMEM((2, KB, WIDE), jnp.float32),
            pltpu.VMEM((2, KB, WIDE), jnp.float32),
            pltpu.VMEM((128, SEQ), jnp.bfloat16),
            pltpu.VMEM((2, SEQ, 2 * QB), jnp.float32),
            pltpu.VMEM((2, SEQ, 2 * QB), jnp.float32),
            pltpu.VMEM((2, SEQ, 2 * QB), jnp.bfloat16),
            pltpu.VMEM((2, SEQ, 2 * QB), jnp.bfloat16),
            pltpu.VMEM((SEQ, 128), jnp.float32),
            pltpu.VMEM((SEQ, 128), jnp.float32),
            pltpu.VMEM((2, SEQ), jnp.float32),
        ],
        input_output_aliases={8: 0} if buffers else {},
        compiler_params=pltpu.CompilerParams(vmem_limit_bytes=VMEM_LIMIT),
        cost_estimate=LIGHT,
        name=f"attn_bwd_{part}",
    )(spans, qkv, qkv, qkv, grad_att, att, lse, diag, *buffers)


def wide_diag(rel_table):
    return jnp.einsum(
        "mb,bh->hm", jnp.asarray(wide_onehot()), rel_table * LOG2E, precision=lax.Precision.HIGHEST
    ).reshape(H // 2, 2, WIDE)


def rel_grad(drel, far):
    sums = drel.reshape(H, WIDE)
    far = jnp.sum(far.reshape(H, 2, 8 * QB), axis=-1)
    sums = sums.at[:, 600].add(far[:, 0]).at[:, 0].add(far[:, 1])
    return jnp.einsum("mb,hm->bh", jnp.asarray(wide_onehot()), sums, precision=lax.Precision.HIGHEST)


FT = 256


def dot_tn(a, b):
    return lax.dot_general(a, b, (((0,), (0,)), ((), ())), preferred_element_type=jnp.float32)


VMEM_MOST = 58 * 1024 * 1024
PARTS = 1


def slot_onehot(meta_ref, n, rows):
    slot = meta_ref[n, 0:1]
    return lax.broadcasted_iota(jnp.int32, (rows, slot.shape[1]), 0) == slot


def expert_fwd_kernel(meta_ref, wr_ref, tok_a, tok_b, cot_a, cot_b, gate_ref, up_ref, down_ref, *rest):
    x_ref, gc_ref, hid_ref, slope_ref, act_ref, p_a, p_b, gg_ref, hot_s, turned_s, hid_s, gate_s = rest[-12:]
    step = pl.program_id(0)
    wide = hid_s.shape[1] // FT
    deep = D // FT
    rows = x_ref.shape[0] // 2
    count = tok_a.shape[0]
    pair = [(0, tok_a, cot_a, slice(0, rows)), (1, tok_b, cot_b, slice(rows, 2 * rows))]
    chunk = 2 * rows // PARTS

    @pl.when(step == 0)
    def _():
        for n, tok_ref, cot_ref, here in pair:
            logits = dot_nt(wr_ref[...], tok_ref[...])
            other, own = meta_ref[n, 1:2], meta_ref[n, 2:3]
            names = lax.broadcasted_iota(jnp.int32, logits.shape, 0)
            mine = jnp.sum(jnp.where(names == own, logits, 0.0), axis=0, keepdims=True)
            theirs = jnp.sum(jnp.where(names == other, logits, 0.0), axis=0, keepdims=True)
            gate = 1.0 / (1.0 + jnp.exp(theirs - mine))
            hot = slot_onehot(meta_ref, n, rows)
            gates = jnp.sum(jnp.where(hot, gate, 0.0), axis=1, keepdims=True)
            lane = lax.broadcasted_iota(jnp.int32, (rows, 128), 1)
            gate_s[here] = jnp.where(lane < 64, gates, 0.0)
            hot = jnp.where(hot, 1.0, 0.0).astype(jnp.bfloat16)
            hot_s[n] = hot
            turned_s[n] = jnp.transpose(hot)
            x_ref[here] = dot_nn(hot_s[n], tok_ref[...]).astype(jnp.bfloat16)

    @pl.when(step < wide)
    def _():
        cols = pl.ds(pl.multiple_of(step * FT, FT), FT)
        root = (2.0 / np.pi) ** 0.5
        for c in range(PARTS):
            here = slice(c * chunk, (c + 1) * chunk)
            g = dot_nn(x_ref[here], gate_ref[0])
            u = dot_nn(x_ref[here], up_ref[0])
            square = g * g
            t = jnp.tanh(g * (root + (root * 0.044715) * square))
            half = 0.5 + 0.5 * t
            act = g * half
            slope = half + (act * (1.0 - t)) * (root + (3.0 * root * 0.044715) * square)
            slope_ref[here] = (u * slope).astype(jnp.bfloat16)
            act_ref[here] = act.astype(jnp.bfloat16)
            hidden = (act * u).astype(jnp.bfloat16)
            hid_s[here, cols] = hidden
            hid_ref[here] = hidden

    @pl.when(step >= wide)
    def _():
        cols = pl.ds(pl.multiple_of((step - wide) * FT, FT), FT)
        outs = dot_nn(hid_s[...], down_ref[0])
        for s, tok_ref, cot_ref, here in pair:
            gates = gate_s[here, 0:1]
            out = outs[here].astype(jnp.bfloat16).astype(jnp.float32)
            cot = dot_nn(hot_s[s], cot_ref[...])
            lane = lax.broadcasted_iota(jnp.int32, (rows, 128), 1)
            gate_s[here] += jnp.where(lane < 64, 0.0, jnp.sum(out * cot, axis=1, keepdims=True))
            gc_ref[here, cols] = (gates * cot).astype(jnp.bfloat16)
            p_ref = (p_a, p_b)[s]
            p_ref[...] = dot_nn(turned_s[s], (gates * out).astype(jnp.bfloat16)).astype(jnp.bfloat16)

    @pl.when(step == wide + deep - 1)
    def _():
        for s, tok_ref, cot_ref, here in pair:
            gg = jnp.where(slot_onehot(meta_ref, s, rows), gate_s[here, 64:65], 0.0)
            gg = jnp.sum(gg, axis=0, keepdims=True)
            own = meta_ref[s, 2:3]
            gg_ref[s] = jnp.where(lax.broadcasted_iota(jnp.int32, (8, count), 0) == own, gg, 0.0)


def expert_bwd_kernel(meta_ref, gc_ref, slope_ref, act_ref, down_ref, gate_ref, up_ref, dg_ref, du_ref, dp_a, dp_b, turned_s, dg_s, du_s):
    step = pl.program_id(0)
    wide = dg_s.shape[1] // FT
    rows = gc_ref.shape[0] // 2

    @pl.when(step == 0)
    def _():
        for n in range(2):
            hot = jnp.where(slot_onehot(meta_ref, n, rows), 1.0, 0.0).astype(jnp.bfloat16)
            turned_s[n] = jnp.transpose(hot)

    @pl.when(step < wide)
    def _():
        cols = pl.ds(pl.multiple_of(step * FT, FT), FT)
        dh = dot_nt(gc_ref[...], down_ref[0])
        dg = (dh * slope_ref[...].astype(jnp.float32)).astype(jnp.bfloat16)
        du = (dh * act_ref[...].astype(jnp.float32)).astype(jnp.bfloat16)
        dg_s[:, cols] = dg
        du_s[:, cols] = du
        dg_ref[...] = dg
        du_ref[...] = du

    @pl.when(step >= wide)
    def _():
        dx = (dot_nt(dg_s[...], gate_ref[0]) + dot_nt(du_s[...], up_ref[0])).astype(jnp.bfloat16)
        for s in range(2):
            dp_ref = (dp_a, dp_b)[s]
            dp_ref[...] = dot_nn(turned_s[s], dx[s * rows : (s + 1) * rows]).astype(jnp.bfloat16)


def low_shape(*shape):
    return jax.ShapeDtypeStruct(shape, jnp.bfloat16)


def expert_fwd(place, rows, meta, router_rows, toks, cots, w_gate, w_up, w_down):
    count = toks[0].shape[0]
    width = w_gate.shape[2]
    wide = width // FT
    deep = D // FT
    once = pl.Buffered(1)
    whole = lambda *shape: pl.BlockSpec(shape, lambda j: (0,) * len(shape), pipeline_mode=once)
    mine = whole(2 * rows, D)
    one = lambda j: jnp.minimum(j, wide - 1)
    two = lambda j: jnp.maximum(j - wide, 0)
    strip = pl.BlockSpec((2 * rows, FT), lambda j: (0, one(j)))
    total = 2 * rows
    return pl.pallas_call(
        expert_fwd_kernel,
        grid=(wide + deep,),
        in_specs=[whole(2, 8, count), whole(8, D)]
        + [whole(count, D)] * 2
        + [pl.BlockSpec((count, FT), lambda j: (0, two(j)))] * 2
        + [pl.BlockSpec((1, D, FT), lambda j: (0, 0, one(j)))] * 2
        + [pl.BlockSpec((1, width, FT), lambda j: (0, 0, two(j)))],
        out_specs=[
            mine,
            mine,
            strip,
            strip,
            strip,
            pl.BlockSpec((count, FT), lambda j: (0, two(j))),
            pl.BlockSpec((count, FT), lambda j: (0, two(j))),
            whole(2, 8, count),
        ],
        out_shape=[low_shape(total, D)] * 2
        + [low_shape(total, width)] * 3
        + [low_shape(count, D)] * 2
        + [jax.ShapeDtypeStruct((2, 8, count), jnp.float32)],
        scratch_shapes=[
            pltpu.VMEM((2, rows, count), jnp.bfloat16),
            pltpu.VMEM((2, count, rows), jnp.bfloat16),
            pltpu.VMEM((2 * rows, width), jnp.bfloat16),
            pltpu.VMEM((2 * rows, 128), jnp.float32),
        ],
        compiler_params=pltpu.CompilerParams(vmem_limit_bytes=VMEM_MOST),
        cost_estimate=LIGHT,
        name=f"expert_fwd_{place}",
    )(meta, router_rows, *toks, *cots, w_gate, w_up, w_down)


def expert_bwd(place, rows, meta, gc, slope, act, w_gate, w_up, w_down):
    count = meta.shape[2]
    total, width = slope.shape
    wide = width // FT
    deep = D // FT
    once = pl.Buffered(1)
    one = lambda j: jnp.minimum(j, wide - 1)
    two = lambda j: jnp.maximum(j - wide, 0)
    strip = pl.BlockSpec((2 * rows, FT), lambda j: (0, one(j)))
    return pl.pallas_call(
        expert_bwd_kernel,
        grid=(wide + deep,),
        in_specs=[
            pl.BlockSpec((2, 8, count), lambda j: (0, 0, 0), pipeline_mode=once),
            pl.BlockSpec((2 * rows, D), lambda j: (0, 0), pipeline_mode=once),
            strip,
            strip,
            pl.BlockSpec((1, FT, D), lambda j: (0, one(j), 0)),
            pl.BlockSpec((1, FT, width), lambda j: (0, two(j), 0)),
            pl.BlockSpec((1, FT, width), lambda j: (0, two(j), 0)),
        ],
        out_specs=[strip] * 2 + [pl.BlockSpec((count, FT), lambda j: (0, two(j)))] * 2,
        out_shape=[low_shape(total, width)] * 2 + [low_shape(count, D)] * 2,
        scratch_shapes=[
            pltpu.VMEM((2, count, rows), jnp.bfloat16),
            pltpu.VMEM((2 * rows, width), jnp.bfloat16),
            pltpu.VMEM((2 * rows, width), jnp.bfloat16),
        ],
        compiler_params=pltpu.CompilerParams(vmem_limit_bytes=VMEM_MOST),
        cost_estimate=LIGHT,
        name=f"expert_bwd_{place}",
    )(meta, gc, slope, act, w_down, w_gate, w_up)


def turn_into(turned_s, refs):
    first = 0
    for ref in refs:
        turned_s[:, first : first + ref.shape[0]] = jnp.transpose(ref[...])
        first += ref.shape[0]


def row_sums(turned_s, refs):
    first, out = 0, None
    for ref in refs:
        part = dot_nn(turned_s[:, first : first + ref.shape[0]], ref[...])
        out = part if out is None else out + part
        first += ref.shape[0]
    return out


def grad_down_kernel(*refs):
    out_ref, turned_s = refs[-2:]
    many = (len(refs) - 2) // 2

    @pl.when(pl.program_id(0) == 0)
    def _():
        turn_into(turned_s, refs[:many])

    out_ref[...] = jnp.transpose(row_sums(turned_s, refs[many : 2 * many])).astype(jnp.bfloat16)


def grad_in_kernel(many, inner, place_ref, *refs):
    sides = refs[3 * many : 3 * many + 2 * inner]
    turned_s, tile_s = refs[-2:]
    blocks, rows, wide = tile_s.shape

    @pl.when(pl.program_id(0) == 0)
    def _():
        turn_into(turned_s, refs[:many])

    for kind in range(2):
        tile = row_sums(turned_s, refs[(kind + 1) * many : (kind + 2) * many]).astype(jnp.bfloat16)
        tile_s[...] = tile.reshape(blocks, rows, wide)
        for away in range(inner):
            side = lax.rem(place_ref[0] + away, inner)
            for block in range(blocks // inner):
                sides[kind * inner + away][block] = tile_s[block * inner + side]


def grad_down(gc, hidden):
    rows, width = hidden[0].shape
    once = pl.Buffered(1)
    return pl.pallas_call(
        grad_down_kernel,
        grid=(width // FT,),
        in_specs=[pl.BlockSpec((rows, D), lambda j: (0, 0), pipeline_mode=once)] * len(gc)
        + [pl.BlockSpec((rows, FT), lambda j: (0, j))] * len(gc),
        out_specs=pl.BlockSpec((FT, D), lambda j: (j, 0)),
        out_shape=low_shape(width, D),
        scratch_shapes=[pltpu.VMEM((D, rows * len(gc)), jnp.bfloat16)],
        compiler_params=pltpu.CompilerParams(vmem_limit_bytes=VMEM_LIMIT),
        cost_estimate=LIGHT,
        name="grad_down",
    )(*gc, *hidden)


def grad_in(place, inner, blocks, xs, dgate, dup):
    rows, width = dgate[0].shape
    many = len(xs)
    once = pl.Buffered(1)
    out = pl.BlockSpec((blocks // inner, D // blocks, FT), lambda j: (0, 0, j))
    made = pl.pallas_call(
        partial(grad_in_kernel, many, inner),
        grid=(width // FT,),
        in_specs=[pl.BlockSpec(memory_space=pltpu.SMEM)]
        + [pl.BlockSpec((rows, D), lambda j: (0, 0), pipeline_mode=once)] * many
        + [pl.BlockSpec((rows, FT), lambda j: (0, j))] * (2 * many),
        out_specs=[out] * (2 * inner),
        out_shape=[low_shape(blocks // inner, D // blocks, width)] * (2 * inner),
        scratch_shapes=[
            pltpu.VMEM((D, rows * many), jnp.bfloat16),
            pltpu.VMEM((blocks, D // blocks, FT), jnp.bfloat16),
        ],
        compiler_params=pltpu.CompilerParams(vmem_limit_bytes=VMEM_LIMIT),
        cost_estimate=LIGHT,
        name="grad_in",
    )(place, *xs, *dgate, *dup)
    return made[:inner], made[inner:]


def grad_attn_kernel(place_ref, normed_ref, attended_ref, right_ref, branch_ref, own_ref, other_ref, turned_s):
    step = pl.program_id(0)
    first = pl.num_programs(0) - 2

    @pl.when(step == 0)
    def _():
        turned_s[...] = jnp.transpose(normed_ref[...])

    @pl.when(step == first)
    def _():
        turned_s[...] = jnp.transpose(attended_ref[...])

    def hand(right):
        made = dot_nn(turned_s[...], right).astype(jnp.bfloat16)
        upper, lower = made[: D // 2], made[D // 2 :]
        swap = place_ref[0] == 1
        own_ref[...] = jnp.where(swap, lower, upper)
        other_ref[...] = jnp.where(swap, upper, lower)

    @pl.when(step < first)
    def _():
        hand(right_ref[...])

    @pl.when(step >= first)
    def _():
        hand(branch_ref[...])


def grad_attn(place, normed, attended, grad_qkv, branch):
    count = normed.shape[0]
    whole = pl.BlockSpec((count, D), lambda j: (0, 0), pipeline_mode=pl.Buffered(1))
    half = pl.BlockSpec((D // 2, 512), lambda j: (0, j))
    return pl.pallas_call(
        grad_attn_kernel,
        grid=(8,),
        in_specs=[
            pl.BlockSpec(memory_space=pltpu.SMEM),
            whole,
            whole,
            pl.BlockSpec((count, 512), lambda j: (0, jnp.minimum(j, 5))),
            pl.BlockSpec((count, 512), lambda j: (0, jnp.maximum(j - 6, 0))),
        ],
        out_specs=[half, half],
        out_shape=[low_shape(D // 2, 4 * D)] * 2,
        scratch_shapes=[pltpu.VMEM((D, count), jnp.bfloat16)],
        compiler_params=pltpu.CompilerParams(vmem_limit_bytes=VMEM_LIMIT),
        cost_estimate=LIGHT,
        name="grad_attn",
    )(place, normed, attended, grad_qkv, branch)


def grad_normed_kernel(grad_ref, w_ref, out_ref):
    @pl.when(pl.program_id(0) == 0)
    def _():
        out_ref[...] = dot_nt(grad_ref[...], w_ref[...])

    @pl.when(pl.program_id(0) > 0)
    def _():
        out_ref[...] += dot_nt(grad_ref[...], w_ref[...])


def grad_normed_of(grad_qkv, w_qkv):
    count = grad_qkv.shape[0]
    return pl.pallas_call(
        grad_normed_kernel,
        grid=(3,),
        in_specs=[pl.BlockSpec((count, D), lambda p: (0, p)), pl.BlockSpec((D, D), lambda p: (0, p))],
        out_specs=pl.BlockSpec((count, D), lambda p: (0, 0)),
        out_shape=jax.ShapeDtypeStruct((count, D), jnp.float32),
        compiler_params=pltpu.CompilerParams(vmem_limit_bytes=VMEM_LIMIT),
        cost_estimate=LIGHT,
        name="grad_normed",
    )(grad_qkv, w_qkv)


def gather_kernel(place_ref, one_own, one_other, two_own, two_other, qkv_ref, out_ref):
    step = pl.program_id(0)
    swap = place_ref[0] == 1
    rows = one_own.shape[0]

    def whole(own_ref, other_ref, target):
        own, other = own_ref[...], other_ref[...]
        target[:rows] = jnp.where(swap, other, own).astype(jnp.float32)
        target[rows:] = jnp.where(swap, own, other).astype(jnp.float32)

    @pl.when(step < 4)
    def _():
        whole(one_own, one_other, qkv_ref)

    @pl.when((step >= 4) & (step < 6))
    def _():
        whole(two_own, two_other, qkv_ref)

    @pl.when(step >= 6)
    def _():
        whole(two_own, two_other, out_ref)


def gather_halves(place, one, two):
    rows = one[0].shape[0]
    left = pl.BlockSpec((rows, 512), lambda j: (0, jnp.minimum(j, 3)))
    right = pl.BlockSpec((rows, 512), lambda j: (0, jnp.maximum(j - 4, 0)))
    return pl.pallas_call(
        gather_kernel,
        grid=(8,),
        in_specs=[pl.BlockSpec(memory_space=pltpu.SMEM), left, left, right, right],
        out_specs=[
            pl.BlockSpec((2 * rows, 512), lambda j: (0, jnp.minimum(j, 5))),
            pl.BlockSpec((2 * rows, 512), lambda j: (0, jnp.maximum(j - 6, 0))),
        ],
        out_shape=[
            jax.ShapeDtypeStruct((2 * rows, 3 * D), jnp.float32),
            jax.ShapeDtypeStruct((2 * rows, D), jnp.float32),
        ],
        compiler_params=pltpu.CompilerParams(vmem_limit_bytes=VMEM_LIMIT),
        cost_estimate=LIGHT,
        name="gather_halves",
    )(place, *one, *two)


def project_kernel(tok_ref, gain_ref, w_ref, normed_ref, qkv_ref):
    @pl.when(pl.program_id(0) == 0)
    def _():
        values = tok_ref[...].astype(jnp.float32)
        scale = lax.rsqrt(jnp.mean(values * values, axis=-1, keepdims=True) + EPSILON)
        normed_ref[...] = (values * scale * gain_ref[...]).astype(jnp.bfloat16)

    qkv_ref[...] = dot_nn(normed_ref[...], w_ref[...]).astype(jnp.bfloat16)


def project(tokens, gain, w_qkv):
    count, width = tokens.shape[0], w_qkv.shape[1]
    once = pl.Buffered(1)
    return pl.pallas_call(
        project_kernel,
        grid=(width // 512,),
        in_specs=[
            pl.BlockSpec((count, D), lambda j: (0, 0), pipeline_mode=once),
            pl.BlockSpec((1, D), lambda j: (0, 0), pipeline_mode=once),
            pl.BlockSpec((D, 512), lambda j: (0, j)),
        ],
        out_specs=[
            pl.BlockSpec((count, D), lambda j: (0, 0), pipeline_mode=once),
            pl.BlockSpec((count, 512), lambda j: (0, j)),
        ],
        out_shape=[low_shape(count, D), low_shape(count, width)],
        compiler_params=pltpu.CompilerParams(vmem_limit_bytes=VMEM_LIMIT),
        cost_estimate=LIGHT,
        name="project",
    )(tokens, gain[None], w_qkv)


OUTER = 4


def rms_forward(values, gain):
    scale_rows = lax.rsqrt(jnp.mean(values * values, axis=-1, keepdims=True) + EPSILON)
    return (values * scale_rows * gain, scale_rows)


def rms_backward(values, scale_rows, gain, upstream):
    scaled_grad = upstream * gain
    gain_grad = jnp.sum(upstream * values * scale_rows, axis=0)
    inner_mean = jnp.mean(scaled_grad * values, axis=-1, keepdims=True)
    return (scale_rows * scaled_grad - values * scale_rows**3 * inner_mean, gain_grad)


def tie(*arrays):
    return lax.optimization_barrier(arrays)


def to_sibling(x):
    groups = lax.axis_size("ep")
    return lax.ppermute(x, "ep", [(e, e ^ 1) for e in range(groups)])


def from_chip(x, away, cross=0):
    groups = lax.axis_size("ep")
    return lax.ppermute(x, "ep", [(e, ((e - 2 * away) % groups) ^ cross) for e in range(groups)])


def core_pairs(step):
    return [(e, e ^ 1) for e in range(lax.axis_size("ep"))]


def chip_pairs(step):
    groups = lax.axis_size("ep")
    return [(e, (e + 2 * step) % groups) for e in range(groups)]


def inner_pairs(step):
    replicas = lax.axis_size("rep")
    inner = replicas // OUTER
    return [(r, r - r % inner + (r + step) % inner) for r in range(replicas)]


def outer_pairs(step):
    replicas = lax.axis_size("rep")
    return [(r, (r + step * (replicas // OUTER)) % replicas) for r in range(replicas)]


def levels():
    ep, rep = lax.axis_index("ep"), lax.axis_index("rep")
    inner = lax.axis_size("rep") // OUTER
    return (
        ("ep", 2, ep % 2, core_pairs),
        ("ep", lax.axis_size("ep") // 2, ep // 2, chip_pairs),
        ("rep", inner, rep % inner, inner_pairs),
        ("rep", OUTER, rep // inner, outer_pairs),
    )


def swapped(x, level, steps=None):
    axis, size, place, pairs = level
    out = [] if steps else [lax.dynamic_index_in_dim(x, place, 0, keepdims=False)]
    for step in steps or range(1, size):
        sent = lax.dynamic_index_in_dim(x, (place + step) % size, 0, keepdims=False)
        out.append(lax.ppermute(sent, axis, pairs(step)))
    return out


def sides_swapped(sides, level):
    axis, size, place, pairs = level
    return [sides[0]] + [lax.ppermute(sides[step], axis, pairs(step)) for step in range(1, size)]


def whole_swapped(x, level):
    axis, size, place, pairs = level
    return [x] + [lax.ppermute(x, axis, pairs(step)) for step in range(1, size)]


def total(arrays):
    return sum([x.astype(jnp.float32) for x in arrays[1:]], arrays[0].astype(jnp.float32))


def low_total(arrays):
    return total(arrays).astype(arrays[0].dtype)


def collected(x, level):
    axis, size, place, pairs = level
    if size == 2:
        other = lax.ppermute(x, axis, pairs(1))
        return jnp.concatenate([jnp.where(place == 0, x, other), jnp.where(place == 0, other, x)])
    out = lax.dynamic_update_index_in_dim(jnp.zeros((size, *x.shape), x.dtype), x, place, 0)
    for step in range(1, size):
        other = lax.ppermute(x, axis, pairs(step))
        out = lax.dynamic_update_index_in_dim(out, other, (place - step) % size, 0)
    return out.reshape(-1, *x.shape[1:])


def rows_swapped(x, level):
    return swapped(x.reshape(level[1], -1, x.shape[1]), level)


def near_swapped(x):
    replicas = lax.axis_size("rep")
    blocks = x.reshape(OUTER, replicas // OUTER, x.shape[0] // replicas, x.shape[1])
    return swapped(jnp.swapaxes(blocks, 0, 1), levels()[2])


def slot_table(expert_ids, priority, experts, capacity):
    ranks = priority.reshape(-1, 2)
    names = jnp.arange(experts, dtype=jnp.int32)[:, None]
    first, second = expert_ids[:, 0][None, :] == names, expert_ids[:, 1][None, :] == names
    rank = jnp.where(first, ranks[:, 0][None, :], jnp.where(second, ranks[:, 1][None, :], 1 << 20))
    slot = jnp.sum((rank[:, :, None] < rank[:, None, :]).astype(jnp.int32), axis=1)
    return jnp.where((first | second) & (slot < capacity), slot, -1)


def per_device(
    tokens,
    cotangent,
    gain_attn,
    w_qkv,
    w_out,
    rel_table,
    gain_moe,
    w_router,
    w_gate,
    w_up,
    w_down,
    expert_ids,
    priority,
    span_starts,
):
    tok_count = tokens.shape[0]
    experts = w_router.shape[1]
    groups = lax.axis_size("ep")
    chips = groups // 2
    capacity = 5 * tok_count // (2 * experts)
    own = lax.axis_index("ep")

    slots = slot_table(expert_ids, priority, experts, capacity)
    ids = jnp.transpose(expert_ids)
    table = jnp.concatenate([slots, ids], axis=0)
    info = [(table, to_sibling(table))] + [(from_chip(table, n), from_chip(table, n, 1)) for n in range(1, chips)]
    cot_sib = to_sibling(cotangent)
    cot_far = [from_chip(cotangent, n) for n in range(1, chips)]
    metas = []
    for pair in info:
        rows = []
        for table in pair:
            slot = lax.dynamic_slice_in_dim(table, own, 1, axis=0)
            one, two = table[experts : experts + 1], table[experts + 1 :]
            other = jnp.where(one == own, two, one)
            rows.append(jnp.concatenate([slot, other, jnp.full((6, tok_count), 1, jnp.int32) * own], axis=0))
        metas.append(jnp.stack(rows))

    diag = wide_diag(rel_table)
    token_float = tokens.astype(jnp.float32)
    normed_low, qkv = project(tokens, gain_attn, w_qkv)
    attended_low, lse = attn_fwd(span_starts, qkv, diag)
    attended_low, cot_sib, cot_far, metas = tie(attended_low, cot_sib, cot_far, metas)
    mixed = token_float + jnp.dot(attended_low, w_out, preferred_element_type=jnp.float32)
    routed, scale_moe = rms_forward(mixed, gain_moe)
    routed_low = routed.astype(jnp.bfloat16)
    logits = jnp.dot(routed_low, w_router, preferred_element_type=jnp.float32)
    choose = expert_ids[:, :, None] == jnp.arange(experts, dtype=jnp.int32)[None, None, :]
    chosen = jnp.sum(jnp.where(choose, logits[:, None, :], 0.0), axis=-1)
    gates = jax.nn.softmax(chosen, axis=-1)

    router_rows = jnp.zeros((8, D), jnp.bfloat16).at[:experts].set(jnp.transpose(w_router))
    weights = (w_gate, w_up, w_down)
    core, chip, inner, outer = levels()

    tok_far = [from_chip(routed_low, n) for n in range(1, chips)]
    cots = [(cotangent, cot_sib)] + [(far, to_sibling(far)) for far in cot_far]
    pair = (routed_low, to_sibling(routed_low))
    made = expert_fwd(0, capacity, metas[0], router_rows, pair, cots[0], *weights)
    made, tok_far, cots = tie(made, tok_far, cots)
    toks = [(far, to_sibling(far)) for far in tok_far]
    outs, dots = [made[5:7]], [(made[7][0], made[7][1])]
    kept = [made[:5]]
    for away in range(1, chips):
        made = expert_fwd(away, capacity, metas[away], router_rows, toks[away - 1], cots[away], *weights)
        kept.append(made[:5])
        outs.append(made[5:7])
        dots.append((made[7][0], made[7][1]))
    rows_in, rows_out, hidden, slope, act = [list(x) for x in zip(*kept)]

    met = [[to_sibling(other) for mine, other in part] for part in (dots, outs)]
    down_low = grad_down(rows_out, hidden)
    down_low, slope, met, dots, outs = tie(down_low, slope, met, dots, outs)
    dots, outs = [
        [total([mine[n][0], got[n]]) for n in range(chips)] for mine, got in zip((dots, outs), met)
    ]
    outs_low = [x.astype(jnp.bfloat16) for x in outs[1:]]
    slope, outs_low, down_low = tie(slope, outs_low, down_low)
    far_outs = [from_chip(x, chips - 1 - n) for n, x in enumerate(outs_low)]
    far_dots = [from_chip(x, chips - 1 - n) for n, x in enumerate(dots[1:])]
    down_near = near_swapped(down_low)
    grads = [None] * chips
    for away in reversed(range(1, chips)):
        slope[away], act[away], *grads[away] = expert_bwd(
            away, capacity, metas[away], rows_out[away], slope[away], act[away], *weights
        )
    slope, far_outs, far_dots = tie(slope, far_outs, far_dots)
    far_grads = []
    for away in range(1, chips):
        far_grads += [from_chip(grads[away][0], chips - away), from_chip(grads[away][1], chips - away, 1)]
    slope[0], act[0], *here = expert_bwd(0, capacity, metas[0], rows_out[0], slope[0], act[0], *weights)
    slope, down_near = tie(slope, down_near)
    down_near = low_total(down_near)
    slope, down_near = tie(slope, down_near)
    near_grads = to_sibling(here[1])
    down_far = swapped(down_near, outer)
    gate_low, up_low = grad_in(
        jnp.reshape(inner[2], (1,)), inner[1], lax.axis_size("rep"), rows_in, slope, act
    )
    gate_low, up_low, far_grads, near_grads = tie(gate_low, up_low, far_grads, near_grads)
    grad_pairs = total([here[0], near_grads] + far_grads)
    grad_gates_all = total([dots[0]] + far_dots)
    block_out = (mixed + total([outs[0]] + far_outs)).astype(jnp.bfloat16)
    gate_near = sides_swapped(gate_low, inner)

    grad_out = cotangent.astype(jnp.float32)
    by_token = jnp.transpose(grad_gates_all[:experts])
    grad_gates = jnp.sum(jnp.where(choose, by_token[:, None, :], 0.0), axis=-1)
    grad_chosen = gates * (grad_gates - jnp.sum(gates * grad_gates, axis=-1, keepdims=True))
    grad_logits = jnp.sum(jnp.where(choose, grad_chosen[:, :, None], 0.0), axis=1).astype(jnp.bfloat16)
    grad_routed = grad_pairs + jnp.einsum(
        "te,de->td", grad_logits, w_router, preferred_element_type=jnp.float32
    )
    grad_norm_moe, grad_gain_moe = rms_backward(mixed, scale_moe, gain_moe, grad_routed)
    grad_mixed = grad_out + grad_norm_moe
    grad_branch = grad_mixed.astype(jnp.bfloat16)
    grad_attended = jnp.einsum(
        "te,de->td", grad_branch, w_out, preferred_element_type=jnp.float32
    ).astype(jnp.bfloat16)

    grad_attended, grad_branch = tie(grad_attended, grad_branch)
    quarters = [None] * 4
    made = None

    def backward(part, grad, made):
        return attn_bwd(span_starts, qkv, grad, attended_low, lse, diag, part, made)

    for part in (0, 1):
        made, *quarters[part] = backward(part, grad_attended, made)
    made, grad_attended, gate_near, down_far, up_low = tie(
        made, grad_attended, gate_near, down_far, up_low
    )
    gate_near = low_total(gate_near)
    gate_near, grad_attended, up_low = tie(gate_near, grad_attended, up_low)
    gate_far = swapped(gate_near, outer)
    up_near = sides_swapped(up_low, inner)
    for part in (2, 3):
        made, *quarters[part] = backward(part, grad_attended, made)
    mine, other = grad_attn(jnp.reshape(core[2], (1,)), normed_low, attended_low, made, grad_branch)
    grad_normed = grad_normed_of(made, w_qkv)
    mine, other, grad_normed, gate_far, up_near = tie(mine, other, grad_normed, gate_far, up_near)
    up_near, other = tie(low_total(up_near), other)
    other = to_sibling(other)
    up_far = swapped(up_near, outer)
    both = low_total([mine, other])
    cut = both.shape[1] // 2
    one, two, quarters, late = tie(both[:, :cut], both[:, cut:], quarters, (routed_low, grad_logits))
    grad_w_router = jnp.einsum("td,te->de", *late, preferred_element_type=jnp.float32)
    one, two = rows_swapped(one, chip), rows_swapped(two, inner)
    scale_attn = lax.rsqrt(jnp.mean(token_float * token_float, axis=-1, keepdims=True) + EPSILON)
    grad_norm_attn, grad_gain_attn = rms_backward(token_float, scale_attn, gain_attn, grad_normed)
    grad_tokens = grad_mixed + grad_norm_attn
    grad_rel_table = rel_grad(
        jnp.concatenate([x[0] for x in quarters]), jnp.concatenate([x[1] for x in quarters])
    )
    small = jnp.concatenate(
        [
            jnp.transpose(grad_w_router),
            jnp.pad(grad_rel_table.reshape(1, -1), ((0, 0), (0, D - BUCKETS * H))),
            grad_gain_attn[None],
            grad_gain_moe[None],
        ]
    )
    one, two, small, grad_tokens = tie(one, two, small, grad_tokens)
    one, two = tie(low_total(one), low_total(two))
    one, two, up_far = tie(rows_swapped(one, inner), rows_swapped(two, chip), up_far)
    both = jnp.concatenate([low_total(one), low_total(two)], axis=1)
    both, small = tie(rows_swapped(both, outer), whole_swapped(small, core))
    both, small = tie(low_total(both), total(small))
    both, small = tie(collected(both, outer), whole_swapped(small, chip))
    one, two, small = tie(both[:, :cut], both[:, cut:], total(small))
    one, two, small = tie(collected(one, inner), collected(two, chip), whole_swapped(small, inner))
    small = whole_swapped(total(small), outer)
    one, two, small = tie(collected(one, chip), collected(two, inner), small)
    one, two = (one, to_sibling(one)), (two, to_sibling(two))
    sum_w_qkv, sum_w_out = gather_halves(jnp.reshape(core[2], (1,)), one, two)
    small = total(small)
    sum_down = total(down_far)
    sum_gate, sum_up = total(gate_far), total(up_far)
    small = (
        small[experts, : BUCKETS * H].reshape(BUCKETS, H),
        jnp.transpose(small[:experts]),
        small[experts + 1],
        small[experts + 2],
    )
    return (
        block_out,
        grad_tokens,
        small[2],
        sum_w_qkv,
        sum_w_out,
        small[0],
        small[3],
        small[1],
        sum_gate[None],
        sum_up[None],
        sum_down[None],
    )


def solution(mesh):
    placed = (
        P(("rep", "ep"), None),
        P(("rep", "ep"), None),
        P(),
        P(),
        P(),
        P(),
        P(),
        P(),
        P("ep", None, None),
        P("ep", None, None),
        P("ep", None, None),
        P(("rep", "ep"), None),
        P(("rep", "ep"), None),
        P(("rep", "ep"), None),
    )
    return jax.shard_map(
        per_device,
        mesh=mesh,
        in_specs=placed,
        out_specs=(
            P(("rep", "ep"), None),
            P(("rep", "ep"), None),
            P(),
            P(),
            P(),
            P(),
            P(),
            P(),
            P("ep", "rep", None),
            P("ep", "rep", None),
            P("ep", "rep", None),
        ),
        check_vma=False,
    )
```

```python
from functools import partial
import jax
import jax.numpy as jnp
import numpy as np
from jax import lax
from jax.sharding import PartitionSpec as P
from jax.experimental import pallas as pl
from jax.experimental.pallas import tpu as pltpu

D = 1024
H = 16
HD = 64
BUCKETS = 32
MAXDIST = 128
SEQ = 1024
PIC = 256
EPSILON = 1e-06
NEGATIVE = -1e30
LOG2E = 1.4426950408889634
QB = 256
KB = 128
WIDE = 768
VMEM_LIMIT = 56 * 1024 * 1024
LIGHT = pl.CostEstimate(flops=1000, bytes_accessed=1000, transcendentals=0)


def bucket_of(offsets):
    half_count = BUCKETS // 2
    near_count = half_count // 2
    upper_part = (offsets > 0).astype(np.int64) * half_count
    distance = np.abs(offsets)
    ratio = np.log(np.maximum(distance, 1) / near_count) / np.log(MAXDIST / near_count)
    distant_bucket = np.minimum(
        near_count + np.floor(ratio * (half_count - near_count)).astype(np.int64), half_count - 1
    )
    return upper_part + np.where(distance < near_count, distance, distant_bucket)


def wide_onehot():
    places = np.arange(WIDE)
    offsets = np.where(places < 640, 256 - places, 1024 - places)
    return (bucket_of(offsets)[:, None] == np.arange(BUCKETS)[None, :]).astype(np.float32)


def dot_nt(a, b):
    return lax.dot_general(a, b, (((1,), (1,)), ((), ())), preferred_element_type=jnp.float32)


def dot_nn(a, b):
    return lax.dot_general(a, b, (((1,), (0,)), ((), ())), preferred_element_type=jnp.float32)


def key_count(i):
    return min((i + 2) * QB, SEQ)


def fill_mask(span_ref, mask_s):
    for i in range(SEQ // QB):
        for d in range(4):
            if 2 * i + d >= SEQ // KB:
                continue
            k = (2 * i + d) * KB + lax.broadcasted_iota(jnp.int32, (KB, QB), 0)
            q = i * QB + lax.broadcasted_iota(jnp.int32, (KB, QB), 1)
            ok = k <= q
            for s in range(2):
                start = span_ref[0, s]
                ok = ok | ((k >= start) & (k < start + PIC) & (q >= start) & (q < start + PIC))
            mask_s[4 * i + d] = jnp.where(ok, 0.0, NEGATIVE)


def spread_bias(diag_ref, h, bias_s):
    row = jnp.broadcast_to(diag_ref[0, h : h + 1, :], (KB, WIDE))
    bias_s[h] = pltpu.roll(row, 0, 1, stride=1, stride_axis=0)


def shifted(s, i, kt, h, bias_s, mask_s, low, high, row):
    d = kt - 2 * i
    if d <= -2:
        return s + (low if row is None else low + row)
    if d >= 3:
        s = s + (high if row is None else high + row)
    else:
        s = s + bias_s[h, :, (2 - d) * 128 : (2 - d) * 128 + 256]
        if row is not None:
            s = s + row
    if d >= 0:
        s = s + mask_s[4 * i + d]
    return s


def diagonal_sums(x):
    rows = x.shape[0]
    while rows > 8:
        rows //= 2
        x = x[:rows] + pltpu.roll(x[rows:], WIDE - rows, 1)
    total = x[0:1]
    for r in range(1, rows):
        total = total + pltpu.roll(x[r : r + 1], WIDE - r, 1)
    return total


def half_lanes(x, h):
    lane = lax.broadcasted_iota(jnp.int32, x.shape, 1)
    return jnp.where((lane < HD) if h == 0 else (lane >= HD), x, jnp.zeros_like(x))


def both_halves(ref, i):
    rows = ref[i * QB : (i + 1) * QB, :]
    return jnp.concatenate([half_lanes(rows, h) for h in range(2)], axis=0)


def attn_fwd_kernel(span_ref, q_ref, k_ref, v_ref, diag_ref, out_ref, lse_ref, mask_s, bias_s, vt_s, s_s, p_s):
    @pl.when(pl.program_id(0) == 0)
    def _():
        fill_mask(span_ref, mask_s)

    vt_s[:128] = jnp.transpose(v_ref[...])
    vt_s[128:] = jnp.ones((16, SEQ), jnp.bfloat16)
    for h in range(2):
        spread_bias(diag_ref, h, bias_s)
    scale = LOG2E * HD ** (-0.5)
    blocks = SEQ // QB

    def products(i):
        s_s[i % 2, : key_count(i)] = dot_nt(k_ref[: key_count(i), :], both_halves(q_ref, i))

    products(0)
    for i in range(blocks):
        nk = key_count(i)
        if i + 1 < blocks:
            products(i + 1)
        tops = []
        for h in range(2):
            low = diag_ref[0, h : h + 1, 600:601]
            high = diag_ref[0, h : h + 1, 0:1]
            cols = slice(h * QB, (h + 1) * QB)
            top = None
            for kt in range(nk // KB):
                tile = slice(kt * KB, (kt + 1) * KB)
                s = shifted(s_s[i % 2, tile, cols] * scale, i, kt, h, bias_s, mask_s, low, high, None)
                s_s[i % 2, tile, cols] = s
                t = jnp.max(s.reshape(KB // 8, 8, QB), axis=0)
                top = t if top is None else jnp.maximum(top, t)
            m = jnp.max(top, axis=0, keepdims=True)
            tops.append(m)
            for kt in range(nk // KB):
                tile = slice(kt * KB, (kt + 1) * KB)
                p_s[i % 2, tile, cols] = jnp.exp2(s_s[i % 2, tile, cols] - m).astype(jnp.bfloat16)
        ot = dot_nn(vt_s[:, :nk], p_s[i % 2, :nk])
        outs = []
        for h in range(2):
            cols = slice(h * QB, (h + 1) * QB)
            total = ot[128:129, cols]
            outs.append(ot[h * HD : (h + 1) * HD, cols] / total)
            lse_ref[0, h : h + 1, i * QB : (i + 1) * QB] = tops[h] + jnp.log2(total)
        out_ref[i * QB : (i + 1) * QB, :] = jnp.transpose(jnp.concatenate(outs, axis=0)).astype(jnp.bfloat16)


def attn_fwd(spans, qkv, diag):
    col = lambda off: pl.BlockSpec((SEQ, 128), lambda g: (0, g + off))
    return pl.pallas_call(
        attn_fwd_kernel,
        grid=(H // 2,),
        in_specs=[
            pl.BlockSpec(memory_space=pltpu.SMEM),
            col(0),
            col(8),
            col(16),
            pl.BlockSpec((1, 2, WIDE), lambda g: (g, 0, 0)),
        ],
        out_specs=[col(0), pl.BlockSpec((1, 2, SEQ), lambda g: (g, 0, 0))],
        out_shape=[
            jax.ShapeDtypeStruct((SEQ, D), jnp.bfloat16),
            jax.ShapeDtypeStruct((H // 2, 2, SEQ), jnp.float32),
        ],
        scratch_shapes=[
            pltpu.VMEM((16, KB, QB), jnp.float32),
            pltpu.VMEM((2, KB, WIDE), jnp.float32),
            pltpu.VMEM((128 + 16, SEQ), jnp.bfloat16),
            pltpu.VMEM((2, SEQ, 2 * QB), jnp.float32),
            pltpu.VMEM((2, SEQ, 2 * QB), jnp.bfloat16),
        ],
        compiler_params=pltpu.CompilerParams(vmem_limit_bytes=VMEM_LIMIT),
        cost_estimate=LIGHT,
        name="attn_fwd",
    )(spans, qkv, qkv, qkv, diag)


def attn_bwd_kernel(
    span_ref, q_ref, k_ref, v_ref, g_ref, o_ref, lse_ref, diag_ref, *rest
):
    (
        out_ref, drel_ref, far_ref,
        mask_s, bias_s, acc_s, kt_s, s_s, dp_s, p_s, ds_s, dk_s, dv_s, delta_s,
    ) = rest[-14:]
    part = pl.program_id(1)

    @pl.when((pl.program_id(0) == 0) & (part == 0))
    def _():
        fill_mask(span_ref, mask_s)

    @pl.when(part == 1)
    def _():
        out_ref[...] = (dk_s[...] * HD ** (-0.5)).astype(jnp.bfloat16)

    @pl.when(part == 2)
    def _():
        out_ref[...] = dv_s[...].astype(jnp.bfloat16)

    @pl.when(part == 0)
    def _():
        kt_s[...] = jnp.transpose(k_ref[...])
        prod = jnp.transpose(g_ref[...].astype(jnp.float32) * o_ref[...].astype(jnp.float32))
        for h in range(2):
            spread_bias(diag_ref, h, bias_s)
            delta_s[h : h + 1] = jnp.sum(prod[h * HD : (h + 1) * HD], axis=0, keepdims=True)
        acc_s[...] = jnp.zeros_like(acc_s)
        far_ref[...] = jnp.zeros_like(far_ref)
        scale = LOG2E * HD ** (-0.5)
        blocks = SEQ // QB

        def products(i):
            nk = key_count(i)
            s_s[i % 2, :nk] = dot_nt(k_ref[:nk, :], both_halves(q_ref, i))
            dp_s[i % 2, :nk] = dot_nt(v_ref[:nk, :], both_halves(g_ref, i))

        products(blocks - 1)
        for i in reversed(range(blocks)):
            nk = key_count(i)
            rows = slice(i * QB, (i + 1) * QB)
            if i > 0:
                products(i - 1)
            for h in range(2):
                low = diag_ref[0, h : h + 1, 600:601]
                high = diag_ref[0, h : h + 1, 0:1]
                nlse = -lse_ref[0, h : h + 1, rows]
                delta = delta_s[h : h + 1, rows]
                cols = slice(h * QB, (h + 1) * QB)
                for kt in range(nk // KB):
                    tile = slice(kt * KB, (kt + 1) * KB)
                    d = kt - 2 * i
                    s = s_s[i % 2, tile, cols] * scale
                    p = jnp.exp2(shifted(s, i, kt, h, bias_s, mask_s, low, high, nlse))
                    ds = p * (dp_s[i % 2, tile, cols] - delta)
                    p_s[i % 2, tile, cols] = p.astype(jnp.bfloat16)
                    ds_s[i % 2, tile, cols] = ds.astype(jnp.bfloat16)
                    if -1 <= d <= 2:
                        near = slice((2 - d) * 128, (2 - d) * 128 + 256)
                        acc_s[h, :, near] += ds
                    else:
                        far_ref[0, h, 0 if d < 0 else 1] += jnp.sum(ds.reshape(KB // 8, 8, QB), axis=0)
            dq = dot_nn(kt_s[:, :nk], ds_s[i % 2, :nk])
            dq = jnp.concatenate([dq[h * HD : (h + 1) * HD, h * QB : (h + 1) * QB] for h in range(2)], axis=0)
            out_ref[rows, :] = (jnp.transpose(dq) * HD ** (-0.5)).astype(jnp.bfloat16)
            dv = dot_nn(p_s[i % 2, :nk], both_halves(g_ref, i))
            dk = dot_nn(ds_s[i % 2, :nk], both_halves(q_ref, i))
            if i == blocks - 1:
                dv_s[...] = dv
                dk_s[...] = dk
            else:
                dv_s[:nk] += dv
                dk_s[:nk] += dk
        for h in range(2):
            drel_ref[0, h : h + 1, :] = diagonal_sums(acc_s[h])


def attn_bwd(spans, qkv, grad_att, att, lse, diag, part, buffer):
    buffers = () if buffer is None else (buffer,)
    pairs = H // 8
    base = part * pairs
    col = lambda off: pl.BlockSpec((SEQ, 128), lambda g, p: (0, base + g + off))
    one = lambda *dims: pl.BlockSpec((1, *dims), lambda g, p: (base + g,) + (0,) * len(dims))
    new = lambda *dims: pl.BlockSpec((1, *dims), lambda g, p: (g,) + (0,) * len(dims))
    return pl.pallas_call(
        attn_bwd_kernel,
        grid=(pairs, 3),
        in_specs=[
            pl.BlockSpec(memory_space=pltpu.SMEM),
            col(0),
            col(8),
            col(16),
            col(0),
            col(0),
            one(2, SEQ),
            one(2, WIDE),
        ]
        + [pl.BlockSpec(memory_space=pl.ANY)] * len(buffers),
        out_specs=[
            pl.BlockSpec((SEQ, 128), lambda g, p: (0, p * (H // 2) + base + g)),
            new(2, WIDE),
            new(2, 2, 8, QB),
        ],
        out_shape=[
            jax.ShapeDtypeStruct((SEQ, 3 * D), jnp.bfloat16),
            jax.ShapeDtypeStruct((pairs, 2, WIDE), jnp.float32),
            jax.ShapeDtypeStruct((pairs, 2, 2, 8, QB), jnp.float32),
        ],
        scratch_shapes=[
            pltpu.VMEM((16, KB, QB), jnp.float32),
            pltpu.VMEM((2, KB, WIDE), jnp.float32),
            pltpu.VMEM((2, KB, WIDE), jnp.float32),
            pltpu.VMEM((128, SEQ), jnp.bfloat16),
            pltpu.VMEM((2, SEQ, 2 * QB), jnp.float32),
            pltpu.VMEM((2, SEQ, 2 * QB), jnp.float32),
            pltpu.VMEM((2, SEQ, 2 * QB), jnp.bfloat16),
            pltpu.VMEM((2, SEQ, 2 * QB), jnp.bfloat16),
            pltpu.VMEM((SEQ, 128), jnp.float32),
            pltpu.VMEM((SEQ, 128), jnp.float32),
            pltpu.VMEM((2, SEQ), jnp.float32),
        ],
        input_output_aliases={8: 0} if buffers else {},
        compiler_params=pltpu.CompilerParams(vmem_limit_bytes=VMEM_LIMIT),
        cost_estimate=LIGHT,
        name=f"attn_bwd_{part}",
    )(spans, qkv, qkv, qkv, grad_att, att, lse, diag, *buffers)


def wide_diag(rel_table):
    return jnp.einsum(
        "mb,bh->hm", jnp.asarray(wide_onehot()), rel_table * LOG2E, precision=lax.Precision.HIGHEST
    ).reshape(H // 2, 2, WIDE)


def rel_grad(drel, far):
    sums = drel.reshape(H, WIDE)
    far = jnp.sum(far.reshape(H, 2, 8 * QB), axis=-1)
    sums = sums.at[:, 600].add(far[:, 0]).at[:, 0].add(far[:, 1])
    return jnp.einsum("mb,hm->bh", jnp.asarray(wide_onehot()), sums, precision=lax.Precision.HIGHEST)


FT = 256


def dot_tn(a, b):
    return lax.dot_general(a, b, (((0,), (0,)), ((), ())), preferred_element_type=jnp.float32)


VMEM_MOST = 58 * 1024 * 1024
PARTS = 1


def slot_onehot(meta_ref, n, rows):
    slot = meta_ref[n, 0:1]
    return lax.broadcasted_iota(jnp.int32, (rows, slot.shape[1]), 0) == slot


def expert_fwd_kernel(meta_ref, wr_ref, tok_a, tok_b, cot_a, cot_b, gate_ref, up_ref, down_ref, *rest):
    x_ref, gc_ref, hid_ref, slope_ref, act_ref, p_a, p_b, gg_ref, hot_s, turned_s, hid_s, gate_s = rest[-12:]
    step = pl.program_id(0)
    wide = hid_s.shape[1] // FT
    deep = D // FT
    rows = x_ref.shape[0] // 2
    count = tok_a.shape[0]
    pair = [(0, tok_a, cot_a, slice(0, rows)), (1, tok_b, cot_b, slice(rows, 2 * rows))]
    chunk = 2 * rows // PARTS

    @pl.when(step == 0)
    def _():
        for n, tok_ref, cot_ref, here in pair:
            logits = dot_nt(wr_ref[...], tok_ref[...])
            other, own = meta_ref[n, 1:2], meta_ref[n, 2:3]
            names = lax.broadcasted_iota(jnp.int32, logits.shape, 0)
            mine = jnp.sum(jnp.where(names == own, logits, 0.0), axis=0, keepdims=True)
            theirs = jnp.sum(jnp.where(names == other, logits, 0.0), axis=0, keepdims=True)
            gate = 1.0 / (1.0 + jnp.exp(theirs - mine))
            hot = slot_onehot(meta_ref, n, rows)
            gates = jnp.sum(jnp.where(hot, gate, 0.0), axis=1, keepdims=True)
            lane = lax.broadcasted_iota(jnp.int32, (rows, 128), 1)
            gate_s[here] = jnp.where(lane < 64, gates, 0.0)
            hot = jnp.where(hot, 1.0, 0.0).astype(jnp.bfloat16)
            hot_s[n] = hot
            turned_s[n] = jnp.transpose(hot)
            x_ref[here] = dot_nn(hot_s[n], tok_ref[...]).astype(jnp.bfloat16)

    @pl.when(step < wide)
    def _():
        cols = pl.ds(pl.multiple_of(step * FT, FT), FT)
        root = (2.0 / np.pi) ** 0.5
        for c in range(PARTS):
            here = slice(c * chunk, (c + 1) * chunk)
            g = dot_nn(x_ref[here], gate_ref[0])
            u = dot_nn(x_ref[here], up_ref[0])
            square = g * g
            t = jnp.tanh(g * (root + (root * 0.044715) * square))
            half = 0.5 + 0.5 * t
            act = g * half
            slope = half + (act * (1.0 - t)) * (root + (3.0 * root * 0.044715) * square)
            slope_ref[here] = (u * slope).astype(jnp.bfloat16)
            act_ref[here] = act.astype(jnp.bfloat16)
            hidden = (act * u).astype(jnp.bfloat16)
            hid_s[here, cols] = hidden
            hid_ref[here] = hidden

    @pl.when(step >= wide)
    def _():
        cols = pl.ds(pl.multiple_of((step - wide) * FT, FT), FT)
        outs = dot_nn(hid_s[...], down_ref[0])
        for s, tok_ref, cot_ref, here in pair:
            gates = gate_s[here, 0:1]
            out = outs[here].astype(jnp.bfloat16).astype(jnp.float32)
            cot = dot_nn(hot_s[s], cot_ref[...])
            lane = lax.broadcasted_iota(jnp.int32, (rows, 128), 1)
            gate_s[here] += jnp.where(lane < 64, 0.0, jnp.sum(out * cot, axis=1, keepdims=True))
            gc_ref[here, cols] = (gates * cot).astype(jnp.bfloat16)
            p_ref = (p_a, p_b)[s]
            p_ref[...] = dot_nn(turned_s[s], (gates * out).astype(jnp.bfloat16)).astype(jnp.bfloat16)

    @pl.when(step == wide + deep - 1)
    def _():
        for s, tok_ref, cot_ref, here in pair:
            gg = jnp.where(slot_onehot(meta_ref, s, rows), gate_s[here, 64:65], 0.0)
            gg = jnp.sum(gg, axis=0, keepdims=True)
            own = meta_ref[s, 2:3]
            gg_ref[s] = jnp.where(lax.broadcasted_iota(jnp.int32, (8, count), 0) == own, gg, 0.0)


def expert_bwd_kernel(meta_ref, gc_ref, slope_ref, act_ref, down_ref, gate_ref, up_ref, dg_ref, du_ref, dp_a, dp_b, turned_s, dg_s, du_s):
    step = pl.program_id(0)
    wide = dg_s.shape[1] // FT
    rows = gc_ref.shape[0] // 2

    @pl.when(step == 0)
    def _():
        for n in range(2):
            hot = jnp.where(slot_onehot(meta_ref, n, rows), 1.0, 0.0).astype(jnp.bfloat16)
            turned_s[n] = jnp.transpose(hot)

    @pl.when(step < wide)
    def _():
        cols = pl.ds(pl.multiple_of(step * FT, FT), FT)
        dh = dot_nt(gc_ref[...], down_ref[0])
        dg = (dh * slope_ref[...].astype(jnp.float32)).astype(jnp.bfloat16)
        du = (dh * act_ref[...].astype(jnp.float32)).astype(jnp.bfloat16)
        dg_s[:, cols] = dg
        du_s[:, cols] = du
        dg_ref[...] = dg
        du_ref[...] = du

    @pl.when(step >= wide)
    def _():
        dx = (dot_nt(dg_s[...], gate_ref[0]) + dot_nt(du_s[...], up_ref[0])).astype(jnp.bfloat16)
        for s in range(2):
            dp_ref = (dp_a, dp_b)[s]
            dp_ref[...] = dot_nn(turned_s[s], dx[s * rows : (s + 1) * rows]).astype(jnp.bfloat16)


def low_shape(*shape):
    return jax.ShapeDtypeStruct(shape, jnp.bfloat16)


def expert_fwd(place, rows, meta, router_rows, toks, cots, w_gate, w_up, w_down):
    count = toks[0].shape[0]
    width = w_gate.shape[2]
    wide = width // FT
    deep = D // FT
    once = pl.Buffered(1)
    whole = lambda *shape: pl.BlockSpec(shape, lambda j: (0,) * len(shape), pipeline_mode=once)
    mine = whole(2 * rows, D)
    one = lambda j: jnp.minimum(j, wide - 1)
    two = lambda j: jnp.maximum(j - wide, 0)
    strip = pl.BlockSpec((2 * rows, FT), lambda j: (0, one(j)))
    total = 2 * rows
    return pl.pallas_call(
        expert_fwd_kernel,
        grid=(wide + deep,),
        in_specs=[whole(2, 8, count), whole(8, D)]
        + [whole(count, D)] * 2
        + [pl.BlockSpec((count, FT), lambda j: (0, two(j)))] * 2
        + [pl.BlockSpec((1, D, FT), lambda j: (0, 0, one(j)))] * 2
        + [pl.BlockSpec((1, width, FT), lambda j: (0, 0, two(j)))],
        out_specs=[
            mine,
            mine,
            strip,
            strip,
            strip,
            pl.BlockSpec((count, FT), lambda j: (0, two(j))),
            pl.BlockSpec((count, FT), lambda j: (0, two(j))),
            whole(2, 8, count),
        ],
        out_shape=[low_shape(total, D)] * 2
        + [low_shape(total, width)] * 3
        + [low_shape(count, D)] * 2
        + [jax.ShapeDtypeStruct((2, 8, count), jnp.float32)],
        scratch_shapes=[
            pltpu.VMEM((2, rows, count), jnp.bfloat16),
            pltpu.VMEM((2, count, rows), jnp.bfloat16),
            pltpu.VMEM((2 * rows, width), jnp.bfloat16),
            pltpu.VMEM((2 * rows, 128), jnp.float32),
        ],
        compiler_params=pltpu.CompilerParams(vmem_limit_bytes=VMEM_MOST),
        cost_estimate=LIGHT,
        name=f"expert_fwd_{place}",
    )(meta, router_rows, *toks, *cots, w_gate, w_up, w_down)


def expert_bwd(place, rows, meta, gc, slope, act, w_gate, w_up, w_down):
    count = meta.shape[2]
    total, width = slope.shape
    wide = width // FT
    deep = D // FT
    once = pl.Buffered(1)
    one = lambda j: jnp.minimum(j, wide - 1)
    two = lambda j: jnp.maximum(j - wide, 0)
    strip = pl.BlockSpec((2 * rows, FT), lambda j: (0, one(j)))
    return pl.pallas_call(
        expert_bwd_kernel,
        grid=(wide + deep,),
        in_specs=[
            pl.BlockSpec((2, 8, count), lambda j: (0, 0, 0), pipeline_mode=once),
            pl.BlockSpec((2 * rows, D), lambda j: (0, 0), pipeline_mode=once),
            strip,
            strip,
            pl.BlockSpec((1, FT, D), lambda j: (0, one(j), 0)),
            pl.BlockSpec((1, FT, width), lambda j: (0, two(j), 0)),
            pl.BlockSpec((1, FT, width), lambda j: (0, two(j), 0)),
        ],
        out_specs=[strip] * 2 + [pl.BlockSpec((count, FT), lambda j: (0, two(j)))] * 2,
        out_shape=[low_shape(total, width)] * 2 + [low_shape(count, D)] * 2,
        scratch_shapes=[
            pltpu.VMEM((2, count, rows), jnp.bfloat16),
            pltpu.VMEM((2 * rows, width), jnp.bfloat16),
            pltpu.VMEM((2 * rows, width), jnp.bfloat16),
        ],
        compiler_params=pltpu.CompilerParams(vmem_limit_bytes=VMEM_MOST),
        cost_estimate=LIGHT,
        name=f"expert_bwd_{place}",
    )(meta, gc, slope, act, w_down, w_gate, w_up)


def turn_into(turned_s, refs):
    first = 0
    for ref in refs:
        turned_s[:, first : first + ref.shape[0]] = jnp.transpose(ref[...])
        first += ref.shape[0]


def row_sums(turned_s, refs):
    first, out = 0, None
    for ref in refs:
        part = dot_nn(turned_s[:, first : first + ref.shape[0]], ref[...])
        out = part if out is None else out + part
        first += ref.shape[0]
    return out


def grad_down_kernel(*refs):
    out_ref, turned_s = refs[-2:]
    many = (len(refs) - 2) // 2

    @pl.when(pl.program_id(0) == 0)
    def _():
        turn_into(turned_s, refs[:many])

    out_ref[...] = jnp.transpose(row_sums(turned_s, refs[many : 2 * many])).astype(jnp.bfloat16)


def grad_in_kernel(many, inner, place_ref, *refs):
    sides = refs[3 * many : 3 * many + 2 * inner]
    turned_s, tile_s = refs[-2:]
    blocks, rows, wide = tile_s.shape

    @pl.when(pl.program_id(0) == 0)
    def _():
        turn_into(turned_s, refs[:many])

    for kind in range(2):
        tile = row_sums(turned_s, refs[(kind + 1) * many : (kind + 2) * many]).astype(jnp.bfloat16)
        tile_s[...] = tile.reshape(blocks, rows, wide)
        for away in range(inner):
            side = lax.rem(place_ref[0] + away, inner)
            for block in range(blocks // inner):
                sides[kind * inner + away][block] = tile_s[block * inner + side]


def grad_down(gc, hidden):
    rows, width = hidden[0].shape
    once = pl.Buffered(1)
    return pl.pallas_call(
        grad_down_kernel,
        grid=(width // FT,),
        in_specs=[pl.BlockSpec((rows, D), lambda j: (0, 0), pipeline_mode=once)] * len(gc)
        + [pl.BlockSpec((rows, FT), lambda j: (0, j))] * len(gc),
        out_specs=pl.BlockSpec((FT, D), lambda j: (j, 0)),
        out_shape=low_shape(width, D),
        scratch_shapes=[pltpu.VMEM((D, rows * len(gc)), jnp.bfloat16)],
        compiler_params=pltpu.CompilerParams(vmem_limit_bytes=VMEM_LIMIT),
        cost_estimate=LIGHT,
        name="grad_down",
    )(*gc, *hidden)


def grad_in(place, inner, blocks, xs, dgate, dup):
    rows, width = dgate[0].shape
    many = len(xs)
    once = pl.Buffered(1)
    out = pl.BlockSpec((blocks // inner, D // blocks, FT), lambda j: (0, 0, j))
    made = pl.pallas_call(
        partial(grad_in_kernel, many, inner),
        grid=(width // FT,),
        in_specs=[pl.BlockSpec(memory_space=pltpu.SMEM)]
        + [pl.BlockSpec((rows, D), lambda j: (0, 0), pipeline_mode=once)] * many
        + [pl.BlockSpec((rows, FT), lambda j: (0, j))] * (2 * many),
        out_specs=[out] * (2 * inner),
        out_shape=[low_shape(blocks // inner, D // blocks, width)] * (2 * inner),
        scratch_shapes=[
            pltpu.VMEM((D, rows * many), jnp.bfloat16),
            pltpu.VMEM((blocks, D // blocks, FT), jnp.bfloat16),
        ],
        compiler_params=pltpu.CompilerParams(vmem_limit_bytes=VMEM_LIMIT),
        cost_estimate=LIGHT,
        name="grad_in",
    )(place, *xs, *dgate, *dup)
    return made[:inner], made[inner:]


def grad_attn_kernel(place_ref, normed_ref, attended_ref, right_ref, branch_ref, own_ref, other_ref, turned_s):
    step = pl.program_id(0)
    first = pl.num_programs(0) - 2

    @pl.when(step == 0)
    def _():
        turned_s[...] = jnp.transpose(normed_ref[...])

    @pl.when(step == first)
    def _():
        turned_s[...] = jnp.transpose(attended_ref[...])

    def hand(right):
        made = dot_nn(turned_s[...], right).astype(jnp.bfloat16)
        upper, lower = made[: D // 2], made[D // 2 :]
        swap = place_ref[0] == 1
        own_ref[...] = jnp.where(swap, lower, upper)
        other_ref[...] = jnp.where(swap, upper, lower)

    @pl.when(step < first)
    def _():
        hand(right_ref[...])

    @pl.when(step >= first)
    def _():
        hand(branch_ref[...])


def grad_attn(place, normed, attended, grad_qkv, branch):
    count = normed.shape[0]
    whole = pl.BlockSpec((count, D), lambda j: (0, 0), pipeline_mode=pl.Buffered(1))
    half = pl.BlockSpec((D // 2, 512), lambda j: (0, j))
    return pl.pallas_call(
        grad_attn_kernel,
        grid=(8,),
        in_specs=[
            pl.BlockSpec(memory_space=pltpu.SMEM),
            whole,
            whole,
            pl.BlockSpec((count, 512), lambda j: (0, jnp.minimum(j, 5))),
            pl.BlockSpec((count, 512), lambda j: (0, jnp.maximum(j - 6, 0))),
        ],
        out_specs=[half, half],
        out_shape=[low_shape(D // 2, 4 * D)] * 2,
        scratch_shapes=[pltpu.VMEM((D, count), jnp.bfloat16)],
        compiler_params=pltpu.CompilerParams(vmem_limit_bytes=VMEM_LIMIT),
        cost_estimate=LIGHT,
        name="grad_attn",
    )(place, normed, attended, grad_qkv, branch)


def grad_normed_kernel(grad_ref, w_ref, out_ref):
    @pl.when(pl.program_id(0) == 0)
    def _():
        out_ref[...] = dot_nt(grad_ref[...], w_ref[...])

    @pl.when(pl.program_id(0) > 0)
    def _():
        out_ref[...] += dot_nt(grad_ref[...], w_ref[...])


def grad_normed_of(grad_qkv, w_qkv):
    count = grad_qkv.shape[0]
    return pl.pallas_call(
        grad_normed_kernel,
        grid=(3,),
        in_specs=[pl.BlockSpec((count, D), lambda p: (0, p)), pl.BlockSpec((D, D), lambda p: (0, p))],
        out_specs=pl.BlockSpec((count, D), lambda p: (0, 0)),
        out_shape=jax.ShapeDtypeStruct((count, D), jnp.float32),
        compiler_params=pltpu.CompilerParams(vmem_limit_bytes=VMEM_LIMIT),
        cost_estimate=LIGHT,
        name="grad_normed",
    )(grad_qkv, w_qkv)


def gather_kernel(place_ref, one_own, one_other, two_own, two_other, qkv_ref, out_ref):
    step = pl.program_id(0)
    swap = place_ref[0] == 1
    rows = one_own.shape[0]

    def whole(own_ref, other_ref, target):
        own, other = own_ref[...], other_ref[...]
        target[:rows] = jnp.where(swap, other, own).astype(jnp.float32)
        target[rows:] = jnp.where(swap, own, other).astype(jnp.float32)

    @pl.when(step < 4)
    def _():
        whole(one_own, one_other, qkv_ref)

    @pl.when((step >= 4) & (step < 6))
    def _():
        whole(two_own, two_other, qkv_ref)

    @pl.when(step >= 6)
    def _():
        whole(two_own, two_other, out_ref)


def gather_halves(place, one, two):
    rows = one[0].shape[0]
    left = pl.BlockSpec((rows, 512), lambda j: (0, jnp.minimum(j, 3)))
    right = pl.BlockSpec((rows, 512), lambda j: (0, jnp.maximum(j - 4, 0)))
    return pl.pallas_call(
        gather_kernel,
        grid=(8,),
        in_specs=[pl.BlockSpec(memory_space=pltpu.SMEM), left, left, right, right],
        out_specs=[
            pl.BlockSpec((2 * rows, 512), lambda j: (0, jnp.minimum(j, 5))),
            pl.BlockSpec((2 * rows, 512), lambda j: (0, jnp.maximum(j - 6, 0))),
        ],
        out_shape=[
            jax.ShapeDtypeStruct((2 * rows, 3 * D), jnp.float32),
            jax.ShapeDtypeStruct((2 * rows, D), jnp.float32),
        ],
        compiler_params=pltpu.CompilerParams(vmem_limit_bytes=VMEM_LIMIT),
        cost_estimate=LIGHT,
        name="gather_halves",
    )(place, *one, *two)


def project_kernel(tok_ref, gain_ref, w_ref, normed_ref, qkv_ref):
    @pl.when(pl.program_id(0) == 0)
    def _():
        values = tok_ref[...].astype(jnp.float32)
        scale = lax.rsqrt(jnp.mean(values * values, axis=-1, keepdims=True) + EPSILON)
        normed_ref[...] = (values * scale * gain_ref[...]).astype(jnp.bfloat16)

    qkv_ref[...] = dot_nn(normed_ref[...], w_ref[...]).astype(jnp.bfloat16)


def project(tokens, gain, w_qkv):
    count, width = tokens.shape[0], w_qkv.shape[1]
    once = pl.Buffered(1)
    return pl.pallas_call(
        project_kernel,
        grid=(width // 512,),
        in_specs=[
            pl.BlockSpec((count, D), lambda j: (0, 0), pipeline_mode=once),
            pl.BlockSpec((1, D), lambda j: (0, 0), pipeline_mode=once),
            pl.BlockSpec((D, 512), lambda j: (0, j)),
        ],
        out_specs=[
            pl.BlockSpec((count, D), lambda j: (0, 0), pipeline_mode=once),
            pl.BlockSpec((count, 512), lambda j: (0, j)),
        ],
        out_shape=[low_shape(count, D), low_shape(count, width)],
        compiler_params=pltpu.CompilerParams(vmem_limit_bytes=VMEM_LIMIT),
        cost_estimate=LIGHT,
        name="project",
    )(tokens, gain[None], w_qkv)


OUTER = 4


def rms_forward(values, gain):
    scale_rows = lax.rsqrt(jnp.mean(values * values, axis=-1, keepdims=True) + EPSILON)
    return (values * scale_rows * gain, scale_rows)


def rms_backward(values, scale_rows, gain, upstream):
    scaled_grad = upstream * gain
    gain_grad = jnp.sum(upstream * values * scale_rows, axis=0)
    inner_mean = jnp.mean(scaled_grad * values, axis=-1, keepdims=True)
    return (scale_rows * scaled_grad - values * scale_rows**3 * inner_mean, gain_grad)


def tie(*arrays):
    return lax.optimization_barrier(arrays)


def to_sibling(x):
    groups = lax.axis_size("ep")
    return lax.ppermute(x, "ep", [(e, e ^ 1) for e in range(groups)])


def from_chip(x, away, cross=0):
    groups = lax.axis_size("ep")
    return lax.ppermute(x, "ep", [(e, ((e - 2 * away) % groups) ^ cross) for e in range(groups)])


def core_pairs(step):
    return [(e, e ^ 1) for e in range(lax.axis_size("ep"))]


def chip_pairs(step):
    groups = lax.axis_size("ep")
    return [(e, (e + 2 * step) % groups) for e in range(groups)]


def inner_pairs(step):
    replicas = lax.axis_size("rep")
    inner = replicas // OUTER
    return [(r, r - r % inner + (r + step) % inner) for r in range(replicas)]


def outer_pairs(step):
    replicas = lax.axis_size("rep")
    return [(r, (r + step * (replicas // OUTER)) % replicas) for r in range(replicas)]


def levels():
    ep, rep = lax.axis_index("ep"), lax.axis_index("rep")
    inner = lax.axis_size("rep") // OUTER
    return (
        ("ep", 2, ep % 2, core_pairs),
        ("ep", lax.axis_size("ep") // 2, ep // 2, chip_pairs),
        ("rep", inner, rep % inner, inner_pairs),
        ("rep", OUTER, rep // inner, outer_pairs),
    )


def swapped(x, level, steps=None):
    axis, size, place, pairs = level
    out = [] if steps else [lax.dynamic_index_in_dim(x, place, 0, keepdims=False)]
    for step in steps or range(1, size):
        sent = lax.dynamic_index_in_dim(x, (place + step) % size, 0, keepdims=False)
        out.append(lax.ppermute(sent, axis, pairs(step)))
    return out


def sides_swapped(sides, level):
    axis, size, place, pairs = level
    return [sides[0]] + [lax.ppermute(sides[step], axis, pairs(step)) for step in range(1, size)]


def whole_swapped(x, level):
    axis, size, place, pairs = level
    return [x] + [lax.ppermute(x, axis, pairs(step)) for step in range(1, size)]


def total(arrays):
    return sum([x.astype(jnp.float32) for x in arrays[1:]], arrays[0].astype(jnp.float32))


def low_total(arrays):
    return total(arrays).astype(arrays[0].dtype)


def collected(x, level):
    axis, size, place, pairs = level
    if size == 2:
        other = lax.ppermute(x, axis, pairs(1))
        return jnp.concatenate([jnp.where(place == 0, x, other), jnp.where(place == 0, other, x)])
    out = lax.dynamic_update_index_in_dim(jnp.zeros((size, *x.shape), x.dtype), x, place, 0)
    for step in range(1, size):
        other = lax.ppermute(x, axis, pairs(step))
        out = lax.dynamic_update_index_in_dim(out, other, (place - step) % size, 0)
    return out.reshape(-1, *x.shape[1:])


def rows_swapped(x, level):
    return swapped(x.reshape(level[1], -1, x.shape[1]), level)


def near_swapped(x):
    replicas = lax.axis_size("rep")
    blocks = x.reshape(OUTER, replicas // OUTER, x.shape[0] // replicas, x.shape[1])
    return swapped(jnp.swapaxes(blocks, 0, 1), levels()[2])


def slot_table(expert_ids, priority, experts, capacity):
    ranks = priority.reshape(-1, 2)
    names = jnp.arange(experts, dtype=jnp.int32)[:, None]
    first, second = expert_ids[:, 0][None, :] == names, expert_ids[:, 1][None, :] == names
    rank = jnp.where(first, ranks[:, 0][None, :], jnp.where(second, ranks[:, 1][None, :], 1 << 20))
    slot = jnp.sum((rank[:, :, None] < rank[:, None, :]).astype(jnp.int32), axis=1)
    return jnp.where((first | second) & (slot < capacity), slot, -1)


def per_device(
    tokens,
    cotangent,
    gain_attn,
    w_qkv,
    w_out,
    rel_table,
    gain_moe,
    w_router,
    w_gate,
    w_up,
    w_down,
    expert_ids,
    priority,
    span_starts,
):
    tok_count = tokens.shape[0]
    experts = w_router.shape[1]
    groups = lax.axis_size("ep")
    chips = groups // 2
    capacity = 5 * tok_count // (2 * experts)
    own = lax.axis_index("ep")

    slots = slot_table(expert_ids, priority, experts, capacity)
    ids = jnp.transpose(expert_ids)
    table = jnp.concatenate([slots, ids], axis=0)
    info = [(table, to_sibling(table))] + [(from_chip(table, n), from_chip(table, n, 1)) for n in range(1, chips)]
    cot_sib = to_sibling(cotangent)
    cot_far = [from_chip(cotangent, n) for n in range(1, chips)]
    metas = []
    for pair in info:
        rows = []
        for table in pair:
            slot = lax.dynamic_slice_in_dim(table, own, 1, axis=0)
            one, two = table[experts : experts + 1], table[experts + 1 :]
            other = jnp.where(one == own, two, one)
            rows.append(jnp.concatenate([slot, other, jnp.full((6, tok_count), 1, jnp.int32) * own], axis=0))
        metas.append(jnp.stack(rows))

    diag = wide_diag(rel_table)
    token_float = tokens.astype(jnp.float32)
    normed_low, qkv = project(tokens, gain_attn, w_qkv)
    attended_low, lse = attn_fwd(span_starts, qkv, diag)
    attended_low, cot_sib, cot_far, metas = tie(attended_low, cot_sib, cot_far, metas)
    mixed = token_float + jnp.dot(attended_low, w_out, preferred_element_type=jnp.float32)
    routed, scale_moe = rms_forward(mixed, gain_moe)
    routed_low = routed.astype(jnp.bfloat16)
    logits = jnp.dot(routed_low, w_router, preferred_element_type=jnp.float32)
    choose = expert_ids[:, :, None] == jnp.arange(experts, dtype=jnp.int32)[None, None, :]
    chosen = jnp.sum(jnp.where(choose, logits[:, None, :], 0.0), axis=-1)
    gates = jax.nn.softmax(chosen, axis=-1)

    router_rows = jnp.zeros((8, D), jnp.bfloat16).at[:experts].set(jnp.transpose(w_router))
    weights = (w_gate, w_up, w_down)
    core, chip, inner, outer = levels()

    tok_far = [from_chip(routed_low, n) for n in range(1, chips)]
    cots = [(cotangent, cot_sib)] + [(far, to_sibling(far)) for far in cot_far]
    pair = (routed_low, to_sibling(routed_low))
    made = expert_fwd(0, capacity, metas[0], router_rows, pair, cots[0], *weights)
    made, tok_far, cots = tie(made, tok_far, cots)
    toks = [(far, to_sibling(far)) for far in tok_far]
    outs, dots = [made[5:7]], [(made[7][0], made[7][1])]
    kept = [made[:5]]
    for away in range(1, chips):
        made = expert_fwd(away, capacity, metas[away], router_rows, toks[away - 1], cots[away], *weights)
        kept.append(made[:5])
        outs.append(made[5:7])
        dots.append((made[7][0], made[7][1]))
    rows_in, rows_out, hidden, slope, act = [list(x) for x in zip(*kept)]

    met = [[to_sibling(other) for mine, other in part] for part in (dots, outs)]
    down_low = grad_down(rows_out, hidden)
    down_low, slope, met, dots, outs = tie(down_low, slope, met, dots, outs)
    dots, outs = [
        [total([mine[n][0], got[n]]) for n in range(chips)] for mine, got in zip((dots, outs), met)
    ]
    outs_low = [x.astype(jnp.bfloat16) for x in outs[1:]]
    slope, outs_low, down_low = tie(slope, outs_low, down_low)
    far_outs = [from_chip(x, chips - 1 - n) for n, x in enumerate(outs_low)]
    far_dots = [from_chip(x, chips - 1 - n) for n, x in enumerate(dots[1:])]
    down_near = near_swapped(down_low)
    grads = [None] * chips
    for away in reversed(range(1, chips)):
        slope[away], act[away], *grads[away] = expert_bwd(
            away, capacity, metas[away], rows_out[away], slope[away], act[away], *weights
        )
    slope, far_outs, far_dots = tie(slope, far_outs, far_dots)
    far_grads = []
    for away in range(1, chips):
        far_grads += [from_chip(grads[away][0], chips - away), from_chip(grads[away][1], chips - away, 1)]
    slope[0], act[0], *here = expert_bwd(0, capacity, metas[0], rows_out[0], slope[0], act[0], *weights)
    slope, down_near = tie(slope, down_near)
    down_near = low_total(down_near)
    slope, down_near = tie(slope, down_near)
    near_grads = to_sibling(here[1])
    down_far = swapped(down_near, outer)
    gate_low, up_low = grad_in(
        jnp.reshape(inner[2], (1,)), inner[1], lax.axis_size("rep"), rows_in, slope, act
    )
    gate_low, up_low, far_grads, near_grads = tie(gate_low, up_low, far_grads, near_grads)
    grad_pairs = total([here[0], near_grads] + far_grads)
    grad_gates_all = total([dots[0]] + far_dots)
    block_out = (mixed + total([outs[0]] + far_outs)).astype(jnp.bfloat16)
    gate_near = sides_swapped(gate_low, inner)

    grad_out = cotangent.astype(jnp.float32)
    by_token = jnp.transpose(grad_gates_all[:experts])
    grad_gates = jnp.sum(jnp.where(choose, by_token[:, None, :], 0.0), axis=-1)
    grad_chosen = gates * (grad_gates - jnp.sum(gates * grad_gates, axis=-1, keepdims=True))
    grad_logits = jnp.sum(jnp.where(choose, grad_chosen[:, :, None], 0.0), axis=1).astype(jnp.bfloat16)
    grad_routed = grad_pairs + jnp.einsum(
        "te,de->td", grad_logits, w_router, preferred_element_type=jnp.float32
    )
    grad_norm_moe, grad_gain_moe = rms_backward(mixed, scale_moe, gain_moe, grad_routed)
    grad_mixed = grad_out + grad_norm_moe
    grad_branch = grad_mixed.astype(jnp.bfloat16)
    grad_attended = jnp.einsum(
        "te,de->td", grad_branch, w_out, preferred_element_type=jnp.float32
    ).astype(jnp.bfloat16)

    grad_attended, grad_branch = tie(grad_attended, grad_branch)
    quarters = [None] * 4
    made = None

    def backward(part, grad, made):
        return attn_bwd(span_starts, qkv, grad, attended_low, lse, diag, part, made)

    for part in (0, 1):
        made, *quarters[part] = backward(part, grad_attended, made)
    made, grad_attended, gate_near, down_far, up_low = tie(
        made, grad_attended, gate_near, down_far, up_low
    )
    gate_near = low_total(gate_near)
    gate_near, grad_attended, up_low = tie(gate_near, grad_attended, up_low)
    gate_far = swapped(gate_near, outer)
    up_near = sides_swapped(up_low, inner)
    for part in (2, 3):
        made, *quarters[part] = backward(part, grad_attended, made)
    mine, other = grad_attn(jnp.reshape(core[2], (1,)), normed_low, attended_low, made, grad_branch)
    grad_normed = grad_normed_of(made, w_qkv)
    mine, other, grad_normed, gate_far, up_near = tie(mine, other, grad_normed, gate_far, up_near)
    up_near, other = tie(low_total(up_near), other)
    other = to_sibling(other)
    up_far = swapped(up_near, outer)
    both = low_total([mine, other])
    cut = both.shape[1] // 2
    one, two, quarters, late, tokens_late = tie(
        both[:, :cut], both[:, cut:], quarters, (routed_low, grad_logits), tokens
    )
    token_float = tokens_late.astype(jnp.float32)
    grad_w_router = jnp.einsum("td,te->de", *late, preferred_element_type=jnp.float32)
    one, two = rows_swapped(one, chip), rows_swapped(two, inner)
    scale_attn = lax.rsqrt(jnp.mean(token_float * token_float, axis=-1, keepdims=True) + EPSILON)
    grad_norm_attn, grad_gain_attn = rms_backward(token_float, scale_attn, gain_attn, grad_normed)
    grad_tokens = grad_mixed + grad_norm_attn
    grad_rel_table = rel_grad(
        jnp.concatenate([x[0] for x in quarters]), jnp.concatenate([x[1] for x in quarters])
    )
    small = jnp.concatenate(
        [
            jnp.transpose(grad_w_router),
            jnp.pad(grad_rel_table.reshape(1, -1), ((0, 0), (0, D - BUCKETS * H))),
            grad_gain_attn[None],
            grad_gain_moe[None],
        ]
    )
    one, two, small, grad_tokens = tie(one, two, small, grad_tokens)
    one, two = tie(low_total(one), low_total(two))
    one, two, up_far = tie(rows_swapped(one, inner), rows_swapped(two, chip), up_far)
    both = jnp.concatenate([low_total(one), low_total(two)], axis=1)
    both, small = tie(rows_swapped(both, outer), whole_swapped(small, core))
    both, small = tie(low_total(both), total(small))
    both, small = tie(collected(both, outer), whole_swapped(small, chip))
    one, two, small = tie(both[:, :cut], both[:, cut:], total(small))
    one, two, small = tie(collected(one, inner), collected(two, chip), whole_swapped(small, inner))
    small = whole_swapped(total(small), outer)
    one, two, small = tie(collected(one, chip), collected(two, inner), small)
    one, two = (one, to_sibling(one)), (two, to_sibling(two))
    sum_w_qkv, sum_w_out = gather_halves(jnp.reshape(core[2], (1,)), one, two)
    small = total(small)
    sum_down = total(down_far)
    sum_gate, sum_up = total(gate_far), total(up_far)
    small = (
        small[experts, : BUCKETS * H].reshape(BUCKETS, H),
        jnp.transpose(small[:experts]),
        small[experts + 1],
        small[experts + 2],
    )
    return (
        block_out,
        grad_tokens,
        small[2],
        sum_w_qkv,
        sum_w_out,
        small[0],
        small[3],
        small[1],
        sum_gate[None],
        sum_up[None],
        sum_down[None],
    )


def solution(mesh):
    placed = (
        P(("rep", "ep"), None),
        P(("rep", "ep"), None),
        P(),
        P(),
        P(),
        P(),
        P(),
        P(),
        P("ep", None, None),
        P("ep", None, None),
        P("ep", None, None),
        P(("rep", "ep"), None),
        P(("rep", "ep"), None),
        P(("rep", "ep"), None),
    )
    return jax.shard_map(
        per_device,
        mesh=mesh,
        in_specs=placed,
        out_specs=(
            P(("rep", "ep"), None),
            P(("rep", "ep"), None),
            P(),
            P(),
            P(),
            P(),
            P(),
            P(),
            P("ep", "rep", None),
            P("ep", "rep", None),
            P("ep", "rep", None),
        ),
        check_vma=False,
    )
```
